32 devices in a mesh: head: 4 (over y, x), blk: 8 (over z, core).
Axes of the slice: x: 2, y: 2, z: 4, core: 2. Of those that a mesh axis runs over, the one named last changes fastest.
Arguments:
- inputs: bfloat16 [8192, 1024], P(('blk', 'head')), may hold values from -6 to 6
- query_weight: bfloat16 [1024, 1024], P(('head', 'blk')), may hold values from -0.1875 to 0.1875
- key_weight: bfloat16 [1024, 512], P(('head', 'blk')), may hold values from -0.1875 to 0.1875
- value_weight: bfloat16 [1024, 512], P(('head', 'blk')), may hold values from -0.1875 to 0.1875
- mixing_weight: bfloat16 [1024, 1024], P(('head', 'blk')), may hold values from -1.5 to 1.5
- gate_weight: bfloat16 [1024, 4608], P(('head', 'blk')), may hold values from -0.1875 to 0.1875
- up_weight: bfloat16 [1024, 4608], P(('head', 'blk')), may hold values from -0.1875 to 0.1875
- down_weight: bfloat16 [4608, 1024], P(('head', 'blk')), may hold values from -0.09375 to 0.09375
- attention_gain: bfloat16 [1024], P(('head', 'blk')), may hold values from 0.5 to 1.5
- feedforward_gain: bfloat16 [1024], P(('head', 'blk')), may hold values from 0.5 to 1.5
- query_gain: bfloat16 [64], replicated, may hold values from 1 to 2
- key_gain: bfloat16 [64], replicated, may hold values from 1 to 2
- cotangent: bfloat16 [8192, 1024], P(('blk', 'head')), may hold values from -6 to 6
Outputs:
- output: bfloat16 [8192, 1024], P(('blk', 'head'))
- input_gradient: bfloat16 [8192, 1024], P(('blk', 'head'))
- query_gradient: float32 [1024, 1024], P(('head', 'blk'))
- key_gradient: float32 [1024, 512], P(('head', 'blk'))
- value_gradient: float32 [1024, 512], P(('head', 'blk'))
- mixing_gradient: float32 [1024, 1024], P(('head', 'blk'))
- gate_gradient: float32 [1024, 4608], P(('head', 'blk'))
- up_gradient: float32 [1024, 4608], P(('head', 'blk'))
- down_gradient: float32 [4608, 1024], P(('head', 'blk'))
- attention_gain_gradient: float32 [1024], P(('head', 'blk'))
- feedforward_gain_gradient: float32 [1024], P(('head', 'blk'))
- query_gain_gradient: float32 [64], replicated
- key_gain_gradient: float32 [64], replicated
The draws below stay inside these ranges and needn't reach their ends.
All inputs are finite; a program needn't handle non-finite values.
Results may differ from the reference program's by a relative error of at most 0.035.
Values may be sent and summed in bfloat16 or wider, within the bound.
No kernel may reach another device: no remote copies, remote signals or barrier semaphores. Data moves between devices by JAX's collectives and lax.ppermute only.
A program may use at most 192 MiB of HBM per device.

```python
import math
import jax
import jax.numpy as jnp
from jax import lax

D = 1024
HQ = 16
KV = 8
HD = 64
FF = 4608
TOKENS = 8192


def levels(key, extent, pieces, smallest, high):
    level = 1.0
    for dim, blocks in pieces:
        steps = jax.random.uniform(jax.random.fold_in(jax.random.fold_in(key, 6), dim), (blocks,), jnp.float32, smallest / len(pieces), high / len(pieces))
        level = level * jnp.repeat(jnp.exp(steps), extent[dim] // blocks).reshape((-1,) + (1,) * (len(extent) - 1 - dim))
    return level


def scatter_about(rng, dims, spread, most, pieces=(), dtype=jnp.bfloat16):
    entries = jax.random.normal(rng, dims, jnp.float32) * spread
    if len(pieces) > 0:
        entries = levels(rng, dims, pieces, -0.22, 0.18) * entries
    return jnp.clip(entries, min=-most, max=most).astype(dtype)


def setup_inputs(seed: int = 0) -> dict:
    arg_keys = jax.random.split(jax.random.key(seed), 14)
    inputs = scatter_about(arg_keys[0], (TOKENS, D), 1.0, 6.0, ((0, 32),))
    query_weight = scatter_about(arg_keys[1], (D, HQ * HD), D ** -0.5, 0.1875, ((0, 32),))
    key_weight = scatter_about(arg_keys[2], (D, KV * HD), D ** -0.5, 0.1875, ((0, 32),))
    value_weight = scatter_about(arg_keys[3], (D, KV * HD), D ** -0.5, 0.1875, ((0, 32),))
    mixing_weight = scatter_about(arg_keys[4], (HQ * HD, D), 16 ** -0.5, 1.5, ((0, 32),))
    gate_weight = scatter_about(arg_keys[5], (D, FF), D ** -0.5, 0.1875, ((0, 32),))
    up_weight = scatter_about(arg_keys[6], (D, FF), D ** -0.5, 0.1875, ((0, 32),))
    down_weight = scatter_about(arg_keys[7], (FF, D), FF ** -0.5, 0.09375, ((0, 32),))
    attention_gain = jnp.clip(1.0 + 0.1 * jax.random.normal(arg_keys[8], (D,), jnp.float32), 0.5, 1.5).astype(jnp.bfloat16)
    feedforward_gain = jnp.clip(1.0 + 0.1 * jax.random.normal(arg_keys[9], (D,), jnp.float32), 0.5, 1.5).astype(jnp.bfloat16)
    query_gain = jnp.clip(jnp.exp(jax.random.uniform(arg_keys[10], (HD,), jnp.float32, math.log(1.0), math.log(2.0))), 1.0, 2.0).astype(jnp.bfloat16)
    key_gain = jnp.clip(jnp.exp(jax.random.uniform(arg_keys[11], (HD,), jnp.float32, math.log(1.0), math.log(2.0))), 1.0, 2.0).astype(jnp.bfloat16)
    cotangent = scatter_about(arg_keys[12], (TOKENS, D), 1.0, 6.0, ((0, 32),))
    return {"inputs": inputs, "query_weight": query_weight, "key_weight": key_weight, "value_weight": value_weight, "mixing_weight": mixing_weight, "gate_weight": gate_weight, "up_weight": up_weight, "down_weight": down_weight, "attention_gain": attention_gain, "feedforward_gain": feedforward_gain, "query_gain": query_gain, "key_gain": key_gain, "cotangent": cotangent}


EPSILON = 1e-05
ROPE_BASE = 1000000.0
NEGATIVE = -1e+30
HIGHEST = lax.Precision.HIGHEST

@jax.custom_vjp
def low(v):
    return lax.optimization_barrier(v.astype(jnp.bfloat16)).astype(jnp.float32)

@jax.custom_vjp
def low_back(v):
    return v

def low_keep(v):
    return (low(v), None)

def low_pass(kept, grad):
    return (grad,)

def back_keep(v):
    return (v, None)

def back_low(kept, grad):
    return (low(grad),)
low.defvjp(low_keep, low_pass)
low_back.defvjp(back_keep, back_low)

def matmul(left, right):
    return jnp.dot(left, right, precision=HIGHEST)

def rms_scale(values, gain_row):
    return values * lax.rsqrt(lax.optimization_barrier(jnp.mean(values * values, axis=-1, keepdims=True)) + EPSILON) * gain_row

def rope_tables(positions, head_size):
    half_size = head_size // 2
    frequency = jnp.exp(jnp.arange(half_size).astype(jnp.float32) * (-2.0 * math.log(ROPE_BASE) / head_size))
    angles = positions.astype(jnp.float32)[:, None] * frequency[None, :]
    return (jnp.cos(angles), jnp.sin(angles))

def rotate(values, cosine_table, sine_table):
    half_size = values.shape[-1] // 2
    first_half = values[..., :half_size]
    second_half = values[..., half_size:]
    cosine_wide = cosine_table[:, None, :]
    sine_wide = sine_table[:, None, :]
    return jnp.concatenate([first_half * cosine_wide - second_half * sine_wide, second_half * cosine_wide + first_half * sine_wide], axis=-1)

def head_norm_rope(raw, gain_row, cosine_table, sine_table):
    row_count = raw.shape[0]
    shaped = raw.reshape(row_count, -1, HD)
    return rotate(rms_scale(shaped, gain_row), cosine_table, sine_table).reshape(row_count, -1)

def swish_product(gate_value, up_value):
    return gate_value * jax.nn.sigmoid(gate_value) * up_value

def attention(query_heads, key_heads, value_heads):
    total_rows = query_heads.shape[0]
    group_size = HQ // KV
    grouped = query_heads.reshape(total_rows, KV, group_size, HD)
    key_grid = key_heads.reshape(total_rows, KV, HD)
    value_grid = value_heads.reshape(total_rows, KV, HD)
    row_block = 512 if total_rows % 512 == 0 else total_rows
    block_total = total_rows // row_block
    key_place = jnp.arange(total_rows).astype(jnp.int32)
    score_scale = HD ** (-0.5)

    def attend_rows(block_number):
        first_row = (block_number * row_block).astype(jnp.int32)
        query_block = lax.dynamic_slice_in_dim(grouped, first_row, row_block, 0)
        scores = low_back(jnp.einsum('qkgd,skd->kgqs', query_block, key_grid, precision=HIGHEST) * score_scale)
        query_place = first_row + jnp.arange(row_block).astype(jnp.int32)
        allowed = key_place[None, :] <= query_place[:, None]
        scores = jnp.where(allowed, scores, NEGATIVE)
        row_max = lax.optimization_barrier(jnp.max(scores, axis=-1, keepdims=True))
        exponent = jnp.exp(scores - row_max)
        probability = low(exponent / lax.optimization_barrier(jnp.sum(exponent, axis=-1, keepdims=True)))
        mixture = jnp.einsum('kgqs,skd->qkgd', probability, value_grid, precision=HIGHEST)
        return mixture.reshape(row_block, HQ * HD)
    blocks = lax.map(jax.checkpoint(attend_rows), jnp.arange(block_total).astype(jnp.int32))
    return blocks.reshape(total_rows, HQ * HD)

def forward(cosine_table, sine_table, inputs, query_weight, key_weight, value_weight, mixing_weight, gate_weight, up_weight, down_weight, attention_gain, feedforward_gain, query_gain, key_gain):
    normed = low(rms_scale(inputs, attention_gain))
    query_raw = low_back(matmul(normed, query_weight))
    key_raw = low_back(matmul(normed, key_weight))
    value_heads = low(low_back(matmul(normed, value_weight)))
    query_heads = low(low_back(head_norm_rope(query_raw, query_gain, cosine_table, sine_table)))
    key_heads = low(low_back(head_norm_rope(key_raw, key_gain, cosine_table, sine_table)))
    mixture = low(low_back(attention(query_heads, key_heads, value_heads)))
    hidden = inputs + low_back(matmul(mixture, mixing_weight))
    normed_ffn = low(rms_scale(hidden, feedforward_gain))
    gate_value = low_back(matmul(normed_ffn, gate_weight))
    up_value = low_back(matmul(normed_ffn, up_weight))
    activation = low(low_back(swish_product(gate_value, up_value)))
    return hidden + low_back(matmul(activation, down_weight))

def reference(inputs, query_weight, key_weight, value_weight, mixing_weight, gate_weight, up_weight, down_weight, attention_gain, feedforward_gain, query_gain, key_gain, cotangent):
    positions = jnp.arange(TOKENS).astype(jnp.int32)
    cosine_table, sine_table = rope_tables(positions, HD)

    def forward_tables(inputs_float, query_float, key_float, value_float, mixing_float, gate_float, up_float, down_float, attention_float, feedforward_float, query_gain_float, key_gain_float):
        return forward(cosine_table, sine_table, inputs_float, query_float, key_float, value_float, mixing_float, gate_float, up_float, down_float, attention_float, feedforward_float, query_gain_float, key_gain_float)
    output, pullback = jax.vjp(forward_tables, inputs.astype(jnp.float32), query_weight.astype(jnp.float32), key_weight.astype(jnp.float32), value_weight.astype(jnp.float32), mixing_weight.astype(jnp.float32), gate_weight.astype(jnp.float32), up_weight.astype(jnp.float32), down_weight.astype(jnp.float32), attention_gain.astype(jnp.float32), feedforward_gain.astype(jnp.float32), query_gain.astype(jnp.float32), key_gain.astype(jnp.float32))
    grads = pullback(cotangent.astype(jnp.float32))
    return (output.astype(jnp.bfloat16), grads[0].astype(jnp.bfloat16), grads[1], grads[2], grads[3], grads[4], grads[5], grads[6], grads[7], grads[8], grads[9], grads[10], grads[11])
```

```python
import functools
import math

import jax
import jax.numpy as jnp
from jax import lax
from jax.experimental import pallas as pl
from jax.experimental.pallas import tpu as pltpu
from jax.sharding import PartitionSpec as P

HQ = 16
KV = 8
HD = 64
EPSILON = 1e-05
ROPE_BASE = 1000000.0
TILE = 1024
QUERY_UNIT = math.log2(math.e) * HD**-0.5

BF = jnp.bfloat16
F32 = jnp.float32
NT = (((1,), (1,)), ((), ()))
NN = (((1,), (0,)), ((), ()))
TN = (((0,), (0,)), ((), ()))
VM = pl.BlockSpec(memory_space=pltpu.VMEM)
SM = pl.BlockSpec(memory_space=pltpu.SMEM)


def dot(a, b, dims=NN):
    return lax.dot_general(a, b, dims, preferred_element_type=F32)


def attend_body(span, local, off_ref, q_ref, kv_ref, acc_ref, out_ref, ones_ref):
    lane = lax.broadcasted_iota(jnp.int32, ones_ref.shape, 1)
    ones_ref[...] = jnp.where(lane < HD, jnp.ones((), BF), kv_ref[...])
    out_ref[...] = jnp.zeros_like(out_ref) if local else acc_ref[...]

    heads = q_ref.shape[0]
    block = min(span, TILE)

    def block_pair(head, q_off, k_off):
        rows = pl.ds(q_off, block)
        keys = pl.ds(k_off, block)
        weight = jnp.exp2(dot(q_ref[head, rows, :], kv_ref[keys, :], NT)).astype(BF)
        out_ref[head, rows, :] += dot(weight, ones_ref[keys, :])

    def full(q_off, k_off):
        for i in range(span // block):
            for j in range(span // block):

                def body(head, carry):
                    block_pair(head, q_off + i * block, k_off + j * block)
                    return carry

                lax.fori_loop(0, heads, body, 0)

    def diagonal(start):
        for i in range(span // block):
            for j in range(i):
                for head in range(heads):
                    block_pair(head, start + i * block, start + j * block)
            diagonal_block(start + i * block)

    def diagonal_block(start):
        size = 256
        for head in range(heads):
            for i in range(block // size):
                rows = slice(start + i * size, start + (i + 1) * size)
                total = None
                pieces = ([(0, i * size)] if i else []) + [(i * size, (i + 1) * size)]
                for low, high in pieces:
                    keys = slice(start + low, start + high)
                    weight = jnp.exp2(dot(q_ref[head, rows, :], kv_ref[keys, :], NT))
                    if low == i * size:
                        place = lax.broadcasted_iota(jnp.int32, (size, size), 0)
                        other = lax.broadcasted_iota(jnp.int32, (size, size), 1)
                        weight = jnp.where(other <= place, weight, 0.0)
                    part = dot(weight.astype(BF), ones_ref[keys, :])
                    total = part if total is None else total + part
                out_ref[head, rows, :] += total

    if local:
        diagonal(0)
        diagonal(span)
        full(pl.multiple_of(off_ref[0], span), pl.multiple_of(off_ref[1], span))
    else:
        for pair in range(2):
            full(
                pl.multiple_of(off_ref[2 * pair], span), pl.multiple_of(off_ref[2 * pair + 1], span)
            )


def attend(offsets, query, kv, acc):
    span = query.shape[1] // 2
    local = acc is None
    if local:

        def body(off_ref, q_ref, kv_ref, out_ref, ones_ref):
            attend_body(span, True, off_ref, q_ref, kv_ref, None, out_ref, ones_ref)
    else:
        body = functools.partial(attend_body, span, False)
    args = (offsets, query, kv) if local else (offsets, query, kv, acc)
    return pl.pallas_call(
        body,
        out_shape=jax.ShapeDtypeStruct(query.shape, F32),
        in_specs=[SM] + [VM] * (len(args) - 1),
        out_specs=VM,
        scratch_shapes=[pltpu.VMEM((2 * span, 2 * HD), BF)],
        cost_estimate=pl.CostEstimate(
            flops=2 * 2 * 2 * 2 * span * span * 256,
            bytes_accessed=8 << 20,
            transcendentals=4 * span * span,
        ),
        compiler_params=pltpu.CompilerParams(vmem_limit_bytes=40 << 20),
    )(*args)


def attend_back_body(
    span, local, off_ref, q_ref, do_ref, kv_ref, acc_ref, dq_ref, dkv_ref, ones_ref, dv_ref
):
    lane = lax.broadcasted_iota(jnp.int32, ones_ref.shape, 1)
    zero = jnp.zeros((), BF)
    ones_ref[...] = jnp.where(
        lane < HD, jnp.where(lane < 3, jnp.ones((), BF), zero), kv_ref[...]
    )
    heads = q_ref.shape[0]
    block = min(span, TILE)
    for head in range(heads):
        dv_ref[head] = jnp.where(lane < HD, zero, do_ref[head])
    dq_ref[...] = jnp.zeros_like(dq_ref) if local else acc_ref[...]
    dkv_ref[...] = jnp.zeros_like(dkv_ref)

    def tile(head, rows, keys, mask):
        query = q_ref[head, rows, :]
        pair = kv_ref[keys, :]
        weight = jnp.exp2(dot(pair, query, NT))
        if mask is not None:
            weight = jnp.where(mask, weight, 0.0)
        score_grad = (weight * dot(ones_ref[keys, :], do_ref[head, rows, :], NT)).astype(BF)
        dkv_ref[keys, :] += dot(weight.astype(BF), dv_ref[head, rows, :]) + dot(score_grad, query)
        dq_ref[head, rows, :] += dot(score_grad, pair, TN)

    def block_pair(head, q_off, k_off):
        tile(head, pl.ds(q_off, block), pl.ds(k_off, block), None)

    def full(q_off, k_off):
        for i in range(span // block):
            for j in range(span // block):

                def body(head, carry):
                    block_pair(head, q_off + i * block, k_off + j * block)
                    return carry

                lax.fori_loop(0, heads, body, 0)

    def diagonal(start):
        for i in range(span // block):
            for j in range(i):
                for head in range(heads):
                    block_pair(head, start + i * block, start + j * block)
            diagonal_block(start + i * block)

    def diagonal_block(start):
        size = 256
        for head in range(heads):
            for i in range(block // size):
                rows = slice(start + i * size, start + (i + 1) * size)
                pieces = ([(0, i * size)] if i else []) + [(i * size, (i + 1) * size)]
                for low, high in pieces:
                    mask = None
                    if low == i * size:
                        key_place = lax.broadcasted_iota(jnp.int32, (size, size), 0)
                        mask = key_place <= lax.broadcasted_iota(jnp.int32, (size, size), 1)
                    tile(head, rows, slice(start + low, start + high), mask)

    if local:
        diagonal(0)
        diagonal(span)
        full(pl.multiple_of(off_ref[0], span), pl.multiple_of(off_ref[1], span))
    else:
        for pair in range(2):
            full(
                pl.multiple_of(off_ref[2 * pair], span), pl.multiple_of(off_ref[2 * pair + 1], span)
            )


def attend_back(offsets, query, out_grad, kv, acc):
    span = query.shape[1] // 2
    local = acc is None
    if local:

        def body(off_ref, q_ref, do_ref, kv_ref, *rest):
            attend_back_body(span, True, off_ref, q_ref, do_ref, kv_ref, None, *rest)
    else:
        body = functools.partial(attend_back_body, span, False)
    args = (offsets, query, out_grad, kv) if local else (offsets, query, out_grad, kv, acc)
    return pl.pallas_call(
        body,
        out_shape=(
            jax.ShapeDtypeStruct(query.shape, F32),
            jax.ShapeDtypeStruct(kv.shape, F32),
        ),
        in_specs=[SM] + [VM] * (len(args) - 1),
        out_specs=(VM, VM),
        scratch_shapes=[
            pltpu.VMEM((2 * span, 2 * HD), BF),
            pltpu.VMEM(query.shape, BF),
        ],
        cost_estimate=pl.CostEstimate(
            flops=5 * 2 * 2 * 2 * span * span * 256,
            bytes_accessed=8 << 20,
            transcendentals=4 * span * span,
        ),
        compiler_params=pltpu.CompilerParams(vmem_limit_bytes=48 << 20),
    )(*args)


def swap_halves(x):
    lane = lax.broadcasted_iota(jnp.int32, x.shape, 1)
    return jnp.where(
        lane % HD < HD // 2, pltpu.roll(x, x.shape[1] - HD // 2, 1), pltpu.roll(x, HD // 2, 1)
    )


def head_mean(x):
    lane = lax.broadcasted_iota(jnp.int32, x.shape, 1)
    low = lane < HD
    first = jnp.sum(jnp.where(low, x, 0.0), axis=1, keepdims=True)
    second = jnp.sum(jnp.where(low, 0.0, x), axis=1, keepdims=True)
    return jnp.where(low, first, second) * (1.0 / HD)


def project_body(x_ref, gain_ref, w_ref, cos_ref, sin_ref, head_gain_ref, normed_ref, raw_ref, pk_ref):
    x = x_ref[...].astype(F32)
    scale = lax.rsqrt(jnp.mean(x * x, axis=1, keepdims=True) + EPSILON)
    normed = (x * scale * gain_ref[...]).astype(BF)
    normed_ref[...] = normed
    raw = dot(normed, w_ref[...])
    raw_ref[...] = raw
    cosine, sine = cos_ref[...], sin_ref[...]
    lane = lax.broadcasted_iota(jnp.int32, cosine.shape, 1)
    for j in range(2):
        query = raw[:, 256 * j : 256 * j + 128]
        pair = raw[:, 256 * j + 128 : 256 * j + 256]
        query = query * lax.rsqrt(head_mean(query * query) + EPSILON) * head_gain_ref[0:1, :]
        query = query * cosine + swap_halves(query) * sine
        pk_ref[j, :, 0:128] = (query * QUERY_UNIT).astype(BF)
        key = pair * lax.rsqrt(head_mean(pair * pair) + EPSILON) * head_gain_ref[1:2, :]
        key = key * cosine + swap_halves(key) * sine
        pk_ref[j, :, 128:256] = jnp.where(lane < HD, key, pair).astype(BF)


def project(x, gain, weight, cosine, sine, head_gain):
    rows, depth = x.shape
    cols = weight.shape[1]
    tile = 256
    return pl.pallas_call(
        project_body,
        grid=(rows // tile,),
        in_specs=[
            pl.BlockSpec((tile, depth), lambda i: (i, 0)),
            pl.BlockSpec((1, depth), lambda i: (0, 0)),
            pl.BlockSpec((depth, cols), lambda i: (0, 0)),
            pl.BlockSpec((tile, 128), lambda i: (i, 0)),
            pl.BlockSpec((tile, 128), lambda i: (i, 0)),
            pl.BlockSpec((8, 128), lambda i: (0, 0)),
        ],
        out_specs=(
            pl.BlockSpec((tile, depth), lambda i: (i, 0)),
            pl.BlockSpec((tile, cols), lambda i: (i, 0)),
            pl.BlockSpec((2, tile, 256), lambda i: (0, i, 0)),
        ),
        out_shape=(
            jax.ShapeDtypeStruct((rows, depth), BF),
            jax.ShapeDtypeStruct((rows, cols), F32),
            jax.ShapeDtypeStruct((2, rows, 256), BF),
        ),
        cost_estimate=pl.CostEstimate(
            flops=4 * rows * depth * cols, bytes_accessed=8 << 20, transcendentals=0
        ),
        compiler_params=pltpu.CompilerParams(vmem_limit_bytes=32 << 20),
    )(x, gain, weight, cosine, sine, head_gain)


def project_back_body(
    raw_ref, grad_ref, normed_ref, w_ref, cos_ref, sin_ref, head_gain_ref,
    part_ref, dw_ref, gain_grad_ref, acc_ref
):
    step = pl.program_id(0)

    @pl.when(step == 0)
    def start():
        acc_ref[...] = jnp.zeros_like(acc_ref)
        gain_grad_ref[...] = jnp.zeros_like(gain_grad_ref)

    cosine, sine = cos_ref[...], sin_ref[...]
    lane = lax.broadcasted_iota(jnp.int32, cosine.shape, 1)
    pieces = []
    gain_sums = [jnp.zeros((1, 128), F32), jnp.zeros((1, 128), F32)]
    for j in range(2):
        for kind in range(2):
            cols = slice(256 * j + 128 * kind, 256 * j + 128 * kind + 128)
            raw = raw_ref[:, cols]
            upstream = grad_ref[j, :, 128 * kind : 128 * kind + 128]
            turned = upstream.astype(F32)
            turned = turned * cosine - swap_halves(turned) * sine
            scale = lax.rsqrt(head_mean(raw * raw) + EPSILON)
            unit = raw * scale
            gain_sums[kind] += jnp.sum(turned * unit, axis=0, keepdims=True)
            turned = turned * head_gain_ref[kind : kind + 1, :]
            grad = scale * (turned - unit * head_mean(turned * unit))
            grad = grad.astype(BF)
            if kind == 1:
                grad = jnp.where(lane < HD, grad, upstream)
            pieces.append(grad)
    gain_grad_ref[0:1, :] += gain_sums[0]
    gain_grad_ref[1:2, :] += gain_sums[1]
    grads = jnp.concatenate(pieces, axis=1)
    part_ref[...] = dot(grads, w_ref[...], NT).astype(BF)
    acc_ref[...] += dot(normed_ref[...], grads, TN)

    @pl.when(step == pl.num_programs(0) - 1)
    def finish():
        dw_ref[...] = acc_ref[...].astype(BF)


def project_back(raw, grad, normed, weight, cosine, sine, head_gain):
    rows, depth = normed.shape
    cols = weight.shape[1]
    tile = 256
    return pl.pallas_call(
        project_back_body,
        grid=(rows // tile,),
        in_specs=[
            pl.BlockSpec((tile, cols), lambda i: (i, 0)),
            pl.BlockSpec((2, tile, 256), lambda i: (0, i, 0)),
            pl.BlockSpec((tile, depth), lambda i: (i, 0)),
            pl.BlockSpec((depth, cols), lambda i: (0, 0)),
            pl.BlockSpec((tile, 128), lambda i: (i, 0)),
            pl.BlockSpec((tile, 128), lambda i: (i, 0)),
            pl.BlockSpec((8, 128), lambda i: (0, 0)),
        ],
        out_specs=(
            pl.BlockSpec((tile, depth), lambda i: (i, 0)),
            pl.BlockSpec((depth, cols), lambda i: (0, 0)),
            pl.BlockSpec((8, 128), lambda i: (0, 0)),
        ),
        out_shape=(
            jax.ShapeDtypeStruct((rows, depth), BF),
            jax.ShapeDtypeStruct((depth, cols), BF),
            jax.ShapeDtypeStruct((8, 128), F32),
        ),
        scratch_shapes=[pltpu.VMEM((depth, cols), F32)],
        cost_estimate=pl.CostEstimate(
            flops=8 * rows * depth * cols, bytes_accessed=8 << 20, transcendentals=0
        ),
        compiler_params=pltpu.CompilerParams(vmem_limit_bytes=40 << 20),
    )(raw, grad, normed, weight, cosine, sine, head_gain)


def permute(x, axis, move):
    count = lax.axis_size(axis)
    return lax.ppermute(x, axis, [(i, move(i) % count) for i in range(count)])


def gather_head(x, place):
    if lax.axis_size("head") != 4:
        return lax.all_gather(x, "head", axis=0, tiled=True)
    half = x.shape[0] // 2
    one = permute(x, "head", lambda i: i ^ 1)
    two = permute(x, "head", lambda i: i ^ 2)
    upper = permute(one[:half], "head", lambda i: i ^ 2)
    lower = permute(two[half:], "head", lambda i: i ^ 1)
    rows = x.shape[0]
    out = jnp.zeros((4 * rows, x.shape[1]), x.dtype)
    for part, other, shift in ((x, 0, 0), (one, 1, 0), (two, 2, 0), (upper, 3, 0), (lower, 3, half)):
        out = lax.dynamic_update_slice(out, part, ((place ^ other) * rows + shift, 0))
    return out


def sum_head(x, place):
    if lax.axis_size("head") != 4:
        return lax.psum_scatter(x, "head", scatter_dimension=0, tiled=True).astype(F32)
    rows = x.shape[0] // 4
    half = rows // 2

    def piece(other, shift):
        return lax.dynamic_slice(x, ((place ^ other) * rows + shift, 0), (half, x.shape[1]))

    first = permute(
        jnp.concatenate([piece(1, 0), piece(3, 0)], axis=0), "head", lambda i: i ^ 1
    ).astype(F32)
    second = permute(
        jnp.concatenate([piece(2, half), piece(3, half)], axis=0), "head", lambda i: i ^ 2
    ).astype(F32)
    upper_far = (first[half:] + piece(2, 0).astype(F32)).astype(BF)
    lower_far = (second[half:] + piece(1, half).astype(F32)).astype(BF)
    upper = permute(upper_far, "head", lambda i: i ^ 2).astype(F32)
    lower = permute(lower_far, "head", lambda i: i ^ 1).astype(F32)
    return jnp.concatenate(
        [
            piece(0, 0).astype(F32) + first[:half] + upper,
            piece(0, half).astype(F32) + second[:half] + lower,
        ],
        axis=0,
    )


def mirror(x):
    count = lax.axis_size("blk")
    return permute(x, "blk", lambda i: count - i if i % 2 else i)


def per_device(
    inputs,
    query_weight,
    key_weight,
    value_weight,
    mixing_weight,
    gate_weight,
    up_weight,
    down_weight,
    attention_gain,
    feedforward_gain,
    query_gain,
    key_gain,
    cotangent,
):
    heads = lax.axis_size("head")
    blocks = lax.axis_size("blk")
    chips = blocks // 2
    place = lax.axis_index("head")
    block = lax.axis_index("blk")
    core = block % 2
    chip = block // 2
    rows, depth = inputs.shape
    span = rows * heads
    piece = query_weight.shape[0]
    width = gate_weight.shape[1] // heads
    shared = KV // heads
    unit_heads = HQ // heads // 2
    unit_cols = unit_heads * HD

    def other_core(x):
        return permute(x, "blk", lambda i: i ^ 1)

    def by_core(mine, theirs):
        first = core == 0
        return jnp.stack([jnp.where(first, mine, theirs), jnp.where(first, theirs, mine)])

    low_rows = lax.all_gather(jnp.concatenate([mixing_weight, down_weight], axis=0), "blk", axis=0)
    mixing_rows = low_rows[:, :piece].reshape(blocks * piece, depth)
    down_full = low_rows[:, piece:].reshape(-1, depth)

    qkv_own = jnp.concatenate(
        [
            jnp.pad(
                query_weight.reshape(piece, heads, 2, unit_cols),
                ((0, 0), (0, 0), (0, 0), (0, 128 - unit_cols)),
            ),
            jnp.repeat(key_weight.reshape(piece, heads, shared, HD), 2 // shared, axis=2),
            jnp.repeat(value_weight.reshape(piece, heads, shared, HD), 2 // shared, axis=2),
        ],
        axis=-1,
    ).reshape(piece, heads, 512)
    gains = jnp.pad(jnp.stack([attention_gain, feedforward_gain], axis=1), ((0, 0), (0, 126)))
    qkv_send = jnp.concatenate(
        [qkv_own, jnp.broadcast_to(gains[:, None, :], (piece, heads, 128))], axis=-1
    ).transpose(1, 0, 2)
    qkv_piece = lax.all_to_all(qkv_send, "head", 0, 0, tiled=True)
    gate_up_send = jnp.concatenate(
        [gate_weight.reshape(piece, heads, width), up_weight.reshape(piece, heads, width)], axis=-1
    ).transpose(1, 0, 2)
    gate_up_piece = lax.all_to_all(gate_up_send, "head", 0, 0, tiled=True)
    qkv_ext = lax.all_gather(qkv_piece, "blk", axis=1).reshape(depth, 640)
    qkv_full = qkv_ext[:, :512]
    attention_row = qkv_ext[:, 512].astype(F32)[None, :]
    feed_row = qkv_ext[:, 513].astype(F32)[None, :]
    gate_up = lax.all_gather(gate_up_piece, "blk", axis=1).reshape(depth, 2 * width)

    span_index = jnp.where(core == 0, block, blocks - block)
    positions = (span_index * span + jnp.arange(span, dtype=jnp.int32)).astype(F32)
    lane = jnp.arange(128, dtype=jnp.int32)
    frequency = jnp.exp(
        (lane % (HD // 2)).astype(F32) * (-2.0 * math.log(ROPE_BASE) / HD)
    )
    angles = positions[:, None] * frequency[None, :]
    cosine = jnp.cos(angles)
    sine = jnp.sin(angles) * jnp.where(lane % HD < HD // 2, -1.0, 1.0)
    head_gain = jnp.concatenate(
        [
            jnp.tile(query_gain.astype(F32), 2)[None, :],
            jnp.tile(key_gain.astype(F32), 2)[None, :],
            jnp.zeros((6, 128), F32),
        ],
        axis=0,
    )

    own = mirror(inputs)
    own_float = own.astype(F32)
    gathered = gather_head(own, place)
    normed, raw, packet = project(gathered, attention_row, qkv_full, cosine, sine, head_gain)

    def to_pairs(x):
        keep = jnp.where(core == 0, x[0], x[1])
        send = jnp.where(core == 0, x[1], x[0])
        return by_core(keep, other_core(send))

    both = to_pairs(packet).reshape(2 * span, 256)
    kv = both[:, 128:]
    zeros = jnp.zeros((2 * span, HD), BF)
    query = jnp.stack(
        [
            jnp.concatenate([both[:, HD * i : HD * (i + 1)], zeros], axis=1)
            for i in range(unit_heads)
        ]
    )

    def low_slot(z):
        return (4 * z >= blocks).astype(jnp.int32)

    def reach(z):
        return jnp.abs(4 * z - (blocks - 1))

    my_low = low_slot(chip)
    my_high = 1 - my_low

    def offsets(step):
        if step == 0:
            return span * jnp.stack([my_high, my_low])
        source = (chip - step) % chips
        low = low_slot(source)
        outer = reach(source) > reach(chip)
        return span * jnp.stack(
            [
                jnp.where(outer, my_low, my_high),
                low,
                my_high,
                jnp.where(outer, low, 1 - low),
            ]
        )

    def next_chip(x):
        return permute(x, "blk", lambda i: i + 2)

    kv_parts = [kv]
    for step in range(1, chips):
        kv_parts.append(next_chip(kv_parts[-1]))
    acc = None
    for step in range(chips):
        acc = attend(offsets(step), query, kv_parts[step], acc)
    total = acc[:, :, 0:1]
    mixture_float = acc[:, :, HD:] / total
    mixture_heads = mixture_float.astype(BF)
    mixture_rows = jnp.concatenate(list(mixture_heads), axis=1).reshape(2, span, unit_cols)

    def from_pairs(x):
        keep = jnp.where(core == 0, x[0], x[1])
        send = jnp.where(core == 0, x[1], x[0])
        return by_core(keep, other_core(send))

    mixture_two = from_pairs(mixture_rows)
    mixture_span = jnp.concatenate([mixture_two[0], mixture_two[1]], axis=1)
    mixture = lax.all_to_all(mixture_span, "head", 0, 1, tiled=True)
    mixing_full = gather_head(mixing_rows, place)
    hidden = own_float + dot(mixture, mixing_full)
    hidden_scale = lax.rsqrt(jnp.mean(hidden * hidden, axis=1, keepdims=True) + EPSILON)
    normed_ffn = (hidden * hidden_scale * feed_row).astype(BF)
    ffn_rows = gather_head(normed_ffn, place)
    own_cot = mirror(cotangent)
    cot_rows = gather_head(own_cot, place)
    gate_value = dot(ffn_rows, gate_up[:, :width])
    up_value = dot(ffn_rows, gate_up[:, width:])
    gate_sigmoid = jax.nn.sigmoid(gate_value)
    activation = (gate_value * gate_sigmoid * up_value).astype(BF)
    activation_grad = dot(cot_rows, down_full, NT).astype(BF).astype(F32)
    gate_grad = (
        activation_grad * up_value * gate_sigmoid * (1.0 + gate_value * (1.0 - gate_sigmoid))
    ).astype(BF)
    up_grad = (activation_grad * gate_value * gate_sigmoid).astype(BF)
    gate_up_grad = jnp.concatenate([gate_grad, up_grad], axis=1)
    normed_ffn_grad = sum_head(dot(gate_up_grad, gate_up, NT).astype(BF), place)

    down_term = sum_head(dot(activation, down_full).astype(BF), place)
    output = mirror((hidden + down_term).astype(BF))
    down_grad = dot(activation, cot_rows, TN).astype(BF)
    down_sum = lax.psum_scatter(down_grad, "blk", scatter_dimension=0, tiled=True).astype(F32)

    def regroup(grad):
        return (
            grad.reshape(heads, blocks, piece, grad.shape[-1])
            .transpose(1, 0, 2, 3)
            .reshape(grad.shape)
        )

    def to_owner(grad):
        part = lax.psum_scatter(regroup(grad), "blk", scatter_dimension=0, tiled=True)
        part = lax.all_to_all(
            part.reshape(heads, piece, -1), "head", split_axis=0, concat_axis=0, tiled=True
        )
        return part.astype(F32)

    gate_up_sum = to_owner(dot(ffn_rows, gate_up_grad, TN).astype(BF))

    unit_ffn = hidden * hidden_scale
    lifted = normed_ffn_grad * feed_row
    hidden_grad = own_cot.astype(F32) + hidden_scale * (
        lifted - unit_ffn * jnp.mean(lifted * unit_ffn, axis=1, keepdims=True)
    )
    hidden_low = hidden_grad.astype(BF)
    mixture_grad = dot(hidden_low, mixing_full, NT).astype(BF)
    hidden_rows = gather_head(hidden_low, place)
    mixing_grad = dot(mixture_span, hidden_rows, TN).astype(BF)
    mixing_sum = lax.psum_scatter(mixing_grad, "blk", scatter_dimension=0, tiled=True).astype(F32)

    grad_span = lax.all_to_all(mixture_grad, "head", 1, 0, tiled=True)
    grad_rows = to_pairs(
        jnp.stack([grad_span[:, :unit_cols], grad_span[:, unit_cols:]])
    ).reshape(2 * span, unit_cols)
    grad_heads = jnp.stack(
        [grad_rows[:, HD * i : HD * (i + 1)] for i in range(unit_heads)]
    ).astype(F32)
    inverse = 1.0 / total
    shift = jnp.sum(grad_heads * mixture_float, axis=-1, keepdims=True) * (-inverse)
    shift_high = shift.astype(BF)
    rest = shift - shift_high.astype(F32)
    shift_mid = rest.astype(BF)
    shift_low = (rest - shift_mid.astype(F32)).astype(BF)
    out_grad = jnp.concatenate(
        [
            shift_high,
            shift_mid,
            shift_low,
            jnp.zeros((unit_heads, 2 * span, HD - 3), BF),
            (grad_heads * inverse).astype(BF),
        ],
        axis=-1,
    )
    query_acc = None
    travelling = None
    for step in list(range(1, chips)) + [0]:
        args = (offsets(step), query, out_grad, kv_parts[step])
        if query_acc is None:
            query_acc, kv_grad = attend_back(
                *args, jnp.zeros(query.shape, F32) if step else None
            )
        else:
            if step == 0:
                local_acc, kv_grad = attend_back(*args, None)
                query_acc = query_acc + local_acc
            else:
                query_acc, kv_grad = attend_back(*args, query_acc)
        if travelling is not None:
            kv_grad = kv_grad + travelling.astype(F32)
        if step:
            travelling = next_chip(kv_grad.astype(BF))
    query_rows_grad = jnp.concatenate(
        [query_acc[i, :, :HD] for i in range(unit_heads)]
        + [jnp.zeros((2 * span, 128 - unit_cols), F32)],
        axis=1,
    ) * (HD**-0.5)
    key_unit = jnp.where(lane < HD, math.log(2.0), 1.0)[None, :]
    grads = jnp.concatenate(
        [query_rows_grad.astype(BF), (kv_grad * key_unit).astype(BF)], axis=1
    ).reshape(2, span, 256)
    grads = from_pairs(grads)
    normed_part, qkv_grad, head_gain_grad = project_back(
        raw, grads, normed, qkv_full, cosine, sine, head_gain
    )
    normed_grad = sum_head(normed_part, place)
    input_scale = lax.rsqrt(jnp.mean(own_float * own_float, axis=1, keepdims=True) + EPSILON)
    unit = own_float * input_scale
    lifted = normed_grad * attention_row
    input_gradient = hidden_grad + input_scale * (
        lifted - unit * jnp.mean(lifted * unit, axis=1, keepdims=True)
    )
    input_gradient = mirror(input_gradient.astype(BF))

    head_gain_grad = head_gain_grad[:2, :]
    bit = 1
    while bit < heads:
        head_gain_grad += permute(head_gain_grad, "head", lambda i, bit=bit: i ^ bit)
        bit *= 2
    bit = 1
    while bit < blocks:
        head_gain_grad += permute(head_gain_grad, "blk", lambda i, bit=bit: i ^ bit)
        bit *= 2
    query_gain_sum = head_gain_grad[0, :HD] + head_gain_grad[0, HD:]
    key_gain_sum = head_gain_grad[1, :HD]

    qkv_sum = to_owner(qkv_grad)
    attention_gain_sum = jnp.sum(
        qkv_sum * qkv_own.transpose(1, 0, 2).astype(F32), axis=(0, 2)
    ) / attention_gain.astype(F32)
    feed_gain_sum = jnp.sum(
        gate_up_sum * gate_up_send.astype(F32), axis=(0, 2)
    ) / feedforward_gain.astype(F32)
    qkv_cols = qkv_sum.transpose(1, 0, 2).reshape(piece, heads, 2, 256)
    gate_up_cols = gate_up_sum.transpose(1, 0, 2)

    def per_head(cols):
        return cols.reshape(piece, heads, shared, 2 // shared, HD).sum(axis=3).reshape(piece, -1)

    return (
        output,
        input_gradient,
        qkv_cols[..., :unit_cols].reshape(piece, -1),
        per_head(qkv_cols[..., 128 : 128 + HD]),
        per_head(qkv_cols[..., 128 + HD :]),
        mixing_sum,
        gate_up_cols[..., :width].reshape(piece, -1),
        gate_up_cols[..., width:].reshape(piece, -1),
        down_sum,
        attention_gain_sum,
        feed_gain_sum,
        query_gain_sum,
        key_gain_sum,
    )


def solution(mesh):
    in_specs = (
        P(("blk", "head"), None),
        P(("head", "blk"), None),
        P(("head", "blk"), None),
        P(("head", "blk"), None),
        P(("head", "blk"), None),
        P(("head", "blk"), None),
        P(("head", "blk"), None),
        P(("head", "blk"), None),
        P(("head", "blk")),
        P(("head", "blk")),
        P(),
        P(),
        P(("blk", "head"), None),
    )
    out_specs = (
        P(("blk", "head"), None),
        P(("blk", "head"), None),
        P(("head", "blk"), None),
        P(("head", "blk"), None),
        P(("head", "blk"), None),
        P(("head", "blk"), None),
        P(("head", "blk"), None),
        P(("head", "blk"), None),
        P(("head", "blk"), None),
        P(("head", "blk")),
        P(("head", "blk")),
        P(),
        P(),
    )
    return jax.shard_map(
        per_device, mesh=mesh, in_specs=in_specs, out_specs=out_specs, check_vma=False
    )
```

```python
import functools
import math

import jax
import jax.numpy as jnp
from jax import lax
from jax.experimental import pallas as pl
from jax.experimental.pallas import tpu as pltpu
from jax.sharding import PartitionSpec as P

HQ = 16
KV = 8
HD = 64
EPSILON = 1e-05
ROPE_BASE = 1000000.0
TILE = 1024
QUERY_UNIT = math.log2(math.e) * HD**-0.5

BF = jnp.bfloat16
F32 = jnp.float32
NT = (((1,), (1,)), ((), ()))
NN = (((1,), (0,)), ((), ()))
TN = (((0,), (0,)), ((), ()))
VM = pl.BlockSpec(memory_space=pltpu.VMEM)
SM = pl.BlockSpec(memory_space=pltpu.SMEM)


def dot(a, b, dims=NN):
    return lax.dot_general(a, b, dims, preferred_element_type=F32)


def run(body, outs, args, flops=0, scalars=None, scratch=(), exps=0, limit=40, far=(), stay=()):
    args = list(args)
    hbm = pl.BlockSpec(memory_space=pltpu.HBM)
    specs = [hbm if i in far or i in stay else VM for i in range(len(args))]
    many = isinstance(outs, (list, tuple))
    outs = list(outs) if many else [outs]
    size = sum(math.prod(a.shape) * a.dtype.itemsize for a in outs + args)
    scratch = list(scratch)
    if far:
        own, lead = len(scratch), 0 if scalars is None else 1
        scratch += [pltpu.VMEM(args[i].shape, args[i].dtype) for i in far]
        scratch.append(pltpu.SemaphoreType.DMA((len(far),)))
        inner = body

        def body(*refs):
            refs = list(refs)
            sems = refs.pop()
            buffers = refs[-len(far) :]
            refs = refs[: -len(far)]
            copies = [
                pltpu.make_async_copy(refs[lead + i], buffer, sems.at[k])
                for k, (i, buffer) in enumerate(zip(far, buffers, strict=True))
            ]
            for copy in copies:
                copy.start()
            for copy in copies:
                copy.wait()
            for i, buffer in zip(far, buffers, strict=True):
                refs[lead + i] = buffer
            inner(*refs)

    if scalars is not None:
        args = [jnp.stack([jnp.asarray(v, jnp.int32) for v in scalars])] + args
        specs = [SM] + specs
    return pl.pallas_call(
        body,
        out_shape=tuple(outs) if many else outs[0],
        in_specs=specs,
        out_specs=tuple([VM] * len(outs)) if many else VM,
        scratch_shapes=scratch,
        cost_estimate=pl.CostEstimate(flops=1, bytes_accessed=1, transcendentals=0),
        compiler_params=pltpu.CompilerParams(vmem_limit_bytes=60 << 20),
    )(*args)


def shape(*dims, dtype=BF):
    return jax.ShapeDtypeStruct(dims, dtype)


def pair_list(off_ref, span, count):
    return [
        (pl.multiple_of(off_ref[2 * i], span), pl.multiple_of(off_ref[2 * i + 1], span))
        for i in range(count)
    ]


def attend_body(span, heads, local, first, last, off_ref, q_ref, kv_ref, *refs):
    refs = list(refs)
    acc_ref = None if first else refs.pop(0)
    out_ref = refs.pop(0)
    mix_ref = refs.pop(0) if last else None
    ones_ref = refs.pop(0)
    lane = lax.broadcasted_iota(jnp.int32, ones_ref.shape, 1)
    ones_ref[...] = jnp.where(lane < HD, jnp.ones((), BF), kv_ref[...])
    out_ref[...] = jnp.zeros_like(out_ref) if first else acc_ref[...]
    block = min(span, TILE)

    def block_pair(head, q_off, k_off):
        rows = pl.ds(q_off, block)
        keys = pl.ds(k_off, block)
        query = q_ref[rows, 128 * head : 128 * head + 128]
        weight = jnp.exp2(dot(query, kv_ref[keys, :], NT)).astype(BF)
        out_ref[head, rows, :] += dot(weight, ones_ref[keys, :])

    def full(q_off, k_off):
        for i in range(span // block):
            for j in range(span // block):
                for head in range(heads):
                    block_pair(head, q_off + i * block, k_off + j * block)

    def diagonal(start):
        for i in range(span // block):
            for j in range(i):
                for head in range(heads):
                    block_pair(head, start + i * block, start + j * block)
            diagonal_block(start + i * block)

    def diagonal_block(start):
        size = 256
        for head in range(heads):
            for i in range(block // size):
                rows = slice(start + i * size, start + (i + 1) * size)
                query = q_ref[rows, 128 * head : 128 * head + 128]
                total = None
                pieces = ([(0, i * size)] if i else []) + [(i * size, (i + 1) * size)]
                for low, high in pieces:
                    keys = slice(start + low, start + high)
                    weight = jnp.exp2(dot(query, kv_ref[keys, :], NT))
                    if low == i * size:
                        place = lax.broadcasted_iota(jnp.int32, (size, size), 0)
                        other = lax.broadcasted_iota(jnp.int32, (size, size), 1)
                        weight = jnp.where(other <= place, weight, 0.0)
                    part = dot(weight.astype(BF), ones_ref[keys, :])
                    total = part if total is None else total + part
                out_ref[head, rows, :] += total

    if local:
        diagonal(0)
        diagonal(span)
    for q_off, k_off in pair_list(off_ref, span, 1 if local else 2):
        full(q_off, k_off)
    if last:
        size = 256
        for i in range(2 * span // size):
            rows = slice(i * size, (i + 1) * size)
            left = lax.broadcasted_iota(jnp.int32, (size, 2 * HD), 1) < HD
            mixed = []
            for head in range(heads):
                total = out_ref[head, rows, :]
                mixed.append(total * pltpu.roll(1.0 / jnp.where(left, total, 1.0), HD, 1))
            out = jnp.where(left, pltpu.roll(mixed[0], HD, 1), mixed[1] if heads > 1 else 0.0)
            mix_ref[i * size // span, pl.ds(i * size % span, size), :] = out.astype(BF)


def attend(offsets, packets, kv, acc, local, last, heads):
    span = packets.shape[0] // 2
    outs = [shape(heads, 2 * span, 2 * HD, dtype=F32)]
    if last:
        outs.append(shape(2, span, 2 * HD))
    return run(
        functools.partial(attend_body, span, heads, local, acc is None, last),
        outs,
        [packets, kv] + ([] if acc is None else [acc]),
        flops=8 * heads * span * span * 256,
        scalars=offsets,
        scratch=[pltpu.VMEM((2 * span, 2 * HD), BF)],
        exps=2 * heads * span * span,
        far=() if local else (0,),
    )


def attend_back_body(
    span, heads, local, first, off_ref, q_ref, do_ref, kv_ref, *refs
):
    refs = list(refs)
    acc_ref = None if first else refs.pop(0)
    if local:
        dq_ref, dkv_ref, ones_ref, dv_ref = refs
    else:
        dq_ref, out_ref, ones_ref, dv_ref, dkv_ref = refs
    lane = lax.broadcasted_iota(jnp.int32, ones_ref.shape, 1)
    zero = jnp.zeros((), BF)
    ones_ref[...] = jnp.where(
        lane < HD, jnp.where(lane < 3, jnp.ones((), BF), zero), kv_ref[...]
    )
    block = min(span, TILE)
    for head in range(heads):
        dv_ref[head] = jnp.where(lane < HD, zero, do_ref[head])
    dq_ref[...] = jnp.zeros_like(dq_ref) if first else acc_ref[...]
    dkv_ref[...] = jnp.zeros_like(dkv_ref)

    def tile(head, rows, keys, mask):
        query = q_ref[rows, 128 * head : 128 * head + 128]
        pair = kv_ref[keys, :]
        weight = jnp.exp2(dot(pair, query, NT))
        if mask is not None:
            weight = jnp.where(mask, weight, 0.0)
        score_grad = (weight * dot(ones_ref[keys, :], do_ref[head, rows, :], NT)).astype(BF)
        dkv_ref[keys, :] += dot(weight.astype(BF), dv_ref[head, rows, :]) + dot(score_grad, query)
        dq_ref[head, rows, :] += dot(score_grad, pair, TN)

    def block_pair(head, q_off, k_off):
        tile(head, pl.ds(q_off, block), pl.ds(k_off, block), None)

    def full(q_off, k_off):
        for i in range(span // block):
            for j in range(span // block):
                for head in range(heads):
                    block_pair(head, q_off + i * block, k_off + j * block)

    def diagonal(start):
        for i in range(span // block):
            for j in range(i):
                for head in range(heads):
                    block_pair(head, start + i * block, start + j * block)
            diagonal_block(start + i * block)

    def diagonal_block(start):
        size = 256
        for head in range(heads):
            for i in range(block // size):
                rows = slice(start + i * size, start + (i + 1) * size)
                pieces = ([(0, i * size)] if i else []) + [(i * size, (i + 1) * size)]
                for low, high in pieces:
                    mask = None
                    if low == i * size:
                        key_place = lax.broadcasted_iota(jnp.int32, (size, size), 0)
                        mask = key_place <= lax.broadcasted_iota(jnp.int32, (size, size), 1)
                    tile(head, rows, slice(start + low, start + high), mask)

    if local:
        diagonal(0)
        diagonal(span)
    for q_off, k_off in pair_list(off_ref, span, 1 if local else 2):
        full(q_off, k_off)
    if not local:
        out_ref[...] = dkv_ref[...].astype(BF)


def attend_back(offsets, packets, out_grad, kv, acc, local):
    heads, rows = out_grad.shape[:2]
    span = rows // 2
    return run(
        functools.partial(attend_back_body, span, heads, local, acc is None),
        [shape(heads, rows, 2 * HD, dtype=F32), shape(rows, 2 * HD, dtype=F32 if local else BF)],
        [packets, out_grad, kv] + ([] if acc is None else [acc]),
        flops=20 * heads * span * span * 256,
        scalars=offsets,
        scratch=[pltpu.VMEM((rows, 2 * HD), BF), pltpu.VMEM((heads, rows, 2 * HD), BF)]
        + ([] if local else [pltpu.VMEM((rows, 2 * HD), F32)]),
        exps=2 * heads * span * span,
        limit=48,
        far=(0, 2),
    )


def out_grad_body(core_ref, mine_ref, theirs_ref, acc_ref, out_ref):
    heads, rows = acc_ref.shape[:2]
    size = 256
    lane = lax.broadcasted_iota(jnp.int32, (size, 2 * HD), 1)
    left = lane < HD
    for i in range(rows // size):
        here = slice(i * size, (i + 1) * size)
        if i * size < rows // 2:
            first = mine_ref[here, 0:128]
            second = mine_ref[here, 128:256]
            both = jnp.where(core_ref[0] == 0, first, second).astype(F32)
        else:
            both = theirs_ref[slice(i * size - rows // 2, (i + 1) * size - rows // 2), :].astype(F32)
        for head in range(heads):
            grad = pltpu.roll(both, HD, 1) if head == 0 else both
            total = acc_ref[head, here, :]
            inverse = pltpu.roll(1.0 / jnp.where(left, total, 1.0), HD, 1)
            scaled = grad * inverse
            delta = jnp.sum(
                jnp.where(left, 0.0, scaled * total * inverse), axis=1, keepdims=True
            )
            shift = jnp.broadcast_to(-delta, (size, 2 * HD))
            high = shift.astype(BF).astype(F32)
            rest = shift - high
            middle = rest.astype(BF).astype(F32)
            parts = jnp.where(lane == 0, high, jnp.where(lane == 1, middle, rest - middle))
            out = jnp.where(left, jnp.where(lane < 3, parts, 0.0), scaled)
            out_ref[head, here, :] = out.astype(BF)


def pack_body(dq_ref, dkv_ref, *refs):
    outs = refs[-2:]
    heads, rows = dq_ref.shape[:2]
    span = rows // 2
    size = 256
    lane = lax.broadcasted_iota(jnp.int32, (size, 2 * HD), 1)
    for i in range(rows // size):
        here = slice(i * size, (i + 1) * size)
        there = slice(i * size % span, i * size % span + size)
        out = outs[i * size // span]
        query = dq_ref[0, here, :]
        other = pltpu.roll(dq_ref[1, here, :], HD, 1) if heads > 1 else 0.0
        query = jnp.where(lane < HD, query, other) * (HD**-0.5)
        pair = dkv_ref[here, :]
        for more in refs[:-2]:
            pair = pair + more[here, :].astype(F32)
        pair = pair * jnp.where(lane < HD, math.log(2.0), 1.0)
        out[there, 0:128] = query.astype(BF)
        out[there, 128:256] = pair.astype(BF)


def swap_halves(x):
    lane = lax.broadcasted_iota(jnp.int32, x.shape, 1)
    return jnp.where(
        lane % HD < HD // 2, pltpu.roll(x, x.shape[1] - HD // 2, 1), pltpu.roll(x, HD // 2, 1)
    )


def head_mean(x):
    size = x.shape[1]
    first = lax.broadcasted_iota(jnp.int32, (size, size), 0) // HD
    second = lax.broadcasted_iota(jnp.int32, (size, size), 1) // HD
    ones = jnp.where(first == second, 1.0 / HD, 0.0).astype(BF)
    high = x.astype(BF)
    low = (x - high.astype(F32)).astype(BF)
    return dot(high, ones) + dot(low, ones)


def unit_norm(x):
    return x * lax.rsqrt(jnp.mean(x * x, axis=1, keepdims=True) + EPSILON)


def tiles_of(refs, size=256):
    for k, ref in enumerate(refs):
        step = min(size, ref.shape[0])
        for low in range(0, ref.shape[0], step):
            yield k, low, step


def assemble_body(heads, index_ref, mine_ref, theirs_ref, out_ref):
    count = mine_ref.shape[0]
    for r in range(count):
        for h in range(heads):
            row = index_ref[2 * count + h]
            out_ref[row, index_ref[r]] = mine_ref[r, h]
            out_ref[row, index_ref[count + r]] = theirs_ref[r, h]


def project_body(count, heads, at_ref, *refs):
    x_refs = refs[:count]
    w_ref, cos_ref, sin_ref, head_gain_ref, keep_ref, send_ref, rows_ref = refs[count:]
    core = at_ref[count]
    rows_ref[...] = w_ref[:, 512:640].astype(F32).T[0:8]
    gain = rows_ref[0:1, :]
    for k, low, size in tiles_of(x_refs):
        start = pl.ds(pl.multiple_of(at_ref[k] + low, 128), size)
        normed = (unit_norm(x_refs[k][low : low + size, :].astype(F32)) * gain).astype(BF)
        cosine, sine = cos_ref[start, :], sin_ref[start, :]
        lane = lax.broadcasted_iota(jnp.int32, cosine.shape, 1)
        for unit, out_ref in ((core, keep_ref), (1 - core, send_ref)):
            raw = dot(normed, w_ref[:, pl.ds(pl.multiple_of(256 * unit, 256), 256)])
            query, pair = raw[:, :128], raw[:, 128:]
            query = query * lax.rsqrt(head_mean(query * query) + EPSILON) * head_gain_ref[0:1, :]
            query = (query * cosine + swap_halves(query) * sine) * QUERY_UNIT
            out_ref[start, 0:128] = jnp.where(lane < HD, query, 0.0).astype(BF)
            if heads > 1:
                shifted = pltpu.roll(query, HD, 1)
                out_ref[start, 128:256] = jnp.where(lane < HD, shifted, 0.0).astype(BF)
            key = pair * lax.rsqrt(head_mean(pair * pair) + EPSILON) * head_gain_ref[1:2, :]
            key = key * cosine + swap_halves(key) * sine
            out_ref[start, 128 * heads : 128 * heads + 128] = jnp.where(lane < HD, key, pair).astype(BF)


def project_back_body(count, outs, dims, at_ref, *refs):
    x_refs = refs[:count]
    w_ref, rows_ref, mixing_ref, cos_ref, sin_ref, mine_ref, theirs_ref, head_gain_ref = refs[
        count : count + 8
    ]
    part_refs = refs[count + 8 : count + 8 + outs]
    dw_ref, acc_ref = refs[count + 8 + outs :]
    core = at_ref[count]
    gain = rows_ref[0:1, :]
    gain_sums = [jnp.zeros((1, 128), F32), jnp.zeros((1, 128), F32)]
    done = 0
    for k, low, size in tiles_of(x_refs):
        start = pl.ds(pl.multiple_of(at_ref[k] + low, 128), size)
        normed = (unit_norm(x_refs[k][low : low + size, :].astype(F32)) * gain).astype(BF)
        cosine, sine = cos_ref[start, :], sin_ref[start, :]
        lane = lax.broadcasted_iota(jnp.int32, cosine.shape, 1)
        part = None
        for u, (unit, grad_ref) in enumerate(((core, mine_ref), (1 - core, theirs_ref))):
            cols = pl.ds(pl.multiple_of(256 * unit, 256), 256)
            weight = w_ref[:, cols]
            raw_both = dot(normed, weight)
            pieces = []
            for kind in range(2):
                raw = raw_both[:, 128 * kind : 128 * kind + 128]
                upstream = grad_ref[start, 128 * kind : 128 * kind + 128].astype(F32)
                turned = upstream * cosine - swap_halves(upstream) * sine
                scale = lax.rsqrt(head_mean(raw * raw) + EPSILON)
                one = raw * scale
                gain_sums[kind] += jnp.sum(turned * one, axis=0, keepdims=True)
                turned = turned * head_gain_ref[kind : kind + 1, :]
                grad = scale * (turned - one * head_mean(turned * one))
                if kind == 1:
                    grad = jnp.where(lane < HD, grad, upstream)
                pieces.append(grad.astype(BF))
            grads = jnp.concatenate(pieces, axis=1)
            term = dot(grads, weight, NT)
            part = term if part is None else part + term
            update = dot(normed, grads, TN)
            acc_ref[u] = update if done == 0 else acc_ref[u] + update
        scatter_rows(part_refs, done, part.astype(BF))
        done += size
    highs = [g.astype(BF) for g in gain_sums]
    lows = [(g - x.astype(F32)).astype(BF) for g, x in zip(gain_sums, highs, strict=True)]
    gain_row = jnp.concatenate(highs + lows, axis=1)
    gain_rows = jnp.concatenate([gain_row, jnp.zeros((7, 512), BF)], axis=0)
    blocks, heads, rows = dims
    for u, unit in enumerate((core, 1 - core)):
        cols = pl.ds(pl.multiple_of(256 * unit, 256), 256)
        for h in range(heads):
            for b in range(blocks):
                low = (h * blocks + b) * rows
                at = h * (rows + 8)
                dw_ref[b, at : at + rows, cols] = acc_ref[u, low : low + rows, :].astype(BF)
                dw_ref[b, at + rows : at + rows + 8, :] = gain_rows
    for b in range(blocks):
        for i in range(mixing_ref.shape[1] // 512):
            at = heads * (rows + 8) + i * rows
            dw_ref[b, at : at + rows, :] = mixing_ref[
                b * rows : (b + 1) * rows, 512 * i : 512 * (i + 1)
            ]


def mix_body(places, at_ref, a_ref, *refs):
    m_refs = refs[: len(places)]
    own_ref, rows_ref, hidden_ref, normed_ref = refs[len(places) :]
    hidden = own_ref[...].astype(F32)
    cols = a_ref.shape[2]
    for (other, shift), m_ref in zip(places, m_refs, strict=True):
        if other is None:
            for h in range(a_ref.shape[0]):
                hidden += dot(a_ref[h], m_ref[h * cols : (h + 1) * cols, :])
        else:
            rows = m_ref.shape[0]
            hidden += dot(a_ref[at_ref[0] ^ other, :, shift : shift + rows], m_ref[...])
    hidden_ref[...] = hidden
    normed_ref[...] = (unit_norm(hidden) * rows_ref[1:2, :]).astype(BF)


def add_parts(addends, refs, rows, depth):
    half = rows // 2
    sums = [jnp.zeros((half, depth), F32), jnp.zeros((half, depth), F32)]
    for low, ref in zip(addends, refs, strict=True):
        whole = len(refs) == 1 or ref is refs[0]
        for i in range(2):
            if whole:
                sums[i] += ref[i * half : (i + 1) * half, :].astype(F32)
            elif low == i * half:
                sums[i] += ref[0:half, :].astype(F32)
    return jnp.concatenate(sums, axis=0)


def hidden_back_body(places, addends, at_ref, hidden_ref, cot_ref, rows_ref, *refs):
    m_refs = refs[: len(places)]
    add_refs = refs[len(places) : len(places) + len(addends)]
    grad_ref, low_ref, mixture_ref = refs[len(places) + len(addends) :]
    hidden = hidden_ref[...]
    upstream = add_parts(addends, add_refs, *hidden.shape) * rows_ref[1:2, :]
    scale = lax.rsqrt(jnp.mean(hidden * hidden, axis=1, keepdims=True) + EPSILON)
    one = hidden * scale
    grad = cot_ref[...].astype(F32) + scale * (
        upstream - one * jnp.mean(upstream * one, axis=1, keepdims=True)
    )
    grad_ref[...] = grad
    low = grad.astype(BF)
    low_ref[...] = low
    cols = mixture_ref.shape[2]
    for (other, shift), m_ref in zip(places, m_refs, strict=True):
        if other is None:
            for h in range(mixture_ref.shape[0]):
                mixture_ref[h] = dot(low, m_ref[h * cols : (h + 1) * cols, :], NT).astype(BF)
        else:
            rows = m_ref.shape[0]
            mixture_ref[at_ref[0] ^ other, :, shift : shift + rows] = dot(
                low, m_ref[...], NT
            ).astype(BF)


def input_back_body(addends, own_ref, grad_ref, rows_ref, *refs):
    out_ref = refs[-1]
    own = own_ref[...].astype(F32)
    upstream = add_parts(addends, refs[:-1], *own.shape) * rows_ref[0:1, :]
    scale = lax.rsqrt(jnp.mean(own * own, axis=1, keepdims=True) + EPSILON)
    one = own * scale
    grad = grad_ref[...] + scale * (
        upstream - one * jnp.mean(upstream * one, axis=1, keepdims=True)
    )
    out_ref[...] = grad.astype(BF)


def finish_feed_body(heads, order_ref, part_ref, weight_ref, gate_ref, up_ref, dot_ref):
    width = part_ref.shape[2]
    total = jnp.zeros(dot_ref.shape, F32)
    for k in range(heads):
        start = order_ref[k] * (width // 2)
        for n in range(0, width, 128):
            value = part_ref[k, :, n : n + 128].astype(F32)
            total += value * weight_ref[order_ref[k], :, n : n + 128].astype(F32)
            out = gate_ref if n % 256 == 0 else up_ref
            out[:, pl.ds(pl.multiple_of(start + n // 256 * 128, 128), 128)] = value
    dot_ref[...] = jnp.broadcast_to(jnp.sum(total, axis=1, keepdims=True), total.shape)


def finish_projections_body(heads, unit_heads, order_ref, part_ref, weight_ref, *refs):
    q_ref, *kv_refs, dot_ref, gain_ref = refs
    rows = dot_ref.shape[0]
    total = jnp.zeros(dot_ref.shape, F32)
    gains = jnp.zeros((8, 512), F32)
    lane = lax.broadcasted_iota(jnp.int32, (rows, 128), 1)
    for k in range(heads):
        head = order_ref[k]
        value = part_ref[k, 0:rows, :].astype(F32)
        gains += part_ref[k, rows : rows + 8, :].astype(F32)
        product = value * weight_ref[head].astype(F32)
        for n in range(0, 512, 128):
            total += product[:, n : n + 128]
        spot = pl.ds(pl.multiple_of(head * 128, 128), 128)
        first, second = value[:, 128:256], value[:, 384:512]
        if unit_heads == 2:
            start = pl.multiple_of(head * 256, 256)
            q_ref[:, pl.ds(start, 128)] = value[:, 0:128]
            q_ref[:, pl.ds(start + 128, 128)] = value[:, 256:384]
            k_ref, v_ref = kv_refs
            k_ref[:, spot] = jnp.where(lane < HD, first, pltpu.roll(second, HD, 1))
            v_ref[:, spot] = jnp.where(lane < HD, pltpu.roll(first, HD, 1), second)
        else:
            q_ref[:, spot] = jnp.where(
                lane < HD, value[:, 0:128], pltpu.roll(value[:, 256:384], HD, 1)
            )
            kv_refs[0][:, spot] = first + second
    dot_ref[...] = jnp.broadcast_to(jnp.sum(total, axis=1, keepdims=True), total.shape)
    gain_ref[...] = gains[:, 0:256] + gains[:, 256:512]


def output_body(addends, hidden_ref, *refs):
    refs[-1][...] = (
        hidden_ref[...] + add_parts(addends, refs[:-1], *hidden_ref.shape)
    ).astype(BF)


def joined(refs, scratch):
    if len(refs) == 1:
        return refs[0]
    at = 0
    for ref in refs:
        scratch[at : at + ref.shape[0], :] = ref[...]
        at += ref.shape[0]
    return scratch


def column_tiles(width, size=512):
    return [(n, min(size, width - n)) for n in range(0, width, size)]


def activation_grad_body(count, order_ref, *refs):
    c_refs, down_ref, out_refs, scratch = refs[:count], refs[count], refs[count + 1 : -1], refs[-1]
    cot = joined(c_refs, scratch)
    for n, size in column_tiles(down_ref.shape[0]):
        grad = dot(cot[...], down_ref[n : n + size, :], NT).astype(BF)
        at = 0
        for out in out_refs:
            out[:, n : n + size] = grad[at : at + out.shape[0]]
            at += out.shape[0]


def feed_forward_body(count, first, outs, place_ref, *refs):
    x_refs, grad_ref, weight_ref = refs[:count], refs[count], refs[count + 1]
    act_ref, out_ref = refs[count + 2 : count + 4]
    back_refs, scratch = refs[count + 4 : count + 4 + outs], refs[-3]
    gu_ref, sems = refs[-2:]
    heads, blocks, piece, width = gu_ref.shape
    depth = heads * blocks * piece
    copies = [
        pltpu.make_async_copy(weight_ref.at[:, h], gu_ref.at[place_ref[h]], sems.at[h])
        for h in range(heads)
    ]
    for copy in copies:
        copy.start()
    x = joined(x_refs, scratch)
    for copy in copies:
        copy.wait()
    for n, size in column_tiles(width):
        both = dot(x[...], gu_ref[:, :, :, n : n + size].reshape(depth, size))
        for m in range(0, size, 256):
            gate, up = both[:, m : m + 128], both[:, m + 128 : m + 256]
            cols = slice((n + m) // 2, (n + m) // 2 + 128)
            grad = grad_ref[:, cols].astype(F32)
            sig = jax.nn.sigmoid(gate)
            swish = gate * sig
            act_ref[:, cols] = (swish * up).astype(BF)
            out_ref[:, n + m : n + m + 128] = (
                grad * up * sig * (1.0 + gate * (1.0 - sig))
            ).astype(BF)
            out_ref[:, n + m + 128 : n + m + 256] = (grad * swish).astype(BF)
    for n, size in column_tiles(depth):
        group = size * heads // depth if size * heads >= depth else 0
        if group:
            first_head = n * heads // depth
            weight = gu_ref[first_head : first_head + group].reshape(size, width)
        back = dot(out_ref[...], weight, NT).astype(BF)
        cols = slice(n, n + size)
        if first is None:
            scatter_rows(back_refs, 0, back, cols)
        elif first:
            back_refs[0][:, cols] = back
        else:
            scatter_rows([None, *back_refs], x.shape[0] // 3, back, cols)


def feed_forward(xs, grad, gate_up, first):
    blocks, heads, piece, width = gate_up.shape
    depth = heads * blocks * piece
    rows = grad.shape[0]
    place = lax.axis_index("head")
    if first is None:
        outs = [shape(rows, depth)]
    elif first:
        outs = [shape(rows, depth)]
    else:
        outs = part_outs(rows // 3, depth)[1:]
    res = run(
        functools.partial(feed_forward_body, len(xs), first, len(outs)),
        [shape(rows, width // 2), shape(rows, width)] + outs,
        list(xs) + [grad, gate_up],
        flops=4 * rows * depth * width,
        exps=rows * width // 2,
        scalars=[place ^ k for k in range(heads)],
        scratch=[
            pltpu.VMEM((rows, depth), BF),
            pltpu.VMEM((heads, blocks, piece, width), BF),
            pltpu.SemaphoreType.DMA((heads,)),
        ],
        limit=48,
        stay=(len(xs) + 1,),
    )
    return res[0], res[1], res[2:]


def down_body(count, outs, *refs):
    a_refs, down_ref, out_refs, scratch = refs[:count], refs[count], refs[count + 1 : -1], refs[-1]
    act = joined(a_refs, scratch)
    for n, size in column_tiles(down_ref.shape[1]):
        scatter_rows(
            out_refs,
            0,
            dot(act[...], down_ref[:, n : n + size]).astype(BF),
            slice(n, n + size),
        )


def packed_rows(blocks, heads, piece, cols, width):
    chunks = cols // 1024
    rest = cols - 1024 * chunks
    aside = 1024 // rest if rest else heads
    tail = -(-heads // aside) * piece if rest else 0
    return chunks, rest, aside, chunks * heads * piece + tail, width // blocks


def weight_grad_body(counts, dims, packed, *refs):
    refs = list(refs)
    x_refs, c_refs, g_refs, a_refs = ([refs.pop(0) for _ in range(n)] for n in counts)
    out_ref, down_ref, x_all, c_all = (refs[0], refs[3], *refs[1:3]) if packed else refs
    blocks, heads, piece, cols, width = dims
    chunks, rest, aside, start, share = packed_rows(blocks, heads, piece, cols, width)

    def product(left, right, tile):
        total, at = None, 0
        for ref in right:
            here = slice(at, at + ref.shape[0])
            term = dot(left[here, :], ref[:, tile], TN)
            total = term if total is None else total + term
            at += ref.shape[0]
        return total.astype(BF)

    x = joined(x_refs, x_all)
    for n, size in column_tiles(cols):
        total = product(x, g_refs, slice(n, n + size))
        for h in range(heads):
            for b in range(blocks):
                low = (h * blocks + b) * piece
                value = total[low : low + piece]
                if n < 1024 * chunks:
                    row = n // 1024 * heads * piece + h * piece
                    out_ref[b, row : row + piece, n % 1024 : n % 1024 + size] = value
                else:
                    row = chunks * heads * piece + h // aside * piece
                    col = h % aside * rest
                    out_ref[b, row : row + piece, col : col + rest] = value
    cot = joined(c_refs, c_all)
    for n, size in column_tiles(down_ref.shape[0], 256):
        total, at = None, 0
        for ref in a_refs:
            here = slice(at, at + ref.shape[0])
            term = dot(ref[:, n : n + size], cot[here, :], TN)
            total = term if total is None else total + term
            at += ref.shape[0]
        down_ref[n : n + size, :] = total.astype(BF)
    if packed:
        for b in range(blocks):
            out_ref[b, start : start + share, :] = down_ref[b * share : (b + 1) * share, :]


def mixing_grad_body(count, at_ref, m_ref, *refs):
    total = None
    for k, low, size in tiles_of(refs[:count]):
        start = pl.ds(pl.multiple_of(at_ref[k] + low, 128), size)
        term = dot(m_ref[start, :], refs[k][low : low + size, :], TN)
        total = term if total is None else total + term
    refs[count][...] = total.astype(BF)


def permute(x, axis, move):
    count = lax.axis_size(axis)
    return lax.ppermute(x, axis, [(i, move(i) % count) for i in range(count)])


def together(*arrays):
    return lax.optimization_barrier(arrays)


def gather_near(x):
    if lax.axis_size("head") != 4:
        return []
    return [permute(x, "head", lambda i: i ^ 1), permute(x, "head", lambda i: i ^ 2)]


def gather_far(x, near):
    if lax.axis_size("head") != 4:
        return [lax.all_gather(x, "head", axis=0, tiled=True)]
    half = x.shape[0] // 2
    return [
        permute(near[0][:half], "head", lambda i: i ^ 2),
        permute(near[1][half:], "head", lambda i: i ^ 1),
    ]


def gathered(x, near, far):
    return [x, *near, *far] if near else list(far)


def part_places(rows):
    if lax.axis_size("head") != 4:
        return [(None, 0)]
    return [(0, 0), (1, 0), (2, 0), (3, 0), (3, rows // 2)]


def part_outs(rows, depth):
    if lax.axis_size("head") != 4:
        return [shape(rows * lax.axis_size("head"), depth)]
    half = rows // 2
    return [shape(rows, depth), shape(rows, depth), shape(rows, depth), shape(half, depth), shape(half, depth)]


def scatter_rows(refs, at, value, cols=None):
    cols = slice(None) if cols is None else cols
    if len(refs) == 1:
        refs[0][at : at + value.shape[0], cols] = value
        return
    own, by_one, by_two, stay_up, stay_low = refs
    half = stay_up.shape[0]
    spots = [
        (own, 0), (own, half), (by_one, 0), (stay_low, 0), (stay_up, 0), (by_two, 0), (by_one, half), (by_two, half)
    ]
    for i in range(value.shape[0] // half):
        ref, low = spots[at // half + i]
        ref[low : low + half, cols] = value[i * half : (i + 1) * half]


def sum_near(pieces):
    if len(pieces) == 1:
        return []
    return [
        permute(pieces[1], "head", lambda i: i ^ 1),
        permute(pieces[2], "head", lambda i: i ^ 2),
    ]


def sum_far(pieces, near):
    if len(pieces) == 1:
        return [lax.psum_scatter(pieces[0], "head", scatter_dimension=0, tiled=True)]
    stay_up, stay_low = pieces[3:]
    half = stay_up.shape[0]
    upper = (near[0][half:].astype(F32) + stay_up.astype(F32)).astype(BF)
    lower = (near[1][half:].astype(F32) + stay_low.astype(F32)).astype(BF)
    return [permute(upper, "head", lambda i: i ^ 2), permute(lower, "head", lambda i: i ^ 1)]


def sum_terms(pieces, near, far):
    if len(pieces) == 1:
        return [0], list(far)
    half = pieces[3].shape[0]
    return [0, 0, half, 0, half], [pieces[0], *near, *far]


def mirror(x):
    count = lax.axis_size("blk")
    return permute(x, "blk", lambda i: count - i if i % 2 else i)


def exchange_head(x):
    count = lax.axis_size("head")
    place = lax.axis_index("head")
    return jnp.stack(
        [
            permute(
                lax.dynamic_index_in_dim(x, place ^ k, 0, keepdims=False),
                "head",
                lambda i, k=k: i ^ k,
            )
            if k
            else lax.dynamic_index_in_dim(x, place, 0, keepdims=False)
            for k in range(count)
        ]
    )


def other_core(x):
    return permute(x, "blk", lambda i: i ^ 1)


def per_device(
    inputs,
    query_weight,
    key_weight,
    value_weight,
    mixing_weight,
    gate_weight,
    up_weight,
    down_weight,
    attention_gain,
    feedforward_gain,
    query_gain,
    key_gain,
    cotangent,
):
    heads = lax.axis_size("head")
    blocks = lax.axis_size("blk")
    chips = blocks // 2
    place = lax.axis_index("head")
    block = lax.axis_index("blk")
    core = block % 2
    chip = block // 2
    rows, depth = inputs.shape
    span = rows * heads
    piece = query_weight.shape[0]
    width = gate_weight.shape[1] // heads
    wide = -(-width // 128) * 128
    shared = KV // heads
    unit_heads = HQ // heads // 2
    unit_cols = unit_heads * HD

    qkv_own = jnp.concatenate(
        [
            jnp.pad(
                query_weight.reshape(piece, heads, 2, unit_cols),
                ((0, 0), (0, 0), (0, 0), (0, 128 - unit_cols)),
            ),
            jnp.repeat(key_weight.reshape(piece, heads, shared, HD), 2 // shared, axis=2),
            jnp.repeat(value_weight.reshape(piece, heads, shared, HD), 2 // shared, axis=2),
        ],
        axis=-1,
    ).reshape(piece, heads, 512)
    gains = jnp.pad(jnp.stack([attention_gain, feedforward_gain], axis=1), ((0, 0), (0, 126)))
    qkv_send = jnp.concatenate(
        [qkv_own, jnp.broadcast_to(gains[:, None, :], (piece, heads, 128))], axis=-1
    ).transpose(1, 0, 2)
    gate_up_send = (
        jnp.stack(
            [
                jnp.pad(
                    w.reshape(piece, heads, width), ((0, 0), (0, 0), (0, wide - width))
                ).reshape(piece, heads, wide // 128, 128)
                for w in (gate_weight, up_weight)
            ],
            axis=3,
        )
        .reshape(piece, heads, 2 * wide)
        .transpose(1, 0, 2)
    )

    own, qkv_piece = together(mirror(inputs), exchange_head(qkv_send))
    qkv_mine = [
        permute(qkv_piece, "blk", lambda i, step=step: i + 2 * step) for step in range(1, chips)
    ]
    qkv_mine, near, own, cotangent = together(qkv_mine, gather_near(own), own, cotangent)
    own_cot = mirror(cotangent)
    qkv_mine = jnp.stack([qkv_piece, *qkv_mine])
    low_rows, qkv_mine = together(
        jnp.concatenate([mixing_weight, down_weight], axis=0), qkv_mine
    )
    low_rows = lax.all_gather(low_rows, "blk", axis=0)
    qkv_theirs, far = together(other_core(qkv_mine), gather_far(own, near))
    xs = gathered(own, near, far)
    sources = [(chip - r) % chips for r in range(chips)]
    qkv_ext = run(
        functools.partial(assemble_body, heads),
        shape(heads, blocks, piece, 640),
        [qkv_mine, qkv_theirs],
        scalars=[2 * z + core for z in sources]
        + [2 * z + 1 - core for z in sources]
        + [place ^ k for k in range(heads)],
    ).reshape(depth, 640)
    span_index = jnp.where(core == 0, block, blocks - block)
    positions = (span_index * span + jnp.arange(span, dtype=jnp.int32)).astype(F32)
    lane = jnp.arange(128, dtype=jnp.int32)
    frequency = jnp.exp(
        (lane % (HD // 2)).astype(F32) * (-2.0 * math.log(ROPE_BASE) / HD)
    )
    angles = positions[:, None] * frequency[None, :]
    cosine = jnp.cos(angles)
    sine = jnp.sin(angles) * jnp.where(lane % HD < HD // 2, -1.0, 1.0)
    head_gain = jnp.concatenate(
        [
            jnp.tile(query_gain.astype(F32), 2)[None, :],
            jnp.tile(key_gain.astype(F32), 2)[None, :],
            jnp.zeros((6, 128), F32),
        ],
        axis=0,
    )

    places = part_places(rows)
    starts = [0 if other is None else (place ^ other) * rows + shift for other, shift in places]
    packet = 128 * (unit_heads + 1)
    keep, send, gain_rows = run(
        functools.partial(project_body, len(xs), unit_heads),
        [shape(span, packet), shape(span, packet), shape(8, depth, dtype=F32)],
        xs + [qkv_ext, cosine, sine, head_gain],
        flops=4 * span * depth * 512,
        scalars=starts + [core],
        far=tuple(range(len(xs) + 4)),
    )
    gate_up_send, keep = together(gate_up_send, keep)
    send, gate_up_piece = together(other_core(send), exchange_head(gate_up_send))
    packets = jnp.concatenate([keep, send], axis=0)
    kv = packets[:, -128:]

    def slot_of(early, z):
        return jnp.where(4 * z < blocks, early, 1 - early) ^ core ^ 1

    def reach(z):
        return jnp.abs(4 * z - (blocks - 1))

    my_low, my_high = slot_of(1, chip), slot_of(0, chip)

    def offsets(step):
        if step == 0:
            return [span * my_high, span * my_low]
        source = (chip - step) % chips
        low, high = slot_of(1, source), slot_of(0, source)
        outer = reach(source) > reach(chip)
        return [
            span * jnp.where(outer, my_low, my_high),
            span * low,
            span * my_high,
            span * jnp.where(outer, low, high),
        ]

    def next_chip(x):
        return permute(x, "blk", lambda i: i + 2)

    kvs = [kv]
    acc = None
    cot_near = cot_far = mixing_near = mixing_far = []
    mixing_rows, down_full = None, None
    for step in range(chips):
        last = step == chips - 1
        res = attend(offsets(step), packets, kvs[step], acc, step == 0, last, unit_heads)
        ahead = [] if last else [next_chip(kvs[step])]
        if step == min(1, chips - 1):
            cot_near = gather_near(own_cot)
        if step == min(2, chips - 1):
            mixing_rows = low_rows[:, :piece].reshape(blocks * piece, depth)
            down_full = jnp.pad(
                low_rows[:, piece:].reshape(-1, depth), ((0, wide - width), (0, 0))
            )
            mixing_near = gather_near(mixing_rows)
            cot_far = gather_far(own_cot, cot_near)
        if last:
            mixing_far = gather_far(mixing_rows, mixing_near)
        res, ahead, own_cot, cot_near, cot_far, mixing_near, mixing_far = together(
            res, ahead, own_cot, cot_near, cot_far, mixing_near, mixing_far
        )
        acc = res[0]
        kvs += ahead
        if step == min(1, chips - 1):
            acc, gate_up_piece = together(acc, gate_up_piece)
            gate_up = lax.all_gather(gate_up_piece, "blk", axis=0)
    cots = gathered(own_cot, cot_near, cot_far)
    mixing_parts = gathered(mixing_rows, mixing_near, mixing_far)
    mixture_pair = res[1][:, :, :unit_cols]
    theirs = other_core(mixture_pair[1])
    mixture_span = jnp.where(
        core == 0,
        jnp.concatenate([mixture_pair[0], theirs], axis=1),
        jnp.concatenate([theirs, mixture_pair[0]], axis=1),
    )
    mixture = lax.all_to_all(
        mixture_span.reshape(heads, rows, 2 * unit_cols), "head", 0, 0, tiled=True
    )
    mix_places = part_places(mixing_rows.shape[0])
    hidden, normed_ffn = run(
        functools.partial(mix_body, mix_places),
        [shape(rows, depth, dtype=F32), shape(rows, depth)],
        [mixture] + mixing_parts + [own, gain_rows],
        flops=2 * rows * depth * depth,
        scalars=[place],
        far=tuple(range(1, len(mixing_parts) + 3)),
    )
    split = heads == 4
    grads = run(
        functools.partial(activation_grad_body, len(cots)),
        [shape(rows, wide), shape(span - rows, wide)] if split else [shape(span, wide)],
        [normed_ffn] + cots + [down_full],
        flops=2 * span * depth * wide,
        scratch=[pltpu.VMEM((span, depth), BF)],
        far=tuple(range(1, len(cots) + 2)),
        stay=(0,),
    )
    near, grads, normed_ffn = together(gather_near(normed_ffn), grads, normed_ffn)
    far = gather_far(normed_ffn, near)
    results = []
    if split:
        results.append(feed_forward([normed_ffn], grads[0], gate_up, True))
    far, results = together(far, results)
    ffn_parts = gathered(normed_ffn, near, far)
    if split:
        results = [*results, feed_forward(ffn_parts[1:], grads[1], gate_up, False)]
    else:
        results = [feed_forward(ffn_parts, grads[0], gate_up, None)]
    acts = [r[0] for r in results]
    gate_up_grads = [r[1] for r in results]
    backs = [b for r in results for b in r[2]]
    counts = (len(ffn_parts), len(cots), len(gate_up_grads), len(acts))
    dims = (blocks, heads, piece, 2 * wide, width)
    chunks, rest_cols, aside, start_row, share = packed_rows(*dims)
    packed = share % 16 == 0 and start_row % 16 == 0
    ffn_rows = start_row + (share if packed else 0)
    res = run(
        functools.partial(weight_grad_body, counts, dims, packed),
        [shape(blocks, ffn_rows, 1024)] + ([] if packed else [shape(wide, depth)]),
        ffn_parts + cots + gate_up_grads + acts,
        flops=6 * span * depth * wide,
        scratch=[pltpu.VMEM((span, depth), BF)] * 2
        + ([pltpu.VMEM((wide, depth), BF)] if packed else []),
        limit=56,
        far=tuple(range(len(ffn_parts) + len(cots))),
    )
    near, res, backs = together(sum_near(backs), list(res) if not packed else list(res)[:1], backs)
    ffn_part = lax.psum_scatter(res[0], "blk", scatter_dimension=0, tiled=True)[0]
    far = sum_far(backs, near)
    down_full, near = together(down_full, near)
    terms = run(
        functools.partial(down_body, len(acts), len(part_outs(rows, depth))),
        part_outs(rows, depth),
        acts + [down_full],
        flops=2 * span * depth * wide,
        scratch=[pltpu.VMEM((span, wide), BF)],
    )
    far, terms = together(far, terms)
    shifts, addends = sum_terms(backs, near, far)
    hidden_grad, hidden_low, mixture_grad = run(
        functools.partial(hidden_back_body, mix_places, shifts),
        [shape(rows, depth, dtype=F32), shape(rows, depth), shape(heads, rows, 2 * unit_cols)],
        [hidden, own_cot, gain_rows] + mixing_parts + addends,
        flops=2 * rows * depth * depth,
        scalars=[place],
        far=tuple(range(len(mixing_parts) + 3)),
    )
    grad_span = lax.all_to_all(mixture_grad, "head", 0, 0, tiled=True).reshape(span, 2 * unit_cols)
    theirs = other_core(
        jnp.where(core == 0, grad_span[:, unit_cols:], grad_span[:, :unit_cols])
    )
    if unit_cols < 128:
        pad = ((0, 0), (0, 128 - unit_cols))
        theirs = jnp.pad(theirs, pad)
        grad_wide = jnp.concatenate(
            [jnp.pad(grad_span[:, :unit_cols], pad), jnp.pad(grad_span[:, unit_cols:], pad)], axis=1
        )
    else:
        grad_wide = grad_span
    out_grad = run(
        out_grad_body,
        shape(unit_heads, 2 * span, 128),
        [grad_wide, theirs, acc],
        scalars=[core],
    )

    def columns_of(ffn_part):
        part = ffn_part[:start_row]
        pieces = [
            part[i * heads * piece : (i + 1) * heads * piece].reshape(heads, piece, 1024)
            for i in range(chunks)
        ]
        if rest_cols:
            part = part[chunks * heads * piece :].reshape(-1, piece, aside, rest_cols)
            pieces.append(part.transpose(0, 2, 1, 3).reshape(heads, piece, rest_cols))
        return jnp.concatenate(pieces, axis=-1)

    query_acc = None
    sent, arrived = [], []
    hidden_near = hidden_far = term_near = term_far = []
    steps = sorted(range(1, chips), key=lambda step: min(step, chips - step)) + [0]
    for at, step in enumerate(steps):
        last = at == len(steps) - 1
        query_acc, kv_grad = attend_back(
            offsets(step), packets, out_grad, kvs[step], query_acc, step == 0
        )
        moved = [
            permute(g, "blk", lambda i, back=back: i - 2 * back) for back, g in sent
        ]
        if at == 0:
            hidden_near = gather_near(hidden_low)
        if at == min(1, chips - 1):
            hidden_far = gather_far(hidden_low, hidden_near)
        if at == min(1, chips - 1):
            term_near = sum_near(terms)
        if at == min(2, chips - 1):
            term_far = sum_far(terms, term_near)
            hidden_parts = gathered(hidden_low, hidden_near, hidden_far)
            mixing_grad = run(
                functools.partial(mixing_grad_body, len(hidden_parts)),
                shape(2 * unit_cols, depth),
                [mixture_span] + hidden_parts,
                flops=4 * span * depth * unit_cols,
                scalars=starts,
                far=tuple(range(len(hidden_parts) + 1)),
            )
        if last:
            gate_up_part = exchange_head(gate_up_part)
        query_acc, kv_grad, hidden_near, hidden_far, terms, term_near, term_far = together(
            query_acc, kv_grad, hidden_near, hidden_far, terms, term_near, term_far
        )
        if at == max(len(steps) - 2, 0):
            query_acc, ffn_part, mixing_grad = together(query_acc, ffn_part, mixing_grad)
            gate_up_part = columns_of(ffn_part)
        arrived += moved
        sent = [(step, kv_grad)] if step else []
    if packed:
        down_sum = ffn_part[start_row:]
    else:
        down_sum = lax.psum_scatter(res[1][:width], "blk", scatter_dimension=0, tiled=True)
    mine, theirs = run(
        pack_body,
        [shape(span, 256), shape(span, 256)],
        [query_acc, kv_grad] + arrived,
    )
    theirs, mine, hidden = together(other_core(theirs), mine, hidden)
    back = run(
        functools.partial(
            project_back_body, len(xs), len(part_outs(rows, depth)), (blocks, heads, piece)
        ),
        part_outs(rows, depth)
        + [shape(blocks, heads * (piece + 8) + depth // 512 * piece, 512)],
        xs + [qkv_ext, gain_rows, mixing_grad, cosine, sine, mine, theirs, head_gain],
        flops=12 * span * depth * 512,
        scalars=starts + [core],
        scratch=[pltpu.VMEM((2, depth, 256), F32)],
        far=tuple(range(len(xs) + 6)),
    )
    *back, projections = back
    projections = lax.psum_scatter(projections, "blk", scatter_dimension=0, tiled=True)[0]
    output_shifts, output_terms = sum_terms(terms, term_near, term_far)
    gate_up_part, back, hidden = together(gate_up_part, back, hidden)
    near = sum_near(back)
    output = run(
        functools.partial(output_body, output_shifts),
        shape(rows, depth),
        [hidden] + output_terms,
        far=(0, 1),
    )
    gate_sum, up_sum, feed_gain_sum = run(
        functools.partial(finish_feed_body, heads),
        [shape(piece, heads * wide, dtype=F32)] * 2 + [shape(piece, 128, dtype=F32)],
        [gate_up_part, gate_up_send],
        scalars=[place ^ k for k in range(heads)],
    )
    near, output, gate_sum, up_sum, feed_gain_sum, down_sum = together(
        near, output, gate_sum, up_sum, feed_gain_sum, down_sum.astype(F32)
    )
    output = mirror(output)
    far = sum_far(back, near)
    input_shifts, addends = sum_terms(back, near, far)
    input_gradient = run(
        functools.partial(input_back_body, input_shifts),
        shape(rows, depth),
        [own, hidden_grad, gain_rows] + addends,
    )
    input_gradient = mirror(input_gradient)
    cut = heads * (piece + 8)
    mixing_sum = (
        projections[cut:].reshape(depth // 512, piece, 512).transpose(1, 0, 2).reshape(piece, depth)
    ).astype(F32)
    qkv_part = exchange_head(projections[:cut].reshape(heads, piece + 8, 512))
    outs = [shape(piece, heads * 2 * unit_cols, dtype=F32)]
    outs += [shape(piece, heads * 128, dtype=F32)] * shared
    *grads, attention_gain_sum, head_gain_sum = run(
        functools.partial(finish_projections_body, heads, unit_heads),
        outs + [shape(piece, 128, dtype=F32), shape(8, 256, dtype=F32)],
        [qkv_part, qkv_own.transpose(1, 0, 2)],
        scalars=[place ^ k for k in range(heads)],
    )
    if shared == 1:
        both = grads[1].reshape(piece, heads, 2, HD)
        grads = [grads[0], both[:, :, 0].reshape(piece, -1), both[:, :, 1].reshape(piece, -1)]

    def only(x):
        return x.reshape(piece, heads, wide)[..., :width].reshape(piece, -1)

    return (
        output,
        input_gradient,
        *grads,
        mixing_sum,
        only(gate_sum),
        only(up_sum),
        down_sum,
        attention_gain_sum[:, 0] / attention_gain.astype(F32),
        feed_gain_sum[:, 0] / feedforward_gain.astype(F32),
        head_gain_sum[0, :HD] + head_gain_sum[0, HD : 2 * HD],
        head_gain_sum[0, 128 : 128 + HD],
    )


def solution(mesh):
    in_specs = (
        P(("blk", "head"), None),
        P(("head", "blk"), None),
        P(("head", "blk"), None),
        P(("head", "blk"), None),
        P(("head", "blk"), None),
        P(("head", "blk"), None),
        P(("head", "blk"), None),
        P(("head", "blk"), None),
        P(("head", "blk")),
        P(("head", "blk")),
        P(),
        P(),
        P(("blk", "head"), None),
    )
    out_specs = (
        P(("blk", "head"), None),
        P(("blk", "head"), None),
        P(("head", "blk"), None),
        P(("head", "blk"), None),
        P(("head", "blk"), None),
        P(("head", "blk"), None),
        P(("head", "blk"), None),
        P(("head", "blk"), None),
        P(("head", "blk"), None),
        P(("head", "blk")),
        P(("head", "blk")),
        P(),
        P(),
    )
    return jax.shard_map(
        per_device, mesh=mesh, in_specs=in_specs, out_specs=out_specs, check_vma=False
    )
```

```python
import functools
import math

import jax
import jax.numpy as jnp
from jax import lax
from jax.experimental import pallas as pl
from jax.experimental.pallas import tpu as pltpu
from jax.sharding import PartitionSpec as P

HQ = 16
KV = 8
HD = 64
EPSILON = 1e-05
ROPE_BASE = 1000000.0
TILE = 1024
QUERY_UNIT = math.log2(math.e) * HD**-0.5

BF = jnp.bfloat16
F32 = jnp.float32
NT = (((1,), (1,)), ((), ()))
NN = (((1,), (0,)), ((), ()))
TN = (((0,), (0,)), ((), ()))
VM = pl.BlockSpec(memory_space=pltpu.VMEM)
SM = pl.BlockSpec(memory_space=pltpu.SMEM)


def dot(a, b, dims=NN):
    return lax.dot_general(a, b, dims, preferred_element_type=F32)


def run(body, outs, args, flops=0, scalars=None, scratch=(), exps=0, limit=20, stay=()):
    args = list(args)
    hbm = pl.BlockSpec(memory_space=pltpu.HBM)
    specs = [hbm if i in stay else VM for i in range(len(args))]
    many = isinstance(outs, (list, tuple))
    outs = list(outs) if many else [outs]
    size = sum(math.prod(a.shape) * a.dtype.itemsize for a in outs + args)
    if scalars is not None:
        args = [jnp.stack([jnp.asarray(v, jnp.int32) for v in scalars])] + args
        specs = [SM] + specs
    return pl.pallas_call(
        body,
        out_shape=tuple(outs) if many else outs[0],
        in_specs=specs,
        out_specs=tuple([VM] * len(outs)) if many else VM,
        scratch_shapes=scratch,
        cost_estimate=pl.CostEstimate(flops=flops, bytes_accessed=size, transcendentals=exps),
        compiler_params=pltpu.CompilerParams(vmem_limit_bytes=limit << 20),
    )(*args)


def shape(*dims, dtype=BF):
    return jax.ShapeDtypeStruct(dims, dtype)


def pair_list(off_ref, span, which, count):
    return [
        (
            pl.multiple_of(off_ref[4 * which + 2 * i], span),
            pl.multiple_of(off_ref[4 * which + 2 * i + 1], span),
        )
        for i in range(count)
    ]


def attend_body(span, heads, count, local, first, last, off_ref, q_ref, *refs):
    refs = list(refs)
    kv_refs = [refs.pop(0) for _ in range(count)]
    acc_ref = None if first else refs.pop(0)
    out_ref = refs.pop(0)
    mix_ref = refs.pop(0) if last else None
    ones_ref = refs.pop(0)
    lane = lax.broadcasted_iota(jnp.int32, ones_ref.shape, 1)
    out_ref[...] = jnp.zeros_like(out_ref) if first else acc_ref[...]
    for which, kv_ref in enumerate(kv_refs):
        ones_ref[...] = jnp.where(lane < HD, jnp.ones((), BF), kv_ref[...])
        attend_block(span, heads, local, which, off_ref, q_ref, kv_ref, out_ref, ones_ref)
    if last:
        size = 256
        for i in range(2 * span // size):
            rows = slice(i * size, (i + 1) * size)
            left = lax.broadcasted_iota(jnp.int32, (size, 2 * HD), 1) < HD
            mixed = []
            for head in range(heads):
                total = out_ref[head, rows, :]
                mixed.append(total * pltpu.roll(1.0 / jnp.where(left, total, 1.0), HD, 1))
            out = jnp.where(left, pltpu.roll(mixed[0], HD, 1), mixed[1] if heads > 1 else 0.0)
            mix_ref[i * size // span, pl.ds(i * size % span, size), :] = out.astype(BF)


def attend_block(span, heads, local, which, off_ref, q_ref, kv_ref, out_ref, ones_ref):
    block = min(span, TILE)

    def block_pair(head, q_off, k_off):
        rows = pl.ds(q_off, block)
        keys = pl.ds(k_off, block)
        query = q_ref[rows, 128 * head : 128 * head + 128]
        weight = jnp.exp2(dot(query, kv_ref[keys, :], NT)).astype(BF)
        out_ref[head, rows, :] += dot(weight, ones_ref[keys, :])

    def full(q_off, k_off):
        for i in range(span // block):
            for j in range(span // block):
                for head in range(heads):
                    block_pair(head, q_off + i * block, k_off + j * block)

    def diagonal(start):
        for i in range(span // block):
            for j in range(i):
                for head in range(heads):
                    block_pair(head, start + i * block, start + j * block)
            diagonal_block(start + i * block)

    def diagonal_block(start):
        size = 256
        for head in range(heads):
            for i in range(block // size):
                rows = slice(start + i * size, start + (i + 1) * size)
                query = q_ref[rows, 128 * head : 128 * head + 128]
                total = None
                pieces = ([(0, i * size)] if i else []) + [(i * size, (i + 1) * size)]
                for low, high in pieces:
                    keys = slice(start + low, start + high)
                    weight = jnp.exp2(dot(query, kv_ref[keys, :], NT))
                    if low == i * size:
                        place = lax.broadcasted_iota(jnp.int32, (size, size), 0)
                        other = lax.broadcasted_iota(jnp.int32, (size, size), 1)
                        weight = jnp.where(other <= place, weight, 0.0)
                    part = dot(weight.astype(BF), ones_ref[keys, :])
                    total = part if total is None else total + part
                out_ref[head, rows, :] += total

    if local:
        diagonal(0)
        diagonal(span)
    for q_off, k_off in pair_list(off_ref, span, which, 1 if local else 2):
        full(q_off, k_off)


def attend(offsets, packets, kvs, acc, local, last, heads):
    span = packets.shape[0] // 2
    outs = [shape(heads, 2 * span, 2 * HD, dtype=F32)]
    if last:
        outs.append(shape(2, span, 2 * HD))
    return run(
        functools.partial(attend_body, span, heads, len(kvs), local, acc is None, last),
        outs,
        [packets, *kvs] + ([] if acc is None else [acc]),
        flops=8 * heads * span * span * 256 * len(kvs),
        scalars=offsets,
        scratch=[pltpu.VMEM((2 * span, 2 * HD), BF)],
        exps=2 * heads * span * span * len(kvs),
    )


def attend_back_body(span, heads, count, local, first, off_ref, q_ref, do_ref, *refs):
    refs = list(refs)
    kv_refs = [refs.pop(0) for _ in range(count)]
    acc_ref = None if first else refs.pop(0)
    dq_ref = refs.pop(0)
    out_refs = [refs.pop(0) for _ in range(count)]
    ones_ref, dv_ref = refs[:2]
    zero = jnp.zeros((), BF)
    lane = lax.broadcasted_iota(jnp.int32, ones_ref.shape, 1)
    for head in range(heads):
        dv_ref[head] = jnp.where(lane < HD, zero, do_ref[head])
    dq_ref[...] = jnp.zeros_like(dq_ref) if first else acc_ref[...]
    for which, (kv_ref, out_ref) in enumerate(zip(kv_refs, out_refs, strict=True)):
        ones_ref[...] = jnp.where(
            lane < HD, jnp.where(lane < 3, jnp.ones((), BF), zero), kv_ref[...]
        )
        dkv_ref = out_ref if local else refs[2]
        attend_back_block(
            span, heads, local, which, off_ref, q_ref, do_ref, kv_ref, dq_ref, dkv_ref, ones_ref, dv_ref
        )
        if not local:
            out_ref[...] = dkv_ref[...].astype(BF)


def attend_back_block(
    span, heads, local, which, off_ref, q_ref, do_ref, kv_ref, dq_ref, dkv_ref, ones_ref, dv_ref
):
    block = min(span, TILE)
    dkv_ref[...] = jnp.zeros_like(dkv_ref)

    def tile(head, rows, keys, mask):
        query = q_ref[rows, 128 * head : 128 * head + 128]
        pair = kv_ref[keys, :]
        weight = jnp.exp2(dot(pair, query, NT))
        if mask is not None:
            weight = jnp.where(mask, weight, 0.0)
        score_grad = (weight * dot(ones_ref[keys, :], do_ref[head, rows, :], NT)).astype(BF)
        dkv_ref[keys, :] += dot(weight.astype(BF), dv_ref[head, rows, :]) + dot(score_grad, query)
        dq_ref[head, rows, :] += dot(score_grad, pair, TN)

    def block_pair(head, q_off, k_off):
        tile(head, pl.ds(q_off, block), pl.ds(k_off, block), None)

    def full(q_off, k_off):
        for i in range(span // block):
            for j in range(span // block):
                for head in range(heads):
                    block_pair(head, q_off + i * block, k_off + j * block)

    def diagonal(start):
        for i in range(span // block):
            for j in range(i):
                for head in range(heads):
                    block_pair(head, start + i * block, start + j * block)
            diagonal_block(start + i * block)

    def diagonal_block(start):
        size = 256
        for head in range(heads):
            for i in range(block // size):
                rows = slice(start + i * size, start + (i + 1) * size)
                pieces = ([(0, i * size)] if i else []) + [(i * size, (i + 1) * size)]
                for low, high in pieces:
                    mask = None
                    if low == i * size:
                        key_place = lax.broadcasted_iota(jnp.int32, (size, size), 0)
                        mask = key_place <= lax.broadcasted_iota(jnp.int32, (size, size), 1)
                    tile(head, rows, slice(start + low, start + high), mask)

    if local:
        diagonal(0)
        diagonal(span)
    for q_off, k_off in pair_list(off_ref, span, which, 1 if local else 2):
        full(q_off, k_off)


def attend_back(offsets, packets, out_grad, kvs, acc, local):
    heads, rows = out_grad.shape[:2]
    span = rows // 2
    count = len(kvs)
    return run(
        functools.partial(attend_back_body, span, heads, count, local, acc is None),
        [shape(heads, rows, 2 * HD, dtype=F32)]
        + [shape(rows, 2 * HD, dtype=F32 if local else BF)] * count,
        [packets, out_grad, *kvs] + ([] if acc is None else [acc]),
        flops=20 * heads * span * span * 256 * count,
        scalars=offsets,
        scratch=[pltpu.VMEM((rows, 2 * HD), BF), pltpu.VMEM((heads, rows, 2 * HD), BF)]
        + ([] if local else [pltpu.VMEM((rows, 2 * HD), F32)]),
        exps=2 * heads * span * span * count,
        limit=36,
    )


def out_grad_body(core_ref, mine_ref, theirs_ref, acc_ref, out_ref):
    heads, rows = acc_ref.shape[:2]
    size = 256
    lane = lax.broadcasted_iota(jnp.int32, (size, 2 * HD), 1)
    left = lane < HD
    for i in range(rows // size):
        here = slice(i * size, (i + 1) * size)
        if i * size < rows // 2:
            first = mine_ref[here, 0:128]
            second = mine_ref[here, 128:256]
            both = jnp.where(core_ref[0] == 0, first, second).astype(F32)
        else:
            both = theirs_ref[slice(i * size - rows // 2, (i + 1) * size - rows // 2), :].astype(F32)
        for head in range(heads):
            grad = pltpu.roll(both, HD, 1) if head == 0 else both
            total = acc_ref[head, here, :]
            inverse = pltpu.roll(1.0 / jnp.where(left, total, 1.0), HD, 1)
            scaled = grad * inverse
            delta = jnp.sum(
                jnp.where(left, 0.0, scaled * total * inverse), axis=1, keepdims=True
            )
            shift = jnp.broadcast_to(-delta, (size, 2 * HD))
            high = shift.astype(BF).astype(F32)
            rest = shift - high
            middle = rest.astype(BF).astype(F32)
            parts = jnp.where(lane == 0, high, jnp.where(lane == 1, middle, rest - middle))
            out = jnp.where(left, jnp.where(lane < 3, parts, 0.0), scaled)
            out_ref[head, here, :] = out.astype(BF)


def pack_body(dq_ref, dkv_ref, *refs):
    outs = refs[-2:]
    heads, rows = dq_ref.shape[:2]
    span = rows // 2
    size = 256
    lane = lax.broadcasted_iota(jnp.int32, (size, 2 * HD), 1)
    for i in range(rows // size):
        here = slice(i * size, (i + 1) * size)
        there = slice(i * size % span, i * size % span + size)
        out = outs[i * size // span]
        query = dq_ref[0, here, :]
        other = pltpu.roll(dq_ref[1, here, :], HD, 1) if heads > 1 else 0.0
        query = jnp.where(lane < HD, query, other) * (HD**-0.5)
        pair = dkv_ref[here, :]
        for more in refs[:-2]:
            pair = pair + more[here, :].astype(F32)
        pair = pair * jnp.where(lane < HD, math.log(2.0), 1.0)
        out[there, 0:128] = query.astype(BF)
        out[there, 128:256] = pair.astype(BF)


def swap_halves(x):
    lane = lax.broadcasted_iota(jnp.int32, x.shape, 1)
    return jnp.where(
        lane % HD < HD // 2, pltpu.roll(x, x.shape[1] - HD // 2, 1), pltpu.roll(x, HD // 2, 1)
    )


def head_mean(x):
    size = x.shape[1]
    first = lax.broadcasted_iota(jnp.int32, (size, size), 0) // HD
    second = lax.broadcasted_iota(jnp.int32, (size, size), 1) // HD
    ones = jnp.where(first == second, 1.0 / HD, 0.0).astype(BF)
    high = x.astype(BF)
    low = (x - high.astype(F32)).astype(BF)
    return dot(high, ones) + dot(low, ones)


def unit_norm(x):
    return x * lax.rsqrt(jnp.mean(x * x, axis=1, keepdims=True) + EPSILON)


def tiles_of(refs, size=256):
    for k, ref in enumerate(refs):
        step = min(size, ref.shape[0])
        for low in range(0, ref.shape[0], step):
            yield k, low, step


def assemble_body(heads, index_ref, *refs):
    out_ref = refs[-1]
    for r, ref in enumerate(refs[:-1]):
        for h in range(heads):
            out_ref[index_ref[len(refs) - 1 + h], index_ref[r]] = ref[h]


def project_body(count, heads, at_ref, *refs):
    x_refs = refs[:count]
    w_ref, cos_ref, sin_ref, head_gain_ref, keep_ref, send_ref, rows_ref = refs[count:]
    core = at_ref[count]
    rows_ref[...] = w_ref[:, 512:640].astype(F32).T[0:8]
    gain = rows_ref[0:1, :]
    for k, low, size in tiles_of(x_refs):
        start = pl.ds(pl.multiple_of(at_ref[k] + low, 128), size)
        normed = (unit_norm(x_refs[k][low : low + size, :].astype(F32)) * gain).astype(BF)
        cosine, sine = cos_ref[start, :], sin_ref[start, :]
        lane = lax.broadcasted_iota(jnp.int32, cosine.shape, 1)
        for unit, out_ref in ((core, keep_ref), (1 - core, send_ref)):
            raw = dot(normed, w_ref[:, pl.ds(pl.multiple_of(256 * unit, 256), 256)])
            query, pair = raw[:, :128], raw[:, 128:]
            query = query * lax.rsqrt(head_mean(query * query) + EPSILON) * head_gain_ref[0:1, :]
            query = (query * cosine + swap_halves(query) * sine) * QUERY_UNIT
            out_ref[start, 0:128] = jnp.where(lane < HD, query, 0.0).astype(BF)
            if heads > 1:
                shifted = pltpu.roll(query, HD, 1)
                out_ref[start, 128:256] = jnp.where(lane < HD, shifted, 0.0).astype(BF)
            key = pair * lax.rsqrt(head_mean(pair * pair) + EPSILON) * head_gain_ref[1:2, :]
            key = key * cosine + swap_halves(key) * sine
            out_ref[start, 128 * heads : 128 * heads + 128] = jnp.where(lane < HD, key, pair).astype(BF)


def project_back_body(count, outs, dims, at_ref, *refs):
    x_refs = refs[:count]
    w_ref, rows_ref, mixing_ref, cos_ref, sin_ref, mine_ref, theirs_ref, head_gain_ref = refs[
        count : count + 8
    ]
    part_refs = refs[count + 8 : count + 8 + outs]
    dw_ref, acc_ref = refs[count + 8 + outs :]
    core = at_ref[count]
    gain = rows_ref[0:1, :]
    gain_sums = [jnp.zeros((1, 128), F32), jnp.zeros((1, 128), F32)]
    done = 0
    for k, low, size in tiles_of(x_refs):
        start = pl.ds(pl.multiple_of(at_ref[k] + low, 128), size)
        normed = (unit_norm(x_refs[k][low : low + size, :].astype(F32)) * gain).astype(BF)
        cosine, sine = cos_ref[start, :], sin_ref[start, :]
        lane = lax.broadcasted_iota(jnp.int32, cosine.shape, 1)
        part = None
        for u, (unit, grad_ref) in enumerate(((core, mine_ref), (1 - core, theirs_ref))):
            cols = pl.ds(pl.multiple_of(256 * unit, 256), 256)
            weight = w_ref[:, cols]
            raw_both = dot(normed, weight)
            pieces = []
            for kind in range(2):
                raw = raw_both[:, 128 * kind : 128 * kind + 128]
                upstream = grad_ref[start, 128 * kind : 128 * kind + 128].astype(F32)
                turned = upstream * cosine - swap_halves(upstream) * sine
                scale = lax.rsqrt(head_mean(raw * raw) + EPSILON)
                one = raw * scale
                gain_sums[kind] += jnp.sum(turned * one, axis=0, keepdims=True)
                turned = turned * head_gain_ref[kind : kind + 1, :]
                grad = scale * (turned - one * head_mean(turned * one))
                if kind == 1:
                    grad = jnp.where(lane < HD, grad, upstream)
                pieces.append(grad.astype(BF))
            grads = jnp.concatenate(pieces, axis=1)
            term = dot(grads, weight, NT)
            part = term if part is None else part + term
            update = dot(normed, grads, TN)
            acc_ref[u] = update if done == 0 else acc_ref[u] + update
        scatter_rows(part_refs, core, done, part.astype(BF))
        done += size
    highs = [g.astype(BF) for g in gain_sums]
    lows = [(g - x.astype(F32)).astype(BF) for g, x in zip(gain_sums, highs, strict=True)]
    gain_row = jnp.concatenate(highs + lows, axis=1)
    gain_rows = jnp.concatenate([gain_row, jnp.zeros((7, 512), BF)], axis=0)
    blocks, heads, rows = dims
    for u, unit in enumerate((core, 1 - core)):
        cols = pl.ds(pl.multiple_of(256 * unit, 256), 256)
        for h in range(heads):
            for b in range(blocks):
                low = (h * blocks + b) * rows
                at = h * (rows + 8)
                dw_ref[b, at : at + rows, cols] = acc_ref[u, low : low + rows, :].astype(BF)
                dw_ref[b, at + rows : at + rows + 8, :] = gain_rows
    for b in range(blocks):
        for i in range(mixing_ref.shape[1] // 512):
            at = heads * (rows + 8) + i * rows
            dw_ref[b, at : at + rows, :] = mixing_ref[
                b * rows : (b + 1) * rows, 512 * i : 512 * (i + 1)
            ]


def mix_body(places, at_ref, a_ref, *refs):
    m_refs = refs[: len(places)]
    own_ref, rows_ref, hidden_ref, normed_ref = refs[len(places) :]
    hidden = own_ref[...].astype(F32)
    cols = a_ref.shape[2]
    for (other, shift), m_ref in zip(places, m_refs, strict=True):
        if other is None:
            for h in range(a_ref.shape[0]):
                hidden += dot(a_ref[h], m_ref[h * cols : (h + 1) * cols, :])
        else:
            rows = m_ref.shape[0]
            hidden += dot(a_ref[at_ref[0] ^ other, :, shift : shift + rows], m_ref[...])
    hidden_ref[...] = hidden
    normed_ref[...] = (unit_norm(hidden) * rows_ref[1:2, :]).astype(BF)


def add_parts(refs, rows):
    total = refs[0][0:rows, :].astype(F32)
    for ref in refs[1:]:
        total += ref[0:rows, :].astype(F32)
    return total


def hidden_back_body(places, at_ref, hidden_ref, cot_ref, rows_ref, *refs):
    m_refs = refs[: len(places)]
    add_refs = refs[len(places) : -3]
    grad_ref, low_ref, mixture_ref = refs[-3:]
    hidden = hidden_ref[...]
    upstream = add_parts(add_refs, hidden.shape[0]) * rows_ref[1:2, :]
    scale = lax.rsqrt(jnp.mean(hidden * hidden, axis=1, keepdims=True) + EPSILON)
    one = hidden * scale
    grad = cot_ref[...].astype(F32) + scale * (
        upstream - one * jnp.mean(upstream * one, axis=1, keepdims=True)
    )
    grad_ref[...] = grad
    low = grad.astype(BF)
    low_ref[...] = low
    cols = mixture_ref.shape[2]
    for (other, shift), m_ref in zip(places, m_refs, strict=True):
        if other is None:
            for h in range(mixture_ref.shape[0]):
                mixture_ref[h] = dot(low, m_ref[h * cols : (h + 1) * cols, :], NT).astype(BF)
        else:
            rows = m_ref.shape[0]
            mixture_ref[at_ref[0] ^ other, :, shift : shift + rows] = dot(
                low, m_ref[...], NT
            ).astype(BF)


def input_back_body(own_ref, grad_ref, rows_ref, *refs):
    out_ref = refs[-1]
    own = own_ref[...].astype(F32)
    upstream = add_parts(refs[:-1], own.shape[0]) * rows_ref[0:1, :]
    scale = lax.rsqrt(jnp.mean(own * own, axis=1, keepdims=True) + EPSILON)
    one = own * scale
    grad = grad_ref[...] + scale * (
        upstream - one * jnp.mean(upstream * one, axis=1, keepdims=True)
    )
    out_ref[...] = grad.astype(BF)


def finish_feed_body(heads, order_ref, part_ref, weight_ref, gate_ref, up_ref, dot_ref):
    width = part_ref.shape[2]
    total = jnp.zeros(dot_ref.shape, F32)
    for k in range(heads):
        start = order_ref[k] * (width // 2)
        for n in range(0, width, 128):
            value = part_ref[k, :, n : n + 128].astype(F32)
            total += value * weight_ref[order_ref[k], :, n : n + 128].astype(F32)
            out = gate_ref if n % 256 == 0 else up_ref
            out[:, pl.ds(pl.multiple_of(start + n // 256 * 128, 128), 128)] = value
    dot_ref[...] = jnp.broadcast_to(jnp.sum(total, axis=1, keepdims=True), total.shape)


def finish_projections_body(heads, unit_heads, order_ref, part_ref, weight_ref, *refs):
    q_ref, *kv_refs, dot_ref, gain_ref = refs
    rows = dot_ref.shape[0]
    total = jnp.zeros(dot_ref.shape, F32)
    gains = jnp.zeros((8, 512), F32)
    lane = lax.broadcasted_iota(jnp.int32, (rows, 128), 1)
    for k in range(heads):
        head = order_ref[k]
        value = part_ref[k, 0:rows, :].astype(F32)
        gains += part_ref[k, rows : rows + 8, :].astype(F32)
        product = value * weight_ref[head].astype(F32)
        for n in range(0, 512, 128):
            total += product[:, n : n + 128]
        spot = pl.ds(pl.multiple_of(head * 128, 128), 128)
        first, second = value[:, 128:256], value[:, 384:512]
        if unit_heads == 2:
            start = pl.multiple_of(head * 256, 256)
            q_ref[:, pl.ds(start, 128)] = value[:, 0:128]
            q_ref[:, pl.ds(start + 128, 128)] = value[:, 256:384]
            k_ref, v_ref = kv_refs
            k_ref[:, spot] = jnp.where(lane < HD, first, pltpu.roll(second, HD, 1))
            v_ref[:, spot] = jnp.where(lane < HD, pltpu.roll(first, HD, 1), second)
        else:
            q_ref[:, spot] = jnp.where(
                lane < HD, value[:, 0:128], pltpu.roll(value[:, 256:384], HD, 1)
            )
            kv_refs[0][:, spot] = first + second
    dot_ref[...] = jnp.broadcast_to(jnp.sum(total, axis=1, keepdims=True), total.shape)
    gain_ref[...] = gains[:, 0:256] + gains[:, 256:512]


def output_body(hidden_ref, *refs):
    refs[-1][...] = (
        hidden_ref[...] + add_parts(refs[:-1], hidden_ref.shape[0])
    ).astype(BF)


def joined(refs, scratch):
    if len(refs) == 1:
        return refs[0]
    at = 0
    for ref in refs:
        scratch[at : at + ref.shape[0], :] = ref[...]
        at += ref.shape[0]
    return scratch


def second_half(down_ref, skip, width, scratch, sems):
    if not skip:
        return down_ref
    share = width // down_ref.shape[0]
    copies = [
        pltpu.make_async_copy(
            down_ref.at[b, skip : skip + share], scratch.at[b * share : (b + 1) * share], sems.at[b]
        )
        for b in range(down_ref.shape[0])
    ]
    for copy in copies:
        copy.start()
    for copy in copies:
        copy.wait()
    return scratch


def column_tiles(width, size=512):
    return [(n, min(size, width - n)) for n in range(0, width, size)]


def activation_grad_body(count, skip, width, order_ref, *refs):
    c_refs, down_ref, out_refs, scratch = refs[:count], refs[count], refs[count + 1 : -3], refs[-3]
    cot = joined(c_refs, scratch)
    down_ref = second_half(down_ref, skip, width, refs[-2], refs[-1])
    for n, size in column_tiles(down_ref.shape[0]):
        grad = dot(cot[...], down_ref[n : n + size, :], NT).astype(BF)
        at = 0
        for out in out_refs:
            out[:, n : n + size] = grad[at : at + out.shape[0]]
            at += out.shape[0]


def feed_forward_body(count, first, outs, place_ref, *refs):
    x_refs, grad_ref, weight_ref = refs[:count], refs[count], refs[count + 1]
    act_ref, out_ref = refs[count + 2 : count + 4]
    back_refs, scratch = refs[count + 4 : count + 4 + outs], refs[-3]
    gu_ref, sems = refs[-2:]
    heads, blocks, piece, width = gu_ref.shape
    depth = heads * blocks * piece
    copies = [
        pltpu.make_async_copy(weight_ref.at[:, h], gu_ref.at[place_ref[h]], sems.at[h])
        for h in range(heads)
    ]
    for copy in copies:
        copy.start()
    x = joined(x_refs, scratch)
    for copy in copies:
        copy.wait()
    for n, size in column_tiles(width):
        both = dot(x[...], gu_ref[:, :, :, n : n + size].reshape(depth, size))
        for m in range(0, size, 256):
            gate, up = both[:, m : m + 128], both[:, m + 128 : m + 256]
            cols = slice((n + m) // 2, (n + m) // 2 + 128)
            grad = grad_ref[:, cols].astype(F32)
            sig = jax.nn.sigmoid(gate)
            swish = gate * sig
            act_ref[:, cols] = (swish * up).astype(BF)
            out_ref[:, n + m : n + m + 128] = (
                grad * up * sig * (1.0 + gate * (1.0 - sig))
            ).astype(BF)
            out_ref[:, n + m + 128 : n + m + 256] = (grad * swish).astype(BF)
    for n, size in column_tiles(depth):
        group = size * heads // depth if size * heads >= depth else 0
        if group:
            first_head = n * heads // depth
            weight = gu_ref[first_head : first_head + group].reshape(size, width)
        back = dot(out_ref[...], weight, NT).astype(BF)
        cols = slice(n, n + size)
        if first is None:
            scatter_rows(back_refs, 0, 0, back, cols)
        elif first:
            back_refs[0][:, cols] = back
        else:
            scatter_rows([None, *back_refs], place_ref[heads], x.shape[0] // 3, back, cols)


def feed_forward(xs, grad, gate_up, first):
    blocks, heads, piece, width = gate_up.shape
    depth = heads * blocks * piece
    rows = grad.shape[0]
    place = lax.axis_index("head")
    if first is None:
        outs = [shape(rows, depth)]
    elif first:
        outs = [shape(rows, depth)]
    else:
        outs = part_outs(rows // 3, depth)[1:]
    res = run(
        functools.partial(feed_forward_body, len(xs), first, len(outs)),
        [shape(rows, width // 2), shape(rows, width)] + outs,
        list(xs) + [grad, gate_up],
        flops=4 * rows * depth * width,
        exps=rows * width // 2,
        scalars=[*range(heads), lax.axis_index("blk") % 2],
        scratch=[
            pltpu.VMEM((rows, depth), BF),
            pltpu.VMEM((heads, blocks, piece, width), BF),
            pltpu.SemaphoreType.DMA((heads,)),
        ],
        limit=24,
        stay=(len(xs) + 1,),
    )
    return res[0], res[1], res[2:]


def down_body(count, skip, width, core_ref, *refs):
    a_refs, down_ref, out_refs, scratch = refs[:count], refs[count], refs[count + 1 : -3], refs[-3]
    act = joined(a_refs, scratch)
    down_ref = second_half(down_ref, skip, width, refs[-2], refs[-1])
    for n, size in column_tiles(down_ref.shape[1]):
        scatter_rows(
            out_refs,
            core_ref[0],
            0,
            dot(act[...], down_ref[:, n : n + size]).astype(BF),
            slice(n, n + size),
        )


def packed_rows(blocks, heads, piece, cols, width):
    chunks = cols // 1024
    rest = cols - 1024 * chunks
    aside = 1024 // rest if rest else heads
    tail = -(-heads // aside) * piece if rest else 0
    return chunks, rest, aside, chunks * heads * piece + tail, width // blocks


def weight_grad_body(counts, dims, packed, *refs):
    refs = list(refs)
    x_refs, c_refs, g_refs, a_refs = ([refs.pop(0) for _ in range(n)] for n in counts)
    out_ref, down_ref, x_all, c_all = (refs[0], refs[3], *refs[1:3]) if packed else refs
    blocks, heads, piece, cols, width = dims
    chunks, rest, aside, start, share = packed_rows(blocks, heads, piece, cols, width)

    def product(left, right, tile):
        total, at = None, 0
        for ref in right:
            here = slice(at, at + ref.shape[0])
            term = dot(left[here, :], ref[:, tile], TN)
            total = term if total is None else total + term
            at += ref.shape[0]
        return total.astype(BF)

    x = joined(x_refs, x_all)
    for n, size in column_tiles(cols):
        total = product(x, g_refs, slice(n, n + size))
        for h in range(heads):
            for b in range(blocks):
                low = (h * blocks + b) * piece
                value = total[low : low + piece]
                if n < 1024 * chunks:
                    row = n // 1024 * heads * piece + h * piece
                    out_ref[b, row : row + piece, n % 1024 : n % 1024 + size] = value
                else:
                    row = chunks * heads * piece + h // aside * piece
                    col = h % aside * rest
                    out_ref[b, row : row + piece, col : col + rest] = value
    cot = joined(c_refs, c_all)
    for n, size in column_tiles(down_ref.shape[0], 256):
        total, at = None, 0
        for ref in a_refs:
            here = slice(at, at + ref.shape[0])
            term = dot(ref[:, n : n + size], cot[here, :], TN)
            total = term if total is None else total + term
            at += ref.shape[0]
        down_ref[n : n + size, :] = total.astype(BF)
    if packed:
        for b in range(blocks):
            out_ref[b, start : start + share, :] = down_ref[b * share : (b + 1) * share, :]


def mixing_grad_body(count, at_ref, m_ref, *refs):
    total = None
    for k, low, size in tiles_of(refs[:count]):
        start = pl.ds(pl.multiple_of(at_ref[k] + low, 128), size)
        term = dot(m_ref[start, :], refs[k][low : low + size, :], TN)
        total = term if total is None else total + term
    refs[count][...] = total.astype(BF)


def permute(x, axis, move):
    count = lax.axis_size(axis)
    return lax.ppermute(x, axis, [(i, move(i) % count) for i in range(count)])


def together(*arrays):
    return lax.optimization_barrier(arrays)


def by_core_permute(x):
    count = lax.axis_size("blk")
    pairs = [
        (h * count + b, (h ^ (1 if b % 2 else 2)) * count + b)
        for h in range(lax.axis_size("head"))
        for b in range(count)
    ]
    return lax.ppermute(x, ("head", "blk"), pairs)


def first_permute(x):
    count = lax.axis_size("blk")
    pairs = [
        (h * count + b, (h ^ (2 if b % 2 else 1)) * count + b)
        for h in range(lax.axis_size("head"))
        for b in range(count)
    ]
    return lax.ppermute(x, ("head", "blk"), pairs)


def gather_near(x):
    if lax.axis_size("head") != 4:
        return []
    return [permute(x, "head", lambda i: i ^ 1), permute(x, "head", lambda i: i ^ 2)]


def gather_far(x, near):
    if lax.axis_size("head") != 4:
        return [lax.all_gather(x, "head", axis=0, tiled=True)]
    first = lax.axis_index("blk") % 2 == 0
    return [by_core_permute(jnp.where(first, near[0], near[1]))]


def gathered(x, near, far):
    return [x, *near, *far] if near else list(far)


def part_places(rows):
    if lax.axis_size("head") != 4:
        return [(None, 0)]
    return [(0, 0), (1, 0), (2, 0), (3, 0)]


def part_outs(rows, depth):
    if lax.axis_size("head") != 4:
        return [shape(rows * lax.axis_size("head"), depth)]
    return [shape(rows, depth), shape(2 * rows, depth), shape(rows, depth)]


def scatter_rows(refs, core, at, value, cols=None):
    cols = slice(None) if cols is None else cols
    if len(refs) == 1:
        refs[0][at : at + value.shape[0], cols] = value
        return
    own, sent, stay = refs
    rows = stay.shape[0]
    size = min(rows, value.shape[0])
    for low in range(0, value.shape[0], size):
        part, row = (at + low) // rows, (at + low) % rows
        here, piece = slice(row, row + size), value[low : low + size]
        if part == 0:
            own[here, cols] = piece
        elif part == 3:
            sent[rows + row : rows + row + size, cols] = piece
        else:
            goes = core == part - 1

            @pl.when(goes)
            def send(here=here, piece=piece):
                sent[here, cols] = piece

            @pl.when(jnp.logical_not(goes))
            def keep(here=here, piece=piece):
                stay[here, cols] = piece


def sum_near(pieces):
    return [] if len(pieces) == 1 else [first_permute(pieces[1])]


def sum_far(pieces, near):
    if len(pieces) == 1:
        return [lax.psum_scatter(pieces[0], "head", scatter_dimension=0, tiled=True)]
    half = near[0][pieces[2].shape[0] :]
    return [by_core_permute((half.astype(F32) + pieces[2].astype(F32)).astype(BF))]


def sum_terms(pieces, near, far):
    return list(far) if len(pieces) == 1 else [pieces[0], *near, *far]


def mirror(x):
    count = lax.axis_size("blk")
    return permute(x, "blk", lambda i: count - i if i % 2 else i)


def exchange_head(x):
    count = lax.axis_size("head")
    place = lax.axis_index("head")
    return jnp.stack(
        [
            permute(
                lax.dynamic_index_in_dim(x, place ^ k, 0, keepdims=False),
                "head",
                lambda i, k=k: i ^ k,
            )
            if k
            else lax.dynamic_index_in_dim(x, place, 0, keepdims=False)
            for k in range(count)
        ]
    )


def other_core(x):
    return permute(x, "blk", lambda i: i ^ 1)


def per_device(
    inputs,
    query_weight,
    key_weight,
    value_weight,
    mixing_weight,
    gate_weight,
    up_weight,
    down_weight,
    attention_gain,
    feedforward_gain,
    query_gain,
    key_gain,
    cotangent,
):
    heads = lax.axis_size("head")
    blocks = lax.axis_size("blk")
    chips = blocks // 2
    place = lax.axis_index("head")
    block = lax.axis_index("blk")
    core = block % 2
    chip = block // 2
    rows, depth = inputs.shape
    span = rows * heads
    piece = query_weight.shape[0]
    width = gate_weight.shape[1] // heads
    wide = -(-width // 128) * 128
    split = heads == 4
    shared = KV // heads
    unit_heads = HQ // heads // 2
    unit_cols = unit_heads * HD

    qkv_own = jnp.concatenate(
        [
            jnp.pad(
                query_weight.reshape(piece, heads, 2, unit_cols),
                ((0, 0), (0, 0), (0, 0), (0, 128 - unit_cols)),
            ),
            jnp.repeat(key_weight.reshape(piece, heads, shared, HD), 2 // shared, axis=2),
            jnp.repeat(value_weight.reshape(piece, heads, shared, HD), 2 // shared, axis=2),
        ],
        axis=-1,
    ).reshape(piece, heads, 512)
    gains = jnp.pad(jnp.stack([attention_gain, feedforward_gain], axis=1), ((0, 0), (0, 126)))
    qkv_send = jnp.concatenate(
        [qkv_own, jnp.broadcast_to(gains[:, None, :], (piece, heads, 128))], axis=-1
    ).transpose(1, 0, 2)
    gate_up_send = (
        jnp.stack(
            [
                jnp.pad(
                    w.reshape(piece, heads, width), ((0, 0), (0, 0), (0, wide - width))
                ).reshape(piece, heads, wide // 128, 128)
                for w in (gate_weight, up_weight)
            ],
            axis=3,
        )
        .reshape(piece, heads, 2 * wide)
        .transpose(1, 0, 2)
    )

    own, cot_up, qkv_piece = together(
        mirror(inputs), mirror(cotangent[: rows // 2]), exchange_head(qkv_send)
    )
    qkv_mine = [
        permute(qkv_piece, "blk", lambda i, step=step: i + 2 * step) for step in range(1, chips)
    ]
    qkv_mine, near, own = together(qkv_mine, gather_near(own), own)
    qkv_mine = [qkv_piece, *qkv_mine]
    low_rows, qkv_mine = together(
        jnp.concatenate([mixing_weight, down_weight], axis=0), qkv_mine
    )
    low_rows = lax.all_gather(low_rows, "blk", axis=0)
    qkv_theirs, far = together([other_core(x) for x in qkv_mine], gather_far(own, near))
    xs = gathered(own, near, far)
    sources = [(chip - r) % chips for r in range(chips)]
    qkv_ext = run(
        functools.partial(assemble_body, heads),
        shape(heads, blocks, piece, 640),
        qkv_mine + qkv_theirs,
        scalars=[2 * z + core for z in sources]
        + [2 * z + 1 - core for z in sources]
        + [place ^ k for k in range(heads)],
    ).reshape(depth, 640)
    span_index = jnp.where(core == 0, block, blocks - block)
    positions = (span_index * span + jnp.arange(span, dtype=jnp.int32)).astype(F32)
    lane = jnp.arange(128, dtype=jnp.int32)
    frequency = jnp.exp(
        (lane % (HD // 2)).astype(F32) * (-2.0 * math.log(ROPE_BASE) / HD)
    )
    angles = positions[:, None] * frequency[None, :]
    cosine = jnp.cos(angles)
    sine = jnp.sin(angles) * jnp.where(lane % HD < HD // 2, -1.0, 1.0)
    head_gain = jnp.concatenate(
        [
            jnp.tile(query_gain.astype(F32), 2)[None, :],
            jnp.tile(key_gain.astype(F32), 2)[None, :],
            jnp.zeros((6, 128), F32),
        ],
        axis=0,
    )

    places = part_places(rows)
    starts = [0 if other is None else (place ^ other) * rows + shift for other, shift in places]
    packet = 128 * (unit_heads + 1)
    keep, send, gain_rows = run(
        functools.partial(project_body, len(xs), unit_heads),
        [shape(span, packet), shape(span, packet), shape(8, depth, dtype=F32)],
        xs + [qkv_ext, cosine, sine, head_gain],
        flops=4 * span * depth * 512,
        scalars=starts + [core],
    )
    send, keep, gate_up_send = together(other_core(send), keep, gate_up_send)
    packets = jnp.concatenate([keep, send], axis=0)
    kv = packets[:, -128:]

    def slot_of(early, z):
        return jnp.where(4 * z < blocks, early, 1 - early) ^ core ^ 1

    def reach(z):
        return jnp.abs(4 * z - (blocks - 1))

    my_low, my_high = slot_of(1, chip), slot_of(0, chip)

    def offsets(step):
        if step == 0:
            return [span * my_high, span * my_low]
        source = (chip - step) % chips
        low, high = slot_of(1, source), slot_of(0, source)
        outer = reach(source) > reach(chip)
        return [
            span * jnp.where(outer, my_low, my_high),
            span * low,
            span * my_high,
            span * jnp.where(outer, low, high),
        ]

    def next_chip(x):
        return permute(x, "blk", lambda i: i + 2)

    groups = [[0], list(range(1, chips - 1)), [chips - 1]] if chips > 2 else [[z] for z in range(chips)]
    groups = [group for group in groups if group]
    res = attend(offsets(0), packets, [kv], None, True, len(groups) == 1, unit_heads)
    kvs = [kv]
    if chips > 1:
        kvs.append(next_chip(kv))
    res, kvs, own_cot, gate_up_piece = together(
        list(res),
        kvs,
        jnp.concatenate([cot_up, mirror(cotangent[rows // 2 :])], axis=0),
        lax.all_to_all(gate_up_send, "head", 0, 0, tiled=True),
    )
    cot_near = gather_near(own_cot)
    for step in range(2, chips - 1):
        kvs.append(next_chip(kvs[-1]))
    mixing_rows = low_rows[:, :piece].reshape(blocks * piece, depth)
    inside = piece % 16 == 0 and (width // blocks) % 16 == 0 and wide == width
    down_full = low_rows
    if not inside:
        down_full = jnp.pad(low_rows[:, piece:].reshape(-1, depth), ((0, wide - width), (0, 0)))
    kvs, cot_near, own_cot, gate_up_piece, mixing_rows = together(
        kvs, cot_near, own_cot, gate_up_piece, mixing_rows
    )
    cot_far = gather_far(own_cot, cot_near)
    gate_up = lax.all_gather(gate_up_piece, "blk", axis=0)
    mixing_near = gather_near(mixing_rows)
    for at, group in enumerate(groups[1:]):
        last = at == len(groups) - 2
        if at == 0 and len(groups) > 2:
            kvs = [*kvs, next_chip(kvs[-1])]
        new = attend(
            sum([offsets(z) for z in group], []),
            packets,
            [kvs[z] for z in group],
            res[0],
            False,
            last,
            unit_heads,
        )
        if last:
            mixing_far = gather_far(mixing_rows, mixing_near)
            res, mixing_far = together(list(new), mixing_far)
        else:
            res, kvs, mixing_near, cot_far = together(list(new), kvs, mixing_near, cot_far)
    if len(groups) == 1:
        mixing_far = gather_far(mixing_rows, mixing_near)
    acc = res[0]
    cots = gathered(own_cot, cot_near, cot_far)
    mixing_parts = gathered(mixing_rows, mixing_near, mixing_far)
    mixture_pair = res[1][:, :, :unit_cols]
    theirs = other_core(mixture_pair[1])
    mixture_span = jnp.where(
        core == 0,
        jnp.concatenate([mixture_pair[0], theirs], axis=1),
        jnp.concatenate([theirs, mixture_pair[0]], axis=1),
    )
    mixture = lax.all_to_all(
        mixture_span.reshape(heads, rows, 2 * unit_cols), "head", 0, 0, tiled=True
    )
    mix_places = part_places(mixing_rows.shape[0])
    hidden, normed_ffn = run(
        functools.partial(mix_body, mix_places),
        [shape(rows, depth, dtype=F32), shape(rows, depth)],
        [mixture] + mixing_parts + [own, gain_rows],
        flops=2 * rows * depth * depth,
        scalars=[place],
    )
    grads = run(
        functools.partial(activation_grad_body, len(cots), piece if inside else 0, width),
        [shape(rows, wide), shape(span - rows, wide)] if split else [shape(span, wide)],
        [normed_ffn] + cots + [down_full],
        flops=2 * span * depth * wide,
        scratch=[
            pltpu.VMEM((span, depth), BF),
            pltpu.VMEM((wide, depth), BF),
            pltpu.SemaphoreType.DMA((blocks,)),
        ],
        stay=(0, len(cots) + 1) if inside else (0,),
    )
    near, grads, normed_ffn = together(gather_near(normed_ffn), grads, normed_ffn)
    far = gather_far(normed_ffn, near)
    results = []
    if split:
        results.append(feed_forward([normed_ffn], grads[0], gate_up, True))
    far, results = together(far, results)
    ffn_parts = gathered(normed_ffn, near, far)
    if split:
        results = [*results, feed_forward(ffn_parts[1:], grads[1], gate_up, False)]
    else:
        results = [feed_forward(ffn_parts, grads[0], gate_up, None)]
    acts = [r[0] for r in results]
    gate_up_grads = [r[1] for r in results]
    backs = [b for r in results for b in r[2]]
    counts = (len(ffn_parts), len(cots), len(gate_up_grads), len(acts))
    dims = (blocks, heads, piece, 2 * wide, width)
    chunks, rest_cols, aside, start_row, share = packed_rows(*dims)
    packed = share % 16 == 0 and start_row % 16 == 0
    ffn_rows = start_row + (share if packed else 0)
    res = run(
        functools.partial(weight_grad_body, counts, dims, packed),
        [shape(blocks, ffn_rows, 1024)] + ([] if packed else [shape(wide, depth)]),
        ffn_parts + cots + gate_up_grads + acts,
        flops=6 * span * depth * wide,
        scratch=[pltpu.VMEM((span, depth), BF)] * 2
        + ([pltpu.VMEM((wide, depth), BF)] if packed else []),
        limit=30,
    )
    near, res, backs = together(sum_near(backs), list(res) if not packed else list(res)[:1], backs)
    ffn_part = lax.psum_scatter(res[0], "blk", scatter_dimension=0, tiled=True)[0]
    far = sum_far(backs, near)
    acts, near = together(acts, near)
    terms = run(
        functools.partial(down_body, len(acts), piece if inside else 0, width),
        part_outs(rows, depth),
        acts + [down_full],
        flops=2 * span * depth * wide,
        scalars=[core],
        scratch=[
            pltpu.VMEM((span, wide), BF),
            pltpu.VMEM((wide, depth), BF),
            pltpu.SemaphoreType.DMA((blocks,)),
        ],
        stay=(len(acts),) if inside else (),
    )
    far, terms = together(far, terms)
    addends = sum_terms(backs, near, far)
    hidden_grad, hidden_low, mixture_grad = run(
        functools.partial(hidden_back_body, mix_places),
        [shape(rows, depth, dtype=F32), shape(rows, depth), shape(heads, rows, 2 * unit_cols)],
        [hidden, own_cot, gain_rows] + mixing_parts + addends,
        flops=2 * rows * depth * depth,
        scalars=[place],
    )
    grad_span = lax.all_to_all(mixture_grad, "head", 0, 0, tiled=True).reshape(span, 2 * unit_cols)
    theirs = other_core(
        jnp.where(core == 0, grad_span[:, unit_cols:], grad_span[:, :unit_cols])
    )
    if unit_cols < 128:
        pad = ((0, 0), (0, 128 - unit_cols))
        theirs = jnp.pad(theirs, pad)
        grad_wide = jnp.concatenate(
            [jnp.pad(grad_span[:, :unit_cols], pad), jnp.pad(grad_span[:, unit_cols:], pad)], axis=1
        )
    else:
        grad_wide = grad_span
    out_grad = run(
        out_grad_body,
        shape(unit_heads, 2 * span, 128),
        [grad_wide, theirs, acc],
        scalars=[core],
    )

    def columns_of(ffn_part):
        part = ffn_part[:start_row]
        pieces = [
            part[i * heads * piece : (i + 1) * heads * piece].reshape(heads, piece, 1024)
            for i in range(chunks)
        ]
        if rest_cols:
            part = part[chunks * heads * piece :].reshape(-1, piece, aside, rest_cols)
            pieces.append(part.transpose(0, 2, 1, 3).reshape(heads, piece, rest_cols))
        return jnp.concatenate(pieces, axis=-1)

    order = sorted(range(1, chips), key=lambda step: -min(step, chips - step))
    groups = [group for group in (order[:1], order[1:], [0]) if group]
    query_acc = None
    arrived, sent = [], []
    hidden_near = hidden_far = term_near = term_far = []
    for at, group in enumerate(groups):
        last = at == len(groups) - 1
        query_acc, *kv_grads = attend_back(
            sum([offsets(z) for z in group], []),
            packets,
            out_grad,
            [kvs[z] for z in group],
            query_acc,
            last,
        )
        moved = [permute(g, "blk", lambda i, back=back: i - 2 * back) for back, g in sent]
        if at == 0:
            hidden_near = gather_near(hidden_low)
            term_near = sum_near(terms)
        if at == min(1, len(groups) - 1):
            hidden_far = gather_far(hidden_low, hidden_near)
            term_far = sum_far(terms, term_near)
        if last:
            hidden_parts = gathered(hidden_low, hidden_near, hidden_far)
            mixing_grad = run(
                functools.partial(mixing_grad_body, len(hidden_parts)),
                shape(2 * unit_cols, depth),
                [mixture_span] + hidden_parts,
                flops=4 * span * depth * unit_cols,
                scalars=starts,
            )
        query_acc, kv_grads, moved, hidden_near, hidden_far, terms, term_near, term_far = together(
            query_acc, kv_grads, moved, hidden_near, hidden_far, terms, term_near, term_far
        )
        arrived += moved
        if at == max(len(groups) - 2, 0):
            query_acc, ffn_part = together(query_acc, ffn_part)
            gate_up_part = columns_of(ffn_part)
        sent = [] if last else list(zip(group, kv_grads, strict=True))
    kv_grad = kv_grads[0]
    if packed:
        down_sum = ffn_part[start_row:]
    else:
        down_sum = lax.psum_scatter(res[1][:width], "blk", scatter_dimension=0, tiled=True)
    mine, theirs = run(
        pack_body,
        [shape(span, 256), shape(span, 256)],
        [query_acc, kv_grad] + arrived,
    )
    output_terms = sum_terms(terms, term_near, term_far)
    mine, theirs, hidden, gate_up_part = together(mine, theirs, hidden, gate_up_part)
    output = run(
        output_body,
        shape(rows, depth),
        [hidden] + output_terms,
    )
    theirs, mine, output = together(other_core(theirs), mine, output)
    output, gate_up_part = mirror(output), exchange_head(gate_up_part)
    back = run(
        functools.partial(
            project_back_body, len(xs), len(part_outs(rows, depth)), (blocks, heads, piece)
        ),
        part_outs(rows, depth)
        + [shape(blocks, heads * (piece + 8) + depth // 512 * piece, 512)],
        xs + [qkv_ext, gain_rows, mixing_grad, cosine, sine, mine, theirs, head_gain],
        flops=12 * span * depth * 512,
        scalars=starts + [core],
        scratch=[pltpu.VMEM((2, depth, 256), F32)],
    )
    gate_up_part, back, output = together(gate_up_part, list(back), output)
    *back, projections = back
    projections = lax.psum_scatter(projections, "blk", scatter_dimension=0, tiled=True)[0]
    near = sum_near(back)
    gate_sum, up_sum, feed_gain_sum = run(
        functools.partial(finish_feed_body, heads),
        [shape(piece, heads * wide, dtype=F32)] * 2 + [shape(piece, 128, dtype=F32)],
        [gate_up_part, gate_up_send],
        scalars=[place ^ k for k in range(heads)],
    )
    near, gate_sum, up_sum, feed_gain_sum, down_sum = together(
        near, gate_sum, up_sum, feed_gain_sum, down_sum.astype(F32)
    )
    far = sum_far(back, near)
    addends = sum_terms(back, near, far)
    input_gradient = run(
        input_back_body,
        shape(rows, depth),
        [own, hidden_grad, gain_rows] + addends,
    )
    input_gradient, projections = together(mirror(input_gradient), projections)
    cut = heads * (piece + 8)
    mixing_sum = (
        projections[cut:].reshape(depth // 512, piece, 512).transpose(1, 0, 2).reshape(piece, depth)
    ).astype(F32)
    qkv_part = exchange_head(projections[:cut].reshape(heads, piece + 8, 512))
    outs = [shape(piece, heads * 2 * unit_cols, dtype=F32)]
    outs += [shape(piece, heads * 128, dtype=F32)] * shared
    *grads, attention_gain_sum, head_gain_sum = run(
        functools.partial(finish_projections_body, heads, unit_heads),
        outs + [shape(piece, 128, dtype=F32), shape(8, 256, dtype=F32)],
        [qkv_part, qkv_own.transpose(1, 0, 2)],
        scalars=[place ^ k for k in range(heads)],
    )
    if shared == 1:
        both = grads[1].reshape(piece, heads, 2, HD)
        grads = [grads[0], both[:, :, 0].reshape(piece, -1), both[:, :, 1].reshape(piece, -1)]

    def only(x):
        return x.reshape(piece, heads, wide)[..., :width].reshape(piece, -1)

    return (
        output,
        input_gradient,
        *grads,
        mixing_sum,
        only(gate_sum),
        only(up_sum),
        down_sum,
        attention_gain_sum[:, 0] / attention_gain.astype(F32),
        feed_gain_sum[:, 0] / feedforward_gain.astype(F32),
        head_gain_sum[0, :HD] + head_gain_sum[0, HD : 2 * HD],
        head_gain_sum[0, 128 : 128 + HD],
    )


def solution(mesh):
    in_specs = (
        P(("blk", "head"), None),
        P(("head", "blk"), None),
        P(("head", "blk"), None),
        P(("head", "blk"), None),
        P(("head", "blk"), None),
        P(("head", "blk"), None),
        P(("head", "blk"), None),
        P(("head", "blk"), None),
        P(("head", "blk")),
        P(("head", "blk")),
        P(),
        P(),
        P(("blk", "head"), None),
    )
    out_specs = (
        P(("blk", "head"), None),
        P(("blk", "head"), None),
        P(("head", "blk"), None),
        P(("head", "blk"), None),
        P(("head", "blk"), None),
        P(("head", "blk"), None),
        P(("head", "blk"), None),
        P(("head", "blk"), None),
        P(("head", "blk"), None),
        P(("head", "blk")),
        P(("head", "blk")),
        P(),
        P(),
    )
    return jax.shard_map(
        per_device, mesh=mesh, in_specs=in_specs, out_specs=out_specs, check_vma=False
    )
```

```python
import functools
import math

import jax
import jax.numpy as jnp
from jax import lax
from jax.experimental import pallas as pl
from jax.experimental.pallas import tpu as pltpu
from jax.sharding import PartitionSpec as P

HQ = 16
KV = 8
HD = 64
EPSILON = 1e-05
ROPE_BASE = 1000000.0
TILE = 1024
QUERY_UNIT = math.log2(math.e) * HD**-0.5

BF = jnp.bfloat16
F32 = jnp.float32
NT = (((1,), (1,)), ((), ()))
NN = (((1,), (0,)), ((), ()))
TN = (((0,), (0,)), ((), ()))
VM = pl.BlockSpec(memory_space=pltpu.VMEM)
SM = pl.BlockSpec(memory_space=pltpu.SMEM)


def dot(a, b, dims=NN):
    return lax.dot_general(a, b, dims, preferred_element_type=F32)


def run(body, outs, args, flops=0, scalars=None, scratch=(), exps=0, limit=20, stay=()):
    args = list(args)
    hbm = pl.BlockSpec(memory_space=pltpu.HBM)
    specs = [hbm if i in stay else VM for i in range(len(args))]
    many = isinstance(outs, (list, tuple))
    outs = list(outs) if many else [outs]
    size = sum(math.prod(a.shape) * a.dtype.itemsize for a in outs + args)
    if scalars is not None:
        args = [jnp.stack([jnp.asarray(v, jnp.int32) for v in scalars])] + args
        specs = [SM] + specs
    return pl.pallas_call(
        body,
        out_shape=tuple(outs) if many else outs[0],
        in_specs=specs,
        out_specs=tuple([VM] * len(outs)) if many else VM,
        scratch_shapes=scratch,
        cost_estimate=pl.CostEstimate(flops=flops, bytes_accessed=size, transcendentals=exps),
        compiler_params=pltpu.CompilerParams(vmem_limit_bytes=limit << 20),
    )(*args)


def shape(*dims, dtype=BF):
    return jax.ShapeDtypeStruct(dims, dtype)


def pair_list(off_ref, span, which, count):
    return [
        (
            pl.multiple_of(off_ref[4 * which + 2 * i], span),
            pl.multiple_of(off_ref[4 * which + 2 * i + 1], span),
        )
        for i in range(count)
    ]


def attend_body(span, heads, count, local, first, last, off_ref, q_ref, *refs):
    refs = list(refs)
    kv_refs = [refs.pop(0) for _ in range(count)]
    acc_ref = None if first else refs.pop(0)
    out_ref = refs.pop(0)
    mix_ref = refs.pop(0) if last else None
    ones_ref = refs.pop(0)
    lane = lax.broadcasted_iota(jnp.int32, ones_ref.shape, 1)
    out_ref[...] = jnp.zeros_like(out_ref) if first else acc_ref[...]
    for which, kv_ref in enumerate(kv_refs):
        ones_ref[...] = jnp.where(lane < HD, jnp.ones((), BF), kv_ref[...])
        attend_block(span, heads, local, which, off_ref, q_ref, kv_ref, out_ref, ones_ref)
    if last:
        size = 256
        for i in range(2 * span // size):
            rows = slice(i * size, (i + 1) * size)
            left = lax.broadcasted_iota(jnp.int32, (size, 2 * HD), 1) < HD
            mixed = []
            for head in range(heads):
                total = out_ref[head, rows, :]
                mixed.append(total * pltpu.roll(1.0 / jnp.where(left, total, 1.0), HD, 1))
            out = jnp.where(left, pltpu.roll(mixed[0], HD, 1), mixed[1] if heads > 1 else 0.0)
            mix_ref[i * size // span, pl.ds(i * size % span, size), :] = out.astype(BF)


def attend_block(span, heads, local, which, off_ref, q_ref, kv_ref, out_ref, ones_ref):
    block = min(span, TILE)

    def block_pair(head, q_off, k_off):
        rows = pl.ds(q_off, block)
        keys = pl.ds(k_off, block)
        query = q_ref[rows, 128 * head : 128 * head + 128]
        weight = jnp.exp2(dot(query, kv_ref[keys, :], NT)).astype(BF)
        out_ref[head, rows, :] += dot(weight, ones_ref[keys, :])

    def full(q_off, k_off):
        for i in range(span // block):
            for j in range(span // block):
                for head in range(heads):
                    block_pair(head, q_off + i * block, k_off + j * block)

    def diagonal(start):
        for i in range(span // block):
            for j in range(i):
                for head in range(heads):
                    block_pair(head, start + i * block, start + j * block)
            diagonal_block(start + i * block)

    def diagonal_block(start):
        size = 256
        for head in range(heads):
            for i in range(block // size):
                rows = slice(start + i * size, start + (i + 1) * size)
                query = q_ref[rows, 128 * head : 128 * head + 128]
                total = None
                pieces = ([(0, i * size)] if i else []) + [(i * size, (i + 1) * size)]
                for low, high in pieces:
                    keys = slice(start + low, start + high)
                    weight = jnp.exp2(dot(query, kv_ref[keys, :], NT))
                    if low == i * size:
                        place = lax.broadcasted_iota(jnp.int32, (size, size), 0)
                        other = lax.broadcasted_iota(jnp.int32, (size, size), 1)
                        weight = jnp.where(other <= place, weight, 0.0)
                    part = dot(weight.astype(BF), ones_ref[keys, :])
                    total = part if total is None else total + part
                out_ref[head, rows, :] += total

    if local:
        diagonal(0)
        diagonal(span)
    for q_off, k_off in pair_list(off_ref, span, which, 1 if local else 2):
        full(q_off, k_off)


def attend(offsets, packets, kvs, acc, local, last, heads):
    span = packets.shape[0] // 2
    outs = [shape(heads, 2 * span, 2 * HD, dtype=F32)]
    if last:
        outs.append(shape(2, span, 2 * HD))
    return run(
        functools.partial(attend_body, span, heads, len(kvs), local, acc is None, last),
        outs,
        [packets, *kvs] + ([] if acc is None else [acc]),
        flops=8 * heads * span * span * 256 * len(kvs),
        scalars=offsets,
        scratch=[pltpu.VMEM((2 * span, 2 * HD), BF)],
        exps=2 * heads * span * span * len(kvs),
    )


def attend_back_body(span, heads, count, local, first, off_ref, q_ref, do_ref, *refs):
    refs = list(refs)
    kv_refs = [refs.pop(0) for _ in range(count)]
    acc_ref = None if first else refs.pop(0)
    dq_ref = refs.pop(0)
    out_refs = [refs.pop(0) for _ in range(count)]
    ones_ref, dv_ref = refs[:2]
    zero = jnp.zeros((), BF)
    lane = lax.broadcasted_iota(jnp.int32, ones_ref.shape, 1)
    for head in range(heads):
        dv_ref[head] = jnp.where(lane < HD, zero, do_ref[head])
    dq_ref[...] = jnp.zeros_like(dq_ref) if first else acc_ref[...]
    for which, (kv_ref, out_ref) in enumerate(zip(kv_refs, out_refs, strict=True)):
        ones_ref[...] = jnp.where(
            lane < HD, jnp.where(lane < 3, jnp.ones((), BF), zero), kv_ref[...]
        )
        dkv_ref = out_ref if local else refs[2]
        attend_back_block(
            span, heads, local, which, off_ref, q_ref, do_ref, kv_ref, dq_ref, dkv_ref, ones_ref, dv_ref
        )
        if not local:
            out_ref[...] = dkv_ref[...].astype(BF)


def attend_back_block(
    span, heads, local, which, off_ref, q_ref, do_ref, kv_ref, dq_ref, dkv_ref, ones_ref, dv_ref
):
    block = min(span, TILE)
    dkv_ref[...] = jnp.zeros_like(dkv_ref)

    def tile(head, rows, keys, mask):
        query = q_ref[rows, 128 * head : 128 * head + 128]
        pair = kv_ref[keys, :]
        weight = jnp.exp2(dot(pair, query, NT))
        if mask is not None:
            weight = jnp.where(mask, weight, 0.0)
        score_grad = (weight * dot(ones_ref[keys, :], do_ref[head, rows, :], NT)).astype(BF)
        dkv_ref[keys, :] += dot(weight.astype(BF), dv_ref[head, rows, :]) + dot(score_grad, query)
        dq_ref[head, rows, :] += dot(score_grad, pair, TN)

    def block_pair(head, q_off, k_off):
        tile(head, pl.ds(q_off, block), pl.ds(k_off, block), None)

    def full(q_off, k_off):
        for i in range(span // block):
            for j in range(span // block):
                for head in range(heads):
                    block_pair(head, q_off + i * block, k_off + j * block)

    def diagonal(start):
        for i in range(span // block):
            for j in range(i):
                for head in range(heads):
                    block_pair(head, start + i * block, start + j * block)
            diagonal_block(start + i * block)

    def diagonal_block(start):
        size = 256
        for head in range(heads):
            for i in range(block // size):
                rows = slice(start + i * size, start + (i + 1) * size)
                pieces = ([(0, i * size)] if i else []) + [(i * size, (i + 1) * size)]
                for low, high in pieces:
                    mask = None
                    if low == i * size:
                        key_place = lax.broadcasted_iota(jnp.int32, (size, size), 0)
                        mask = key_place <= lax.broadcasted_iota(jnp.int32, (size, size), 1)
                    tile(head, rows, slice(start + low, start + high), mask)

    if local:
        diagonal(0)
        diagonal(span)
    for q_off, k_off in pair_list(off_ref, span, which, 1 if local else 2):
        full(q_off, k_off)


def attend_back(offsets, packets, out_grad, kvs, acc, local):
    heads, rows = out_grad.shape[:2]
    span = rows // 2
    count = len(kvs)
    return run(
        functools.partial(attend_back_body, span, heads, count, local, acc is None),
        [shape(heads, rows, 2 * HD, dtype=F32)]
        + [shape(rows, 2 * HD, dtype=F32 if local else BF)] * count,
        [packets, out_grad, *kvs] + ([] if acc is None else [acc]),
        flops=20 * heads * span * span * 256 * count,
        scalars=offsets,
        scratch=[pltpu.VMEM((rows, 2 * HD), BF), pltpu.VMEM((heads, rows, 2 * HD), BF)]
        + ([] if local else [pltpu.VMEM((rows, 2 * HD), F32)]),
        exps=2 * heads * span * span * count,
        limit=36,
    )


def out_grad_body(core_ref, mine_ref, theirs_ref, acc_ref, out_ref):
    heads, rows = acc_ref.shape[:2]
    size = 256
    lane = lax.broadcasted_iota(jnp.int32, (size, 2 * HD), 1)
    left = lane < HD
    for i in range(rows // size):
        here = slice(i * size, (i + 1) * size)
        if i * size < rows // 2:
            first = mine_ref[here, 0:128]
            second = mine_ref[here, 128:256]
            both = jnp.where(core_ref[0] == 0, first, second).astype(F32)
        else:
            both = theirs_ref[slice(i * size - rows // 2, (i + 1) * size - rows // 2), :].astype(F32)
        for head in range(heads):
            grad = pltpu.roll(both, HD, 1) if head == 0 else both
            total = acc_ref[head, here, :]
            inverse = pltpu.roll(1.0 / jnp.where(left, total, 1.0), HD, 1)
            scaled = grad * inverse
            delta = jnp.sum(
                jnp.where(left, 0.0, scaled * total * inverse), axis=1, keepdims=True
            )
            shift = jnp.broadcast_to(-delta, (size, 2 * HD))
            high = shift.astype(BF).astype(F32)
            rest = shift - high
            middle = rest.astype(BF).astype(F32)
            parts = jnp.where(lane == 0, high, jnp.where(lane == 1, middle, rest - middle))
            out = jnp.where(left, jnp.where(lane < 3, parts, 0.0), scaled)
            out_ref[head, here, :] = out.astype(BF)


def pack_body(dq_ref, dkv_ref, *refs):
    outs = refs[-2:]
    heads, rows = dq_ref.shape[:2]
    span = rows // 2
    size = 256
    lane = lax.broadcasted_iota(jnp.int32, (size, 2 * HD), 1)
    for i in range(rows // size):
        here = slice(i * size, (i + 1) * size)
        there = slice(i * size % span, i * size % span + size)
        out = outs[i * size // span]
        query = dq_ref[0, here, :]
        other = pltpu.roll(dq_ref[1, here, :], HD, 1) if heads > 1 else 0.0
        query = jnp.where(lane < HD, query, other) * (HD**-0.5)
        pair = dkv_ref[here, :]
        for more in refs[:-2]:
            pair = pair + more[here, :].astype(F32)
        pair = pair * jnp.where(lane < HD, math.log(2.0), 1.0)
        out[there, 0:128] = query.astype(BF)
        out[there, 128:256] = pair.astype(BF)


def swap_halves(x):
    lane = lax.broadcasted_iota(jnp.int32, x.shape, 1)
    return jnp.where(
        lane % HD < HD // 2, pltpu.roll(x, x.shape[1] - HD // 2, 1), pltpu.roll(x, HD // 2, 1)
    )


def head_mean(x):
    size = x.shape[1]
    first = lax.broadcasted_iota(jnp.int32, (size, size), 0) // HD
    second = lax.broadcasted_iota(jnp.int32, (size, size), 1) // HD
    ones = jnp.where(first == second, 1.0 / HD, 0.0).astype(BF)
    high = x.astype(BF)
    low = (x - high.astype(F32)).astype(BF)
    return dot(high, ones) + dot(low, ones)


def unit_norm(x):
    return x * lax.rsqrt(jnp.mean(x * x, axis=1, keepdims=True) + EPSILON)


def tiles_of(refs, size=256):
    for k, ref in enumerate(refs):
        step = min(size, ref.shape[0])
        for low in range(0, ref.shape[0], step):
            yield k, low, step


def assemble_body(heads, index_ref, *refs):
    out_ref = refs[-1]
    for r, ref in enumerate(refs[:-1]):
        for h in range(heads):
            out_ref[index_ref[len(refs) - 1 + h], index_ref[r]] = ref[h]


def project_body(count, heads, at_ref, *refs):
    x_refs = refs[:count]
    w_ref, cos_ref, sin_ref, head_gain_ref, keep_ref, send_ref, rows_ref = refs[count:]
    core = at_ref[count]
    rows_ref[...] = w_ref[:, 512:640].astype(F32).T[0:8]
    gain = rows_ref[0:1, :]
    for k, low, size in tiles_of(x_refs):
        start = pl.ds(pl.multiple_of(at_ref[k] + low, 128), size)
        normed = (unit_norm(x_refs[k][low : low + size, :].astype(F32)) * gain).astype(BF)
        cosine, sine = cos_ref[start, :], sin_ref[start, :]
        lane = lax.broadcasted_iota(jnp.int32, cosine.shape, 1)
        for unit, out_ref in ((core, keep_ref), (1 - core, send_ref)):
            raw = dot(normed, w_ref[:, pl.ds(pl.multiple_of(256 * unit, 256), 256)])
            query, pair = raw[:, :128], raw[:, 128:]
            query = query * lax.rsqrt(head_mean(query * query) + EPSILON) * head_gain_ref[0:1, :]
            query = (query * cosine + swap_halves(query) * sine) * QUERY_UNIT
            out_ref[start, 0:128] = jnp.where(lane < HD, query, 0.0).astype(BF)
            if heads > 1:
                shifted = pltpu.roll(query, HD, 1)
                out_ref[start, 128:256] = jnp.where(lane < HD, shifted, 0.0).astype(BF)
            key = pair * lax.rsqrt(head_mean(pair * pair) + EPSILON) * head_gain_ref[1:2, :]
            key = key * cosine + swap_halves(key) * sine
            out_ref[start, 128 * heads : 128 * heads + 128] = jnp.where(lane < HD, key, pair).astype(BF)


def project_back_body(count, outs, dims, at_ref, *refs):
    x_refs = refs[:count]
    w_ref, rows_ref, mixing_ref, cos_ref, sin_ref, mine_ref, theirs_ref, head_gain_ref = refs[
        count : count + 8
    ]
    part_refs = refs[count + 8 : count + 8 + outs]
    dw_ref, acc_ref, normed_ref, grads_ref = refs[count + 8 + outs :]
    core = at_ref[count]
    gain = rows_ref[0:1, :]
    gain_sums = [jnp.zeros((1, 128), F32), jnp.zeros((1, 128), F32)]
    done = 0
    for k, low, size in tiles_of(x_refs):
        start = pl.ds(pl.multiple_of(at_ref[k] + low, 128), size)
        normed = (unit_norm(x_refs[k][low : low + size, :].astype(F32)) * gain).astype(BF)
        cosine, sine = cos_ref[start, :], sin_ref[start, :]
        lane = lax.broadcasted_iota(jnp.int32, cosine.shape, 1)
        normed_ref[done : done + size, :] = normed
        for u, (unit, grad_ref) in enumerate(((core, mine_ref), (1 - core, theirs_ref))):
            raw_both = dot(normed, w_ref[:, pl.ds(pl.multiple_of(256 * unit, 256), 256)])
            for kind in range(2):
                raw = raw_both[:, 128 * kind : 128 * kind + 128]
                upstream = grad_ref[start, 128 * kind : 128 * kind + 128].astype(F32)
                turned = upstream * cosine - swap_halves(upstream) * sine
                scale = lax.rsqrt(head_mean(raw * raw) + EPSILON)
                one = raw * scale
                gain_sums[kind] += jnp.sum(turned * one, axis=0, keepdims=True)
                turned = turned * head_gain_ref[kind : kind + 1, :]
                grad = scale * (turned - one * head_mean(turned * one))
                if kind == 1:
                    grad = jnp.where(lane < HD, grad, upstream)
                col = 256 * u + 128 * kind
                grads_ref[done : done + size, col : col + 128] = grad.astype(BF)
        done += size
    for u in range(2):
        acc_ref[u] = dot(normed_ref[...], grads_ref[:, 256 * u : 256 * u + 256], TN)
    depth = acc_ref.shape[1]
    for n in range(0, depth, 512):
        part = None
        for u, unit in enumerate((core, 1 - core)):
            weight = w_ref[n : n + 512, pl.ds(pl.multiple_of(256 * unit, 256), 256)]
            term = dot(grads_ref[:, 256 * u : 256 * u + 256], weight, NT)
            part = term if part is None else part + term
        scatter_rows(part_refs, core, 0, part.astype(BF), slice(n, n + 512))
    highs = [g.astype(BF) for g in gain_sums]
    lows = [(g - x.astype(F32)).astype(BF) for g, x in zip(gain_sums, highs, strict=True)]
    gain_row = jnp.concatenate(highs + lows, axis=1)
    gain_rows = jnp.concatenate([gain_row, jnp.zeros((7, 512), BF)], axis=0)
    blocks, heads, rows = dims
    for u, unit in enumerate((core, 1 - core)):
        cols = pl.ds(pl.multiple_of(256 * unit, 256), 256)
        for h in range(heads):
            for b in range(blocks):
                low = (h * blocks + b) * rows
                at = h * (rows + 8)
                dw_ref[b, at : at + rows, cols] = acc_ref[u, low : low + rows, :].astype(BF)
                dw_ref[b, at + rows : at + rows + 8, :] = gain_rows
    for b in range(blocks):
        for i in range(mixing_ref.shape[1] // 512):
            at = heads * (rows + 8) + i * rows
            dw_ref[b, at : at + rows, :] = mixing_ref[
                b * rows : (b + 1) * rows, 512 * i : 512 * (i + 1)
            ]


def mix_body(places, at_ref, a_ref, *refs):
    m_refs = refs[: len(places)]
    own_ref, rows_ref, hidden_ref, normed_ref = refs[len(places) :]
    hidden = own_ref[...].astype(F32)
    cols = a_ref.shape[2]
    for (other, shift), m_ref in zip(places, m_refs, strict=True):
        if other is None:
            for h in range(a_ref.shape[0]):
                hidden += dot(a_ref[h], m_ref[h * cols : (h + 1) * cols, :])
        else:
            rows = m_ref.shape[0]
            hidden += dot(a_ref[at_ref[0] ^ other, :, shift : shift + rows], m_ref[...])
    hidden_ref[...] = hidden
    normed_ref[...] = (unit_norm(hidden) * rows_ref[1:2, :]).astype(BF)


def add_parts(refs, rows):
    total = refs[0][0:rows, :].astype(F32)
    for ref in refs[1:]:
        total += ref[0:rows, :].astype(F32)
    return total


def hidden_back_body(places, at_ref, hidden_ref, cot_ref, rows_ref, *refs):
    m_refs = refs[: len(places)]
    add_refs = refs[len(places) : -3]
    grad_ref, low_ref, mixture_ref = refs[-3:]
    hidden = hidden_ref[...]
    upstream = add_parts(add_refs, hidden.shape[0]) * rows_ref[1:2, :]
    scale = lax.rsqrt(jnp.mean(hidden * hidden, axis=1, keepdims=True) + EPSILON)
    one = hidden * scale
    grad = cot_ref[...].astype(F32) + scale * (
        upstream - one * jnp.mean(upstream * one, axis=1, keepdims=True)
    )
    grad_ref[...] = grad
    low = grad.astype(BF)
    low_ref[...] = low
    cols = mixture_ref.shape[2]
    for (other, shift), m_ref in zip(places, m_refs, strict=True):
        if other is None:
            for h in range(mixture_ref.shape[0]):
                mixture_ref[h] = dot(low, m_ref[h * cols : (h + 1) * cols, :], NT).astype(BF)
        else:
            rows = m_ref.shape[0]
            mixture_ref[at_ref[0] ^ other, :, shift : shift + rows] = dot(
                low, m_ref[...], NT
            ).astype(BF)


def input_back_body(own_ref, grad_ref, rows_ref, *refs):
    out_ref = refs[-1]
    own = own_ref[...].astype(F32)
    upstream = add_parts(refs[:-1], own.shape[0]) * rows_ref[0:1, :]
    scale = lax.rsqrt(jnp.mean(own * own, axis=1, keepdims=True) + EPSILON)
    one = own * scale
    grad = grad_ref[...] + scale * (
        upstream - one * jnp.mean(upstream * one, axis=1, keepdims=True)
    )
    out_ref[...] = grad.astype(BF)


def finish_feed_body(heads, order_ref, part_ref, weight_ref, gate_ref, up_ref, dot_ref):
    width = part_ref.shape[2]
    total = jnp.zeros(dot_ref.shape, F32)
    for k in range(heads):
        start = order_ref[k] * (width // 2)
        for n in range(0, width, 128):
            value = part_ref[k, :, n : n + 128].astype(F32)
            total += value * weight_ref[order_ref[k], :, n : n + 128].astype(F32)
            out = gate_ref if n % 256 == 0 else up_ref
            out[:, pl.ds(pl.multiple_of(start + n // 256 * 128, 128), 128)] = value
    dot_ref[...] = jnp.broadcast_to(jnp.sum(total, axis=1, keepdims=True), total.shape)


def finish_projections_body(heads, unit_heads, order_ref, part_ref, weight_ref, *refs):
    q_ref, *kv_refs, dot_ref, gain_ref = refs
    rows = dot_ref.shape[0]
    total = jnp.zeros(dot_ref.shape, F32)
    gains = jnp.zeros((8, 512), F32)
    lane = lax.broadcasted_iota(jnp.int32, (rows, 128), 1)
    for k in range(heads):
        head = order_ref[k]
        value = part_ref[k, 0:rows, :].astype(F32)
        gains += part_ref[k, rows : rows + 8, :].astype(F32)
        product = value * weight_ref[head].astype(F32)
        for n in range(0, 512, 128):
            total += product[:, n : n + 128]
        spot = pl.ds(pl.multiple_of(head * 128, 128), 128)
        first, second = value[:, 128:256], value[:, 384:512]
        if unit_heads == 2:
            start = pl.multiple_of(head * 256, 256)
            q_ref[:, pl.ds(start, 128)] = value[:, 0:128]
            q_ref[:, pl.ds(start + 128, 128)] = value[:, 256:384]
            k_ref, v_ref = kv_refs
            k_ref[:, spot] = jnp.where(lane < HD, first, pltpu.roll(second, HD, 1))
            v_ref[:, spot] = jnp.where(lane < HD, pltpu.roll(first, HD, 1), second)
        else:
            q_ref[:, spot] = jnp.where(
                lane < HD, value[:, 0:128], pltpu.roll(value[:, 256:384], HD, 1)
            )
            kv_refs[0][:, spot] = first + second
    dot_ref[...] = jnp.broadcast_to(jnp.sum(total, axis=1, keepdims=True), total.shape)
    gain_ref[...] = gains[:, 0:256] + gains[:, 256:512]


def output_body(hidden_ref, *refs):
    refs[-1][...] = (
        hidden_ref[...] + add_parts(refs[:-1], hidden_ref.shape[0])
    ).astype(BF)


def joined(refs, scratch):
    if len(refs) == 1:
        return refs[0]
    at = 0
    for ref in refs:
        scratch[at : at + ref.shape[0], :] = ref[...]
        at += ref.shape[0]
    return scratch


def second_half(down_ref, skip, width, scratch, sems):
    if not skip:
        return down_ref
    share = width // down_ref.shape[0]
    copies = [
        pltpu.make_async_copy(
            down_ref.at[b, skip : skip + share], scratch.at[b * share : (b + 1) * share], sems.at[b]
        )
        for b in range(down_ref.shape[0])
    ]
    for copy in copies:
        copy.start()
    for copy in copies:
        copy.wait()
    return scratch


def column_tiles(width, size=512):
    return [(n, min(size, width - n)) for n in range(0, width, size)]


def activation_grad_body(count, skip, width, order_ref, *refs):
    c_refs, down_ref, out_refs, scratch = refs[:count], refs[count], refs[count + 1 : -3], refs[-3]
    cot = joined(c_refs, scratch)
    down_ref = second_half(down_ref, skip, width, refs[-2], refs[-1])
    for n, size in column_tiles(down_ref.shape[0]):
        grad = dot(cot[...], down_ref[n : n + size, :], NT).astype(BF)
        at = 0
        for out in out_refs:
            out[:, n : n + size] = grad[at : at + out.shape[0]]
            at += out.shape[0]


def feed_forward_body(count, first, outs, place_ref, *refs):
    x_refs, grad_ref, weight_ref = refs[:count], refs[count], refs[count + 1]
    act_ref, out_ref = refs[count + 2 : count + 4]
    back_refs, scratch = refs[count + 4 : count + 4 + outs], refs[-3]
    gu_ref, sems = refs[-2:]
    heads, blocks, piece, width = gu_ref.shape
    depth = heads * blocks * piece
    copies = [
        pltpu.make_async_copy(weight_ref.at[:, h], gu_ref.at[place_ref[h]], sems.at[h])
        for h in range(heads)
    ]
    for copy in copies:
        copy.start()
    x = joined(x_refs, scratch)
    for copy in copies:
        copy.wait()
    for n, size in column_tiles(width):
        both = dot(x[...], gu_ref[:, :, :, n : n + size].reshape(depth, size))
        for m in range(0, size, 256):
            gate, up = both[:, m : m + 128], both[:, m + 128 : m + 256]
            cols = slice((n + m) // 2, (n + m) // 2 + 128)
            grad = grad_ref[:, cols].astype(F32)
            sig = jax.nn.sigmoid(gate)
            swish = gate * sig
            act_ref[:, cols] = (swish * up).astype(BF)
            out_ref[:, n + m : n + m + 128] = (
                grad * up * sig * (1.0 + gate * (1.0 - sig))
            ).astype(BF)
            out_ref[:, n + m + 128 : n + m + 256] = (grad * swish).astype(BF)
    for n, size in column_tiles(depth):
        group = size * heads // depth if size * heads >= depth else 0
        if group:
            first_head = n * heads // depth
            weight = gu_ref[first_head : first_head + group].reshape(size, width)
        back = dot(out_ref[...], weight, NT).astype(BF)
        cols = slice(n, n + size)
        if first is None:
            scatter_rows(back_refs, 0, 0, back, cols)
        elif first:
            back_refs[0][:, cols] = back
        else:
            scatter_rows([None, *back_refs], place_ref[heads], x.shape[0] // 3, back, cols)


def feed_forward(xs, grad, gate_up, first):
    blocks, heads, piece, width = gate_up.shape
    depth = heads * blocks * piece
    rows = grad.shape[0]
    place = lax.axis_index("head")
    if first is None:
        outs = [shape(rows, depth)]
    elif first:
        outs = [shape(rows, depth)]
    else:
        outs = part_outs(rows // 3, depth)[1:]
    res = run(
        functools.partial(feed_forward_body, len(xs), first, len(outs)),
        [shape(rows, width // 2), shape(rows, width)] + outs,
        list(xs) + [grad, gate_up],
        flops=4 * rows * depth * width,
        exps=rows * width // 2,
        scalars=[*range(heads), lax.axis_index("blk") % 2],
        scratch=[
            pltpu.VMEM((rows, depth), BF),
            pltpu.VMEM((heads, blocks, piece, width), BF),
            pltpu.SemaphoreType.DMA((heads,)),
        ],
        limit=24,
        stay=(len(xs) + 1,),
    )
    return res[0], res[1], res[2:]


def down_body(count, skip, width, core_ref, *refs):
    a_refs, down_ref, out_refs, scratch = refs[:count], refs[count], refs[count + 1 : -3], refs[-3]
    act = joined(a_refs, scratch)
    down_ref = second_half(down_ref, skip, width, refs[-2], refs[-1])
    for n, size in column_tiles(down_ref.shape[1]):
        scatter_rows(
            out_refs,
            core_ref[0],
            0,
            dot(act[...], down_ref[:, n : n + size]).astype(BF),
            slice(n, n + size),
        )


def packed_rows(blocks, heads, piece, cols, width):
    chunks = cols // 1024
    rest = cols - 1024 * chunks
    aside = 1024 // rest if rest else heads
    tail = -(-heads // aside) * piece if rest else 0
    return chunks, rest, aside, chunks * heads * piece + tail, width // blocks


def weight_grad_body(counts, dims, packed, *refs):
    refs = list(refs)
    x_refs, c_refs, g_refs, a_refs = ([refs.pop(0) for _ in range(n)] for n in counts)
    out_ref, down_ref, x_all, c_all = (refs[0], refs[3], *refs[1:3]) if packed else refs
    blocks, heads, piece, cols, width = dims
    chunks, rest, aside, start, share = packed_rows(blocks, heads, piece, cols, width)

    def product(left, right, tile):
        total, at = None, 0
        for ref in right:
            here = slice(at, at + ref.shape[0])
            term = dot(left[here, :], ref[:, tile], TN)
            total = term if total is None else total + term
            at += ref.shape[0]
        return total.astype(BF)

    x = joined(x_refs, x_all)
    for n, size in column_tiles(cols):
        total = product(x, g_refs, slice(n, n + size))
        for h in range(heads):
            for b in range(blocks):
                low = (h * blocks + b) * piece
                value = total[low : low + piece]
                if n < 1024 * chunks:
                    row = n // 1024 * heads * piece + h * piece
                    out_ref[b, row : row + piece, n % 1024 : n % 1024 + size] = value
                else:
                    row = chunks * heads * piece + h // aside * piece
                    col = h % aside * rest
                    out_ref[b, row : row + piece, col : col + rest] = value
    cot = joined(c_refs, c_all)
    for n, size in column_tiles(down_ref.shape[0], 256):
        total, at = None, 0
        for ref in a_refs:
            here = slice(at, at + ref.shape[0])
            term = dot(ref[:, n : n + size], cot[here, :], TN)
            total = term if total is None else total + term
            at += ref.shape[0]
        down_ref[n : n + size, :] = total.astype(BF)
    if packed:
        for b in range(blocks):
            out_ref[b, start : start + share, :] = down_ref[b * share : (b + 1) * share, :]


def mixing_grad_body(count, at_ref, m_ref, *refs):
    total = None
    for k, low, size in tiles_of(refs[:count]):
        start = pl.ds(pl.multiple_of(at_ref[k] + low, 128), size)
        term = dot(m_ref[start, :], refs[k][low : low + size, :], TN)
        total = term if total is None else total + term
    refs[count][...] = total.astype(BF)


def permute(x, axis, move):
    count = lax.axis_size(axis)
    return lax.ppermute(x, axis, [(i, move(i) % count) for i in range(count)])


def together(*arrays):
    return lax.optimization_barrier(arrays)


def by_core_permute(x):
    count = lax.axis_size("blk")
    pairs = [
        (h * count + b, (h ^ (1 if b % 2 else 2)) * count + b)
        for h in range(lax.axis_size("head"))
        for b in range(count)
    ]
    return lax.ppermute(x, ("head", "blk"), pairs)


def first_permute(x):
    count = lax.axis_size("blk")
    pairs = [
        (h * count + b, (h ^ (2 if b % 2 else 1)) * count + b)
        for h in range(lax.axis_size("head"))
        for b in range(count)
    ]
    return lax.ppermute(x, ("head", "blk"), pairs)


def gather_near(x):
    if lax.axis_size("head") != 4:
        return []
    return [permute(x, "head", lambda i: i ^ 1), permute(x, "head", lambda i: i ^ 2)]


def gather_far(x, near):
    if lax.axis_size("head") != 4:
        return [lax.all_gather(x, "head", axis=0, tiled=True)]
    first = lax.axis_index("blk") % 2 == 0
    return [by_core_permute(jnp.where(first, near[0], near[1]))]


def gathered(x, near, far):
    return [x, *near, *far] if near else list(far)


def part_places(rows):
    if lax.axis_size("head") != 4:
        return [(None, 0)]
    return [(0, 0), (1, 0), (2, 0), (3, 0)]


def part_outs(rows, depth):
    if lax.axis_size("head") != 4:
        return [shape(rows * lax.axis_size("head"), depth)]
    return [shape(rows, depth), shape(2 * rows, depth), shape(rows, depth)]


def scatter_rows(refs, core, at, value, cols=None):
    cols = slice(None) if cols is None else cols
    if len(refs) == 1:
        refs[0][at : at + value.shape[0], cols] = value
        return
    own, sent, stay = refs
    rows = stay.shape[0]
    size = min(rows, value.shape[0])
    for low in range(0, value.shape[0], size):
        part, row = (at + low) // rows, (at + low) % rows
        here, piece = slice(row, row + size), value[low : low + size]
        if part == 0:
            own[here, cols] = piece
        elif part == 3:
            sent[rows + row : rows + row + size, cols] = piece
        else:
            goes = core == part - 1

            @pl.when(goes)
            def send(here=here, piece=piece):
                sent[here, cols] = piece

            @pl.when(jnp.logical_not(goes))
            def keep(here=here, piece=piece):
                stay[here, cols] = piece


def sum_near(pieces):
    return [] if len(pieces) == 1 else [first_permute(pieces[1])]


def sum_far(pieces, near):
    if len(pieces) == 1:
        return [lax.psum_scatter(pieces[0], "head", scatter_dimension=0, tiled=True)]
    half = near[0][pieces[2].shape[0] :]
    return [by_core_permute((half.astype(F32) + pieces[2].astype(F32)).astype(BF))]


def sum_terms(pieces, near, far):
    return list(far) if len(pieces) == 1 else [pieces[0], *near, *far]


def mirror(x):
    count = lax.axis_size("blk")
    return permute(x, "blk", lambda i: count - i if i % 2 else i)


def exchange_head(x):
    count = lax.axis_size("head")
    place = lax.axis_index("head")
    return jnp.stack(
        [
            permute(
                lax.dynamic_index_in_dim(x, place ^ k, 0, keepdims=False),
                "head",
                lambda i, k=k: i ^ k,
            )
            if k
            else lax.dynamic_index_in_dim(x, place, 0, keepdims=False)
            for k in range(count)
        ]
    )


def other_core(x):
    return permute(x, "blk", lambda i: i ^ 1)


def per_device(
    inputs,
    query_weight,
    key_weight,
    value_weight,
    mixing_weight,
    gate_weight,
    up_weight,
    down_weight,
    attention_gain,
    feedforward_gain,
    query_gain,
    key_gain,
    cotangent,
):
    heads = lax.axis_size("head")
    blocks = lax.axis_size("blk")
    chips = blocks // 2
    place = lax.axis_index("head")
    block = lax.axis_index("blk")
    core = block % 2
    chip = block // 2
    rows, depth = inputs.shape
    span = rows * heads
    piece = query_weight.shape[0]
    width = gate_weight.shape[1] // heads
    wide = -(-width // 128) * 128
    split = heads == 4
    shared = KV // heads
    unit_heads = HQ // heads // 2
    unit_cols = unit_heads * HD

    qkv_own = jnp.concatenate(
        [
            jnp.pad(
                query_weight.reshape(piece, heads, 2, unit_cols),
                ((0, 0), (0, 0), (0, 0), (0, 128 - unit_cols)),
            ),
            jnp.repeat(key_weight.reshape(piece, heads, shared, HD), 2 // shared, axis=2),
            jnp.repeat(value_weight.reshape(piece, heads, shared, HD), 2 // shared, axis=2),
        ],
        axis=-1,
    ).reshape(piece, heads, 512)
    gains = jnp.pad(jnp.stack([attention_gain, feedforward_gain], axis=1), ((0, 0), (0, 126)))
    qkv_send = jnp.concatenate(
        [qkv_own, jnp.broadcast_to(gains[:, None, :], (piece, heads, 128))], axis=-1
    ).transpose(1, 0, 2)
    gate_up_send = (
        jnp.stack(
            [
                jnp.pad(
                    w.reshape(piece, heads, width), ((0, 0), (0, 0), (0, wide - width))
                ).reshape(piece, heads, wide // 128, 128)
                for w in (gate_weight, up_weight)
            ],
            axis=3,
        )
        .reshape(piece, heads, 2 * wide)
        .transpose(1, 0, 2)
    )

    own, cot_up, qkv_piece = together(
        mirror(inputs), mirror(cotangent[: rows // 2]), exchange_head(qkv_send)
    )
    qkv_mine = [
        permute(qkv_piece, "blk", lambda i, step=step: i + 2 * step) for step in range(1, chips)
    ]
    qkv_mine, near, own = together(qkv_mine, gather_near(own), own)
    qkv_mine = [qkv_piece, *qkv_mine]
    low_rows, qkv_mine = together(
        jnp.concatenate([mixing_weight, down_weight], axis=0), qkv_mine
    )
    low_rows = lax.all_gather(low_rows, "blk", axis=0)
    qkv_theirs, far = together([other_core(x) for x in qkv_mine], gather_far(own, near))
    xs = gathered(own, near, far)
    sources = [(chip - r) % chips for r in range(chips)]
    qkv_ext = run(
        functools.partial(assemble_body, heads),
        shape(heads, blocks, piece, 640),
        qkv_mine + qkv_theirs,
        scalars=[2 * z + core for z in sources]
        + [2 * z + 1 - core for z in sources]
        + [place ^ k for k in range(heads)],
    ).reshape(depth, 640)
    span_index = jnp.where(core == 0, block, blocks - block)
    positions = (span_index * span + jnp.arange(span, dtype=jnp.int32)).astype(F32)
    lane = jnp.arange(128, dtype=jnp.int32)
    frequency = jnp.exp(
        (lane % (HD // 2)).astype(F32) * (-2.0 * math.log(ROPE_BASE) / HD)
    )
    angles = positions[:, None] * frequency[None, :]
    cosine = jnp.cos(angles)
    sine = jnp.sin(angles) * jnp.where(lane % HD < HD // 2, -1.0, 1.0)
    head_gain = jnp.concatenate(
        [
            jnp.tile(query_gain.astype(F32), 2)[None, :],
            jnp.tile(key_gain.astype(F32), 2)[None, :],
            jnp.zeros((6, 128), F32),
        ],
        axis=0,
    )

    places = part_places(rows)
    starts = [0 if other is None else (place ^ other) * rows + shift for other, shift in places]
    packet = 128 * (unit_heads + 1)
    keep, send, gain_rows = run(
        functools.partial(project_body, len(xs), unit_heads),
        [shape(span, packet), shape(span, packet), shape(8, depth, dtype=F32)],
        xs + [qkv_ext, cosine, sine, head_gain],
        flops=4 * span * depth * 512,
        scalars=starts + [core],
    )
    send, keep, gate_up_send = together(other_core(send), keep, gate_up_send)
    packets = jnp.concatenate([keep, send], axis=0)
    kv = packets[:, -128:]

    def slot_of(early, z):
        return jnp.where(4 * z < blocks, early, 1 - early) ^ core ^ 1

    def reach(z):
        return jnp.abs(4 * z - (blocks - 1))

    my_low, my_high = slot_of(1, chip), slot_of(0, chip)

    def offsets(step):
        if step == 0:
            return [span * my_high, span * my_low]
        source = (chip - step) % chips
        low, high = slot_of(1, source), slot_of(0, source)
        outer = reach(source) > reach(chip)
        return [
            span * jnp.where(outer, my_low, my_high),
            span * low,
            span * my_high,
            span * jnp.where(outer, low, high),
        ]

    def next_chip(x):
        return permute(x, "blk", lambda i: i + 2)

    groups = [[0], list(range(1, chips - 1)), [chips - 1]] if chips > 2 else [[z] for z in range(chips)]
    groups = [group for group in groups if group]
    res = attend(offsets(0), packets, [kv], None, True, len(groups) == 1, unit_heads)
    kvs = [kv]
    if chips > 1:
        kvs.append(next_chip(kv))
    res, kvs, own_cot, gate_up_piece = together(
        list(res),
        kvs,
        jnp.concatenate([cot_up, mirror(cotangent[rows // 2 :])], axis=0),
        lax.all_to_all(gate_up_send, "head", 0, 0, tiled=True),
    )
    cot_near = gather_near(own_cot)
    for step in range(2, chips - 1):
        kvs.append(next_chip(kvs[-1]))
    mixing_rows = low_rows[:, :piece].reshape(blocks * piece, depth)
    inside = piece % 16 == 0 and (width // blocks) % 16 == 0 and wide == width
    down_full = low_rows
    if not inside:
        down_full = jnp.pad(low_rows[:, piece:].reshape(-1, depth), ((0, wide - width), (0, 0)))
    kvs, cot_near, own_cot, gate_up_piece, mixing_rows = together(
        kvs, cot_near, own_cot, gate_up_piece, mixing_rows
    )
    cot_far = gather_far(own_cot, cot_near)
    gate_up = lax.all_gather(gate_up_piece, "blk", axis=0)
    mixing_near = gather_near(mixing_rows)
    for at, group in enumerate(groups[1:]):
        last = at == len(groups) - 2
        if at == 0 and len(groups) > 2:
            kvs = [*kvs, next_chip(kvs[-1])]
        new = attend(
            sum([offsets(z) for z in group], []),
            packets,
            [kvs[z] for z in group],
            res[0],
            False,
            last,
            unit_heads,
        )
        if last:
            mixing_far = gather_far(mixing_rows, mixing_near)
            res, mixing_far = together(list(new), mixing_far)
        else:
            res, kvs, mixing_near, cot_far = together(list(new), kvs, mixing_near, cot_far)
    if len(groups) == 1:
        mixing_far = gather_far(mixing_rows, mixing_near)
    acc = res[0]
    cots = gathered(own_cot, cot_near, cot_far)
    mixing_parts = gathered(mixing_rows, mixing_near, mixing_far)
    mixture_pair = res[1][:, :, :unit_cols]
    theirs = other_core(mixture_pair[1])
    mixture_span = jnp.where(
        core == 0,
        jnp.concatenate([mixture_pair[0], theirs], axis=1),
        jnp.concatenate([theirs, mixture_pair[0]], axis=1),
    )
    mixture = lax.all_to_all(
        mixture_span.reshape(heads, rows, 2 * unit_cols), "head", 0, 0, tiled=True
    )
    mix_places = part_places(mixing_rows.shape[0])
    hidden, normed_ffn = run(
        functools.partial(mix_body, mix_places),
        [shape(rows, depth, dtype=F32), shape(rows, depth)],
        [mixture] + mixing_parts + [own, gain_rows],
        flops=2 * rows * depth * depth,
        scalars=[place],
    )
    grads = run(
        functools.partial(activation_grad_body, len(cots), piece if inside else 0, width),
        [shape(rows, wide), shape(span - rows, wide)] if split else [shape(span, wide)],
        [normed_ffn] + cots + [down_full],
        flops=2 * span * depth * wide,
        scratch=[
            pltpu.VMEM((span, depth), BF),
            pltpu.VMEM((wide, depth), BF),
            pltpu.SemaphoreType.DMA((blocks,)),
        ],
        stay=(0, len(cots) + 1) if inside else (0,),
    )
    near, grads, normed_ffn = together(gather_near(normed_ffn), grads, normed_ffn)
    far = gather_far(normed_ffn, near)
    results = []
    if split:
        results.append(feed_forward([normed_ffn], grads[0], gate_up, True))
    far, results = together(far, results)
    ffn_parts = gathered(normed_ffn, near, far)
    if split:
        results = [*results, feed_forward(ffn_parts[1:], grads[1], gate_up, False)]
    else:
        results = [feed_forward(ffn_parts, grads[0], gate_up, None)]
    acts = [r[0] for r in results]
    gate_up_grads = [r[1] for r in results]
    backs = [b for r in results for b in r[2]]
    counts = (len(ffn_parts), len(cots), len(gate_up_grads), len(acts))
    dims = (blocks, heads, piece, 2 * wide, width)
    chunks, rest_cols, aside, start_row, share = packed_rows(*dims)
    packed = share % 16 == 0 and start_row % 16 == 0
    ffn_rows = start_row + (share if packed else 0)
    res = run(
        functools.partial(weight_grad_body, counts, dims, packed),
        [shape(blocks, ffn_rows, 1024)] + ([] if packed else [shape(wide, depth)]),
        ffn_parts + cots + gate_up_grads + acts,
        flops=6 * span * depth * wide,
        scratch=[pltpu.VMEM((span, depth), BF)] * 2
        + ([pltpu.VMEM((wide, depth), BF)] if packed else []),
        limit=30,
    )
    near, res, backs = together(sum_near(backs), list(res) if not packed else list(res)[:1], backs)
    ffn_part = lax.psum_scatter(res[0], "blk", scatter_dimension=0, tiled=True)[0]
    far = sum_far(backs, near)
    acts, near = together(acts, near)
    terms = run(
        functools.partial(down_body, len(acts), piece if inside else 0, width),
        part_outs(rows, depth),
        acts + [down_full],
        flops=2 * span * depth * wide,
        scalars=[core],
        scratch=[
            pltpu.VMEM((span, wide), BF),
            pltpu.VMEM((wide, depth), BF),
            pltpu.SemaphoreType.DMA((blocks,)),
        ],
        stay=(len(acts),) if inside else (),
    )
    far, terms = together(far, terms)
    addends = sum_terms(backs, near, far)
    hidden_grad, hidden_low, mixture_grad = run(
        functools.partial(hidden_back_body, mix_places),
        [shape(rows, depth, dtype=F32), shape(rows, depth), shape(heads, rows, 2 * unit_cols)],
        [hidden, own_cot, gain_rows] + mixing_parts + addends,
        flops=2 * rows * depth * depth,
        scalars=[place],
    )
    grad_span = lax.all_to_all(mixture_grad, "head", 0, 0, tiled=True).reshape(span, 2 * unit_cols)
    theirs = other_core(
        jnp.where(core == 0, grad_span[:, unit_cols:], grad_span[:, :unit_cols])
    )
    if unit_cols < 128:
        pad = ((0, 0), (0, 128 - unit_cols))
        theirs = jnp.pad(theirs, pad)
        grad_wide = jnp.concatenate(
            [jnp.pad(grad_span[:, :unit_cols], pad), jnp.pad(grad_span[:, unit_cols:], pad)], axis=1
        )
    else:
        grad_wide = grad_span
    out_grad = run(
        out_grad_body,
        shape(unit_heads, 2 * span, 128),
        [grad_wide, theirs, acc],
        scalars=[core],
    )

    def columns_of(ffn_part):
        part = ffn_part[:start_row]
        pieces = [
            part[i * heads * piece : (i + 1) * heads * piece].reshape(heads, piece, 1024)
            for i in range(chunks)
        ]
        if rest_cols:
            part = part[chunks * heads * piece :].reshape(-1, piece, aside, rest_cols)
            pieces.append(part.transpose(0, 2, 1, 3).reshape(heads, piece, rest_cols))
        return jnp.concatenate(pieces, axis=-1)

    order = sorted(range(1, chips), key=lambda step: -min(step, chips - step))
    groups = [group for group in (order[:1], order[1:], [0]) if group]
    query_acc = None
    arrived, sent = [], []
    hidden_near = hidden_far = term_near = term_far = []
    for at, group in enumerate(groups):
        last = at == len(groups) - 1
        query_acc, *kv_grads = attend_back(
            sum([offsets(z) for z in group], []),
            packets,
            out_grad,
            [kvs[z] for z in group],
            query_acc,
            last,
        )
        moved = [permute(g, "blk", lambda i, back=back: i - 2 * back) for back, g in sent]
        if at == 0:
            hidden_near = gather_near(hidden_low)
            term_near = sum_near(terms)
        if at == min(1, len(groups) - 1):
            hidden_far = gather_far(hidden_low, hidden_near)
            term_far = sum_far(terms, term_near)
        if last:
            hidden_parts = gathered(hidden_low, hidden_near, hidden_far)
            mixing_grad = run(
                functools.partial(mixing_grad_body, len(hidden_parts)),
                shape(2 * unit_cols, depth),
                [mixture_span] + hidden_parts,
                flops=4 * span * depth * unit_cols,
                scalars=starts,
            )
        query_acc, kv_grads, moved, hidden_near, hidden_far, terms, term_near, term_far = together(
            query_acc, kv_grads, moved, hidden_near, hidden_far, terms, term_near, term_far
        )
        arrived += moved
        if at == max(len(groups) - 2, 0):
            query_acc, ffn_part = together(query_acc, ffn_part)
            gate_up_part = columns_of(ffn_part)
        sent = [] if last else list(zip(group, kv_grads, strict=True))
    kv_grad = kv_grads[0]
    if packed:
        down_sum = ffn_part[start_row:]
    else:
        down_sum = lax.psum_scatter(res[1][:width], "blk", scatter_dimension=0, tiled=True)
    mine, theirs = run(
        pack_body,
        [shape(span, 256), shape(span, 256)],
        [query_acc, kv_grad] + arrived,
    )
    output_terms = sum_terms(terms, term_near, term_far)
    mine, theirs, hidden, gate_up_part = together(mine, theirs, hidden, gate_up_part)
    output = run(
        output_body,
        shape(rows, depth),
        [hidden] + output_terms,
    )
    theirs, mine, output = together(other_core(theirs), mine, output)
    output, gate_up_part = mirror(output), exchange_head(gate_up_part)
    back = run(
        functools.partial(
            project_back_body, len(xs), len(part_outs(rows, depth)), (blocks, heads, piece)
        ),
        part_outs(rows, depth)
        + [shape(blocks, heads * (piece + 8) + depth // 512 * piece, 512)],
        xs + [qkv_ext, gain_rows, mixing_grad, cosine, sine, mine, theirs, head_gain],
        flops=12 * span * depth * 512,
        scalars=starts + [core],
        scratch=[
            pltpu.VMEM((2, depth, 256), F32),
            pltpu.VMEM((span, depth), BF),
            pltpu.VMEM((span, 512), BF),
        ],
        limit=32,
    )
    gate_up_part, back, output = together(gate_up_part, list(back), output)
    *back, projections = back
    projections = lax.psum_scatter(projections, "blk", scatter_dimension=0, tiled=True)[0]
    near = sum_near(back)
    gate_sum, up_sum, feed_gain_sum = run(
        functools.partial(finish_feed_body, heads),
        [shape(piece, heads * wide, dtype=F32)] * 2 + [shape(piece, 128, dtype=F32)],
        [gate_up_part, gate_up_send],
        scalars=[place ^ k for k in range(heads)],
    )
    near, gate_sum, up_sum, feed_gain_sum, down_sum = together(
        near, gate_sum, up_sum, feed_gain_sum, down_sum.astype(F32)
    )
    far = sum_far(back, near)
    addends = sum_terms(back, near, far)
    input_gradient = run(
        input_back_body,
        shape(rows, depth),
        [own, hidden_grad, gain_rows] + addends,
    )
    input_gradient, projections = together(input_gradient, projections)
    cut = heads * (piece + 8)
    mixing_sum = (
        projections[cut:].reshape(depth // 512, piece, 512).transpose(1, 0, 2).reshape(piece, depth)
    ).astype(F32)
    qkv_part = exchange_head(projections[:cut].reshape(heads, piece + 8, 512))
    input_gradient, qkv_part = together(mirror(input_gradient), qkv_part)
    outs = [shape(piece, heads * 2 * unit_cols, dtype=F32)]
    outs += [shape(piece, heads * 128, dtype=F32)] * shared
    *grads, attention_gain_sum, head_gain_sum = run(
        functools.partial(finish_projections_body, heads, unit_heads),
        outs + [shape(piece, 128, dtype=F32), shape(8, 256, dtype=F32)],
        [qkv_part, qkv_own.transpose(1, 0, 2)],
        scalars=[place ^ k for k in range(heads)],
    )
    if shared == 1:
        both = grads[1].reshape(piece, heads, 2, HD)
        grads = [grads[0], both[:, :, 0].reshape(piece, -1), both[:, :, 1].reshape(piece, -1)]

    def only(x):
        return x.reshape(piece, heads, wide)[..., :width].reshape(piece, -1)

    return (
        output,
        input_gradient,
        *grads,
        mixing_sum,
        only(gate_sum),
        only(up_sum),
        down_sum,
        attention_gain_sum[:, 0] / attention_gain.astype(F32),
        feed_gain_sum[:, 0] / feedforward_gain.astype(F32),
        head_gain_sum[0, :HD] + head_gain_sum[0, HD : 2 * HD],
        head_gain_sum[0, 128 : 128 + HD],
    )


def solution(mesh):
    in_specs = (
        P(("blk", "head"), None),
        P(("head", "blk"), None),
        P(("head", "blk"), None),
        P(("head", "blk"), None),
        P(("head", "blk"), None),
        P(("head", "blk"), None),
        P(("head", "blk"), None),
        P(("head", "blk"), None),
        P(("head", "blk")),
        P(("head", "blk")),
        P(),
        P(),
        P(("blk", "head"), None),
    )
    out_specs = (
        P(("blk", "head"), None),
        P(("blk", "head"), None),
        P(("head", "blk"), None),
        P(("head", "blk"), None),
        P(("head", "blk"), None),
        P(("head", "blk"), None),
        P(("head", "blk"), None),
        P(("head", "blk"), None),
        P(("head", "blk"), None),
        P(("head", "blk")),
        P(("head", "blk")),
        P(),
        P(),
    )
    return jax.shard_map(
        per_device, mesh=mesh, in_specs=in_specs, out_specs=out_specs, check_vma=False
    )
```
